512 devices in a mesh: elem: 16 (over z, y_hi), span: 32 (over y_lo, x, core).
Axes of the slice: x: 4, y: 8 (y_hi: 2, y_lo: 4; y = y_hi * 4 + y_lo), z: 8, core: 2. Of those that a mesh axis runs over, the one named last changes fastest.
Arguments:
- state: float32 [4, 256, 36864], P(None, 'span', 'elem'), may hold values from -6 to 6
- metric: float32 [2, 1024], P(None, 'elem'), may hold values from -40 to 40, as said below
- neighbour: int32 [1024, 4], P('elem'), may hold values from 0 to 287, as said below
- orient: int32 [1024, 4], P('elem'), may hold values from 0 to 1, as said below
- wall: int32 [1024, 4], P('elem'), may hold values from 0 to 1, as said below
- rim: int32 [2, 256], P(None, 'elem'), may hold values from 0 to 255, as said below
Outputs:
- updated: float32 [4, 256, 36864], P(None, 'span', 'elem')
The draws below stay inside these ranges and needn't reach their ends.
Inputs may be any that keep to these rules, and one draw needn't show every extreme that they name: neighbour[e, s] is a slot of e's element group's trace pool: e' * 4 + s' for the facing side s' of a local element e' (local index within the group), 256 + r for row r of the lower group's rim, 272 + r for row r of the upper group's rim; on a wall side it is e's own slot. Elements form a channel of 16 rows and 4 columns per group, periodic in x over the groups, in an order drawn per group; elements may be reflected in either reference direction. `orient`: 0 on wall sides. `wall`: 1 exactly on the sides of the first and last rows that face the walls. rim[0, g * 16 + r] is the local slot e * 4 + s of the side of group g's first-column element in row r that faces the lower group; rim[1] likewise for the last column and the upper group. Nonzero; the magnitude of metric[0] is equal along a global column of elements, that of metric[1] along a row; the sign is -1 where the element is reflected in that direction.
All inputs are finite; a program needn't handle non-finite values.
Results may differ from the reference program's by a relative error of at most 0.0003.
Values sent between devices are 32-bit elements; how exact they have to be, the bound alone decides.
A program may use at most 64 MiB of HBM per device.

```python
import math
import jax
import jax.numpy as jnp
import numpy as np
from jax import lax

MODES = 256
ROWS = 16
COLS_DEV = 4
ELEMENTS = 1024


def layout(key):
    base = jax.random.fold_in(key, 11)
    per_group = ROWS * COLS_DEV
    groups = ELEMENTS // per_group
    group_keys = jax.random.split(base, groups)
    slot_cell = jax.vmap(lambda single: jax.random.permutation(single, per_group))(group_keys).astype(jnp.int32)
    cell_slot = jnp.argsort(slot_cell, axis=1, stable=True).astype(jnp.int32)
    flips = jax.random.randint(jax.random.fold_in(base, 5), (groups, per_group, 2), 0, 2).astype(jnp.int32)
    return (slot_cell, cell_slot, flips)


def tables(key):
    slot_cell, cell_slot, flips = layout(key)
    groups, per_group = slot_cell.shape
    column = slot_cell // ROWS
    row_of = slot_cell % ROWS
    flip_x = flips[:, :, 0]
    flip_y = flips[:, :, 1]
    group_ids = jnp.zeros_like(column) + jnp.arange(groups, dtype=jnp.int32)[:, None]
    own_slots = jnp.zeros_like(column) + jnp.arange(per_group, dtype=jnp.int32)[None, :]
    indices = []
    orients = []
    walls = []
    for side in range(4):
        if side < 2:
            upward = jnp.bitwise_xor(flip_x, side) == 1
            stride = jnp.where(upward, 1, -1)
            next_col = column + stride
            inside = (next_col >= 0) & (next_col < COLS_DEV)
            next_group = (group_ids + jnp.where(inside, 0, stride)) % groups
            next_slot = cell_slot[next_group, next_col % COLS_DEV * ROWS + row_of]
            next_fx = flips[next_group, next_slot, 0]
            next_fy = flips[next_group, next_slot, 1]
            facing = jnp.where(upward, next_fx, 1 - next_fx)
            remote = 4 * per_group + jnp.where(upward, ROWS, 0) + row_of
            indices.append(jnp.where(inside, next_slot * 4 + facing, remote))
            orients.append(jnp.where(flip_y != next_fy, 1, 0))
            walls.append(jnp.zeros_like(column))
        else:
            upward = jnp.bitwise_xor(flip_y, side - 2) == 1
            stride = jnp.where(upward, 1, -1)
            next_row = row_of + stride
            inside = (next_row >= 0) & (next_row < ROWS)
            next_slot = cell_slot[group_ids, column * ROWS + next_row % ROWS]
            next_fx = flips[group_ids, next_slot, 0]
            next_fy = flips[group_ids, next_slot, 1]
            facing = 2 + jnp.where(upward, next_fy, 1 - next_fy)
            indices.append(jnp.where(inside, next_slot * 4 + facing, own_slots * 4 + side))
            orients.append(jnp.where(inside & (flip_x != next_fx), 1, 0))
            walls.append(jnp.where(inside, 0, 1))
    row_cells = jnp.arange(ROWS, dtype=jnp.int32)
    lower_slot = cell_slot[:, row_cells]
    lower_fx = jnp.take_along_axis(flip_x, lower_slot, axis=1)
    upper_slot = cell_slot[:, (COLS_DEV - 1) * ROWS + row_cells]
    upper_fx = jnp.take_along_axis(flip_x, upper_slot, axis=1)
    rim_table = jnp.stack([(lower_slot * 4 + lower_fx).reshape(-1), (upper_slot * 4 + 1 - upper_fx).reshape(-1)])
    index_table = jnp.stack(indices, axis=2).reshape(groups * per_group, 4).astype(jnp.int32)
    orient_table = jnp.stack(orients, axis=2).reshape(groups * per_group, 4).astype(jnp.int32)
    wall_table = jnp.stack(walls, axis=2).reshape(groups * per_group, 4).astype(jnp.int32)
    return (index_table, orient_table, wall_table, rim_table.astype(jnp.int32))


def draw_neighbour(key, part):
    return tables(key)[0]


def draw_orient(key, part):
    return tables(key)[1]


def draw_wall(key, part):
    return tables(key)[2]


def draw_rim(key, part):
    return tables(key)[3]


def draw_metric(key, part):
    slot_cell, cell_slot, flips = layout(key)
    groups, per_group = slot_cell.shape
    col_key, row_key = jax.random.split(jax.random.fold_in(key, 29))
    widths = jnp.exp(jax.random.uniform(col_key, (groups * COLS_DEV,), jnp.float32, math.log(10.0), math.log(40.0)))
    heights = jnp.exp(jax.random.uniform(row_key, (ROWS,), jnp.float32, math.log(10.0), math.log(40.0)))
    global_col = slot_cell // ROWS + jnp.arange(groups, dtype=jnp.int32)[:, None] * COLS_DEV
    along_x = widths[global_col] * (1.0 - 2.0 * flips[:, :, 0].astype(jnp.float32))
    along_y = heights[slot_cell % ROWS] * (1.0 - 2.0 * flips[:, :, 1].astype(jnp.float32))
    return jnp.stack([along_x.reshape(-1), along_y.reshape(-1)]).astype(jnp.float32)


def shard_levels(key, dims, pieces, low, largest):
    loudness, own = 1.0, jax.random.fold_in(key, 6)
    for axis_at, blocks in pieces:
        draws = jnp.exp(jax.random.uniform(jax.random.fold_in(own, axis_at), (blocks,), jnp.float32, low / len(pieces), largest / len(pieces)))
        loudness = loudness * jnp.repeat(draws, dims[axis_at] // blocks).reshape([-1 if axis == axis_at else 1 for axis in range(len(dims))])
    return loudness


def scatter_about(rng, shape, spread, limit, pieces=(), kind=jnp.bfloat16):
    values = jax.random.normal(rng, shape, jnp.float32) * spread
    if len(pieces) > 0:
        values = shard_levels(rng, shape, pieces, -0.22, 0.18) * values
    return jnp.clip(values, min=-limit, max=limit).astype(kind)


def setup_inputs(seed: int = 0) -> dict:
    streams_of = jax.random.split(jax.random.key(seed), 7)
    state = scatter_about(streams_of[0], (4, MODES, ELEMENTS * 36), 1.0, 6.0, ((1, 32), (2, 16)), jnp.float32)
    metric = draw_metric(jax.random.fold_in(streams_of[6], 71), 0)
    neighbour = draw_neighbour(jax.random.fold_in(streams_of[6], 71), 0)
    orient = draw_orient(jax.random.fold_in(streams_of[6], 71), 0)
    wall = draw_wall(jax.random.fold_in(streams_of[6], 71), 0)
    rim = draw_rim(jax.random.fold_in(streams_of[6], 71), 0)
    return dict(state=state, metric=metric, neighbour=neighbour, orient=orient, wall=wall, rim=rim)


TIME_STEP = 0.001
VISCOSITY = 0.02
PENALTY = 1.0
HIGHEST = lax.Precision.HIGHEST

def gll_tables():
    near_point = math.sqrt(1.0 / 3.0 - 2.0 * math.sqrt(7.0) / 21.0)
    far_point = math.sqrt(1.0 / 3.0 + 2.0 * math.sqrt(7.0) / 21.0)
    points = np.array([-1.0, -far_point, -near_point, near_point, far_point, 1.0])
    weights = np.array([1.0 / np.prod([points[column] - points[second] for second in range(6) if second != column]) for column in range(6)])
    deriv = np.zeros((6, 6))
    for target in range(6):
        for source in range(6):
            if source != target:
                deriv[target, source] = weights[source] / weights[target] / (points[target] - points[source])
        deriv[target, target] = -np.sum(deriv[target])
    identity = np.eye(6)
    along_x = np.kron(deriv, identity)
    along_y = np.kron(identity, deriv)
    edge_nodes = np.array([[offset for offset in range(6)], [30 + offset for offset in range(6)], [6 * offset for offset in range(6)], [6 * offset + 5 for offset in range(6)]]).reshape(-1)
    lifting = np.zeros((36, 24))
    lifting[edge_nodes, np.arange(24)] = 1.0
    return (jnp.asarray(along_x, jnp.float32), jnp.asarray(along_y, jnp.float32), edge_nodes, jnp.asarray(lifting, jnp.float32))

def spanwise_basis(count):
    mode_index = jnp.arange(count, dtype=jnp.int32)
    planes = jnp.arange(count, dtype=jnp.int32)
    phase = mode_index[:, None] // 2 * planes[None, :] % count
    phase_angle = phase.astype(jnp.float32) * (2.0 * math.pi / count)
    odd_rows = (mode_index % 2 == 1)[:, None]
    basis_table = jnp.where(odd_rows, jnp.sin(phase_angle), jnp.cos(phase_angle)) * math.sqrt(2.0 / count)
    alternate = (1 - 2 * (planes % 2)).astype(jnp.float32) / math.sqrt(count)
    constant = jnp.ones((count,), jnp.float32) / math.sqrt(count)
    basis_table = jnp.where(mode_index[:, None] == 0, constant[None, :], basis_table)
    basis_table = jnp.where(mode_index[:, None] == 1, alternate[None, :], basis_table)
    return basis_table

def spanwise_derivative(modal):
    shape_in = modal.shape
    paired = modal.reshape(shape_in[0], shape_in[1] // 2, 2, shape_in[2])
    wavenumber = jnp.arange(shape_in[1] // 2, dtype=jnp.int32).astype(jnp.float32)[None, :, None]
    return jnp.stack([wavenumber * paired[:, :, 1], -wavenumber * paired[:, :, 0]], axis=2).reshape(shape_in)

def modal_divergence(flux_x, flux_y, along_z, metric_local):
    along_x, along_y, edge_nodes, lifting = gll_tables()
    scale_x = metric_local[0]
    scale_y = metric_local[1]
    grad_x = jnp.einsum('pq,vmqe->vmpe', along_x, flux_x, precision=HIGHEST)
    grad_y = jnp.einsum('pq,vmqe->vmpe', along_y, flux_y, precision=HIGHEST)
    divergence = scale_x * grad_x + scale_y * grad_y + along_z
    sign_x = jnp.sign(scale_x)
    sign_y = jnp.sign(scale_y)
    normal_flux = jnp.concatenate([-sign_x * flux_x[:, :, edge_nodes[0:6]], sign_x * flux_x[:, :, edge_nodes[6:12]], -sign_y * flux_y[:, :, edge_nodes[12:18]], sign_y * flux_y[:, :, edge_nodes[18:24]]], axis=2)
    return (divergence, normal_flux)

def trace_pool(traces):
    shape_in = traces.shape
    return traces.reshape(shape_in[0], shape_in[1], 4, 6, shape_in[3]).transpose(0, 1, 3, 4, 2).reshape(shape_in[0], shape_in[1], 6, 4 * shape_in[3])

def own_pools(state_local, normal_flux):
    edge_nodes = gll_tables()[2]
    return (trace_pool(state_local[:, :, edge_nodes, :]), trace_pool(normal_flux))

def update(state_local, divergence, own_q, own_flux, from_lower, from_upper, neighbour, orient, wall, metric_local, first_mode, total_modes):
    lifting = gll_tables()[3]
    num_vars, modes_here, num_nodes, count = state_local.shape
    pool_q = jnp.concatenate([own_q, from_lower[0], from_upper[0]], axis=3)
    pool_flux = jnp.concatenate([own_flux, from_lower[1], from_upper[1]], axis=3)
    flat_index = neighbour.reshape(-1)
    other_q = jnp.take(pool_q, flat_index, axis=3)
    other_flux = jnp.take(pool_flux, flat_index, axis=3)
    flipped = orient.reshape(-1) == 1
    other_q = jnp.where(flipped, other_q[:, :, ::-1, :], other_q)
    other_flux = jnp.where(flipped, other_flux[:, :, ::-1, :], other_flux)
    mirror = jnp.array([-1.0, -1.0, -1.0, 1.0], jnp.float32).reshape(4, 1, 1, 1)
    walled = wall.reshape(-1) == 1
    other_q = jnp.where(walled, mirror * own_q, other_q)
    other_flux = jnp.where(walled, mirror * own_flux, other_flux)
    magnitude = jnp.abs(jnp.stack([metric_local[0], metric_local[0], metric_local[1], metric_local[1]], axis=1)).reshape(-1) * 15.0
    surface_jump = magnitude * (0.5 * (own_flux + other_flux) - 0.5 * PENALTY * (own_q - other_q))
    unpooled = surface_jump.reshape(num_vars, modes_here, 6, count, 4).transpose(0, 1, 4, 2, 3).reshape(num_vars, modes_here, 24, count)
    surface = jnp.einsum('pq,vmqe->vmpe', lifting, unpooled, precision=HIGHEST)
    mode_index = first_mode + jnp.arange(modes_here, dtype=jnp.int32)
    wavenumber = jnp.where(mode_index == 1, total_modes // 2, mode_index // 2).astype(jnp.float32)
    damping = 1.0 + TIME_STEP * VISCOSITY * wavenumber * wavenumber
    return (state_local + TIME_STEP * (surface - divergence)) / damping[None, :, None, None]

def volume_terms(block):
    state_local, metric_local, rim_local = block
    num_vars, total_modes, num_nodes, count = state_local.shape
    basis_table = spanwise_basis(total_modes)
    physical = jnp.einsum('mn,vmk->vnk', basis_table, state_local.reshape(num_vars, total_modes, num_nodes * count), precision=HIGHEST)
    fields = jnp.concatenate([physical[0:1] * physical, physical[1:2] * physical, physical[2:3] * physical], axis=0)
    modal = jnp.einsum('mn,vnk->vmk', basis_table, fields, precision=HIGHEST)
    shape_back = (num_vars, total_modes, num_nodes, count)
    along_z = spanwise_derivative(modal[8:12]).reshape(shape_back)
    divergence, normal_flux = modal_divergence(modal[0:4].reshape(shape_back), modal[4:8].reshape(shape_back), along_z, metric_local)
    own_q, own_flux = own_pools(state_local, normal_flux)
    to_upper = jnp.stack([jnp.take(own_q, rim_local[1], axis=3), jnp.take(own_flux, rim_local[1], axis=3)])
    to_lower = jnp.stack([jnp.take(own_q, rim_local[0], axis=3), jnp.take(own_flux, rim_local[0], axis=3)])
    return (divergence, normal_flux, to_upper, to_lower)

def reference(state, metric, neighbour, orient, wall, rim):
    num_vars, total_modes, flat_size = state.shape
    num_nodes = 36
    total_elems = flat_size // num_nodes
    state_nodes = jnp.transpose(state.reshape(num_vars, total_modes, total_elems, num_nodes), (0, 1, 3, 2))
    groups = rim.shape[1] // ROWS
    per_group = total_elems // groups
    blocks = jnp.moveaxis(state_nodes.reshape(num_vars, total_modes, num_nodes, groups, per_group), 3, 0)
    metrics = jnp.moveaxis(metric.reshape(2, groups, per_group), 1, 0)
    rims = jnp.moveaxis(rim.reshape(2, groups, ROWS), 1, 0)
    divergence, normal_flux, to_upper, to_lower = lax.map(volume_terms, (blocks, metrics, rims))
    from_lower = jnp.roll(to_upper, 1, axis=0)
    from_upper = jnp.roll(to_lower, -1, axis=0)
    neighbours = neighbour.reshape(groups, per_group, 4)
    orients = orient.reshape(groups, per_group, 4)
    walls = wall.reshape(groups, per_group, 4)

    def finish(block):
        state_local, divergence_local, flux_local, lower_local, upper_local, neighbour_local, orient_local, wall_local, metric_local = block
        own_q, own_flux = own_pools(state_local, flux_local)
        return update(state_local, divergence_local, own_q, own_flux, lower_local, upper_local, neighbour_local, orient_local, wall_local, metric_local, 0, total_modes)
    result = lax.map(finish, (blocks, divergence, normal_flux, from_lower, from_upper, neighbours, orients, walls, metrics))
    result_nodes = jnp.moveaxis(result, 0, 3).reshape(num_vars, total_modes, num_nodes, total_elems)
    return jnp.transpose(result_nodes, (0, 1, 3, 2)).reshape(num_vars, total_modes, flat_size)
```

```python
import functools
import math

import jax
import jax.numpy as jnp
import numpy as np
from jax import lax
from jax.experimental import pallas as pl
from jax.experimental.pallas import tpu as pltpu
from jax.sharding import PartitionSpec as P

TIME_STEP = 0.001
VISCOSITY = 0.02
MESH = pl.DeviceIdType.MESH
F32 = jnp.float32
BF16 = jnp.bfloat16
NODES = 36
PAIR = 72
LANES = 128


def differentiation():
    near = math.sqrt(1.0 / 3.0 - 2.0 * math.sqrt(7.0) / 21.0)
    far = math.sqrt(1.0 / 3.0 + 2.0 * math.sqrt(7.0) / 21.0)
    points = np.array([-1.0, -far, -near, near, far, 1.0])
    weights = np.array(
        [1.0 / np.prod([points[c] - points[s] for s in range(6) if s != c]) for c in range(6)]
    )
    deriv = np.zeros((6, 6))
    for t in range(6):
        for s in range(6):
            if s != t:
                deriv[t, s] = weights[s] / weights[t] / (points[t] - points[s])
        deriv[t, t] = -np.sum(deriv[t])
    return deriv


def split_np(x):
    high = x.astype(jnp.bfloat16)
    low = (x - high.astype(np.float64)).astype(jnp.bfloat16)
    return high, low


def basis_tables(count):
    m = np.arange(count)[:, None]
    n = np.arange(count)[None, :]
    angle = (m // 2 * n % count) * (2.0 * math.pi / count)
    basis = np.where(m % 2 == 1, np.sin(angle), np.cos(angle)) * math.sqrt(2.0 / count)
    basis[0] = 1.0 / math.sqrt(count)
    basis[1] = (1.0 - 2.0 * (np.arange(count) % 2)) / math.sqrt(count)
    minus = np.zeros_like(basis)
    k = np.arange(count // 2)[:, None]
    minus[0::2] = -k * basis[1::2]
    minus[1::2] = k * basis[0::2]
    both = np.concatenate([basis, minus], axis=1)
    return split_np(both)


def node_tables():
    deriv = differentiation()
    ident = np.eye(6)
    two = np.eye(2)
    along_x = np.zeros((PAIR, 192))
    along_y = np.zeros((PAIR, 192))
    lift = np.zeros((PAIR, 192))
    along_x[:, 0:72] = -np.kron(two, np.kron(deriv, ident))
    along_y[:, 72:144] = -np.kron(two, np.kron(ident, deriv))
    for e in range(2):
        for s2 in range(2):
            for j in range(6):
                lane = e * 12 + s2 * 6 + j
                lift[e * 36 + 6 * j + 5 * s2, 144 + lane] = 1.0
                lift[e * 36 + 30 * s2 + j, 168 + lane] = 1.0
    tables = np.stack([along_x, along_y, lift]).astype(np.float32)
    marks = np.zeros((PAIR, 8), np.float32)
    p = np.arange(PAIR) % 36
    marks[:, 0] = 1.0 * (p // 6 == 5) - 1.0 * (p // 6 == 0)
    marks[:, 1] = 1.0 * (p % 6 == 5) - 1.0 * (p % 6 == 0)
    marks[:, 2] = np.abs(marks[:, 0])
    marks[:, 3] = np.abs(marks[:, 1])
    return tables, marks


def lookup_tables(elems, rows):
    spread = np.zeros((elems, elems // 2 * 32))
    marks = np.zeros((8, elems // 2 * 32), np.float32)
    lane = np.arange(elems // 2 * 32)
    r = lane % 32
    used = r < 24
    e = 2 * (lane // 32) + r % 24 // 12
    spread[e[used], lane[used]] = 1.0
    marks[0] = np.where(used, r % 6, 0)
    marks[1] = np.where(used, r // 6 % 2, 0)
    rim_spread = np.zeros((rows, LANES))
    rim_lane = np.arange(6 * rows)
    rim_spread[rim_lane // 6, rim_lane] = 1.0
    marks[2, : 6 * rows] = rim_lane % 6
    return spread.astype(jnp.bfloat16), rim_spread.astype(jnp.bfloat16), marks


def split(x):
    high = x.astype(BF16)
    low = (x - high.astype(F32)).astype(BF16)
    return high, low


def dot3(a, b, dims):
    go = lambda x, y: lax.dot_general(x, y, (dims, ((), ())), preferred_element_type=F32)
    return go(a[0], b[0]) + (go(a[0], b[1]) + go(a[1], b[0]))


def pieces(src, dst, length):
    out = []
    done = 0
    while done < length:
        s, d = src + done, dst + done
        size = min(length - done, LANES - s % LANES, LANES - d % LANES)
        out.append((s // LANES, d // LANES, (d - s) % LANES, d % LANES, d % LANES + size))
        done += size
    return out


class Builder:
    def __init__(self, lane):
        self.lane = lane
        self.tiles = {}
        self.turned = {}

    def add(self, key, load, src, dst, length):
        for st, dt, shift, lo, hi in pieces(src, dst, length):
            name = (key, st, shift)
            if name not in self.turned:
                tile = load(st)
                self.turned[name] = pltpu.roll(tile, shift, 1) if shift else tile
            value = self.turned[name]
            if dt in self.tiles:
                value = jnp.where((self.lane >= lo) & (self.lane < hi), value, self.tiles[dt])
            self.tiles[dt] = value


def kernel(
    groups, span,
    state, metric, neighbour, orient, wall, rim,
    both_high, both_low, node_tab, node_marks, spread, rim_spread, lane_marks,
    out,
    index, flip, others, rim_send, rim_recv, send_a, send_b, recv_a, recv_b,
    fields, rows_r, back_send, back_recv,
    rim_sems, a_sems, b_sems, back_sems,
):
    me = lax.axis_index("span")
    group = lax.axis_index("elem")
    lower = lax.rem(group + groups - 1, groups)
    upper = lax.rem(group + 1, groups)
    elems = metric.shape[1]
    modes = span * 8
    state_tiles = elems * NODES // LANES
    halves = span // 16

    barrier = pltpu.get_barrier_semaphore()

    def greet(k, carry):
        pl.semaphore_signal(
            barrier, 1, device_id=(group, lax.rem(me + k, span)), device_id_type=MESH
        )
        return carry

    pl.semaphore_signal(barrier, 1, device_id=(lower, me), device_id_type=MESH)
    pl.semaphore_signal(barrier, 1, device_id=(upper, me), device_id_type=MESH)
    lax.fori_loop(1, span, greet, 0)

    def bases(slot, reverse):
        side = slot & 3
        vertical = side >= 2
        step = jnp.where(vertical, 6, 1)
        first = jnp.where(vertical, jnp.where(side == 3, 5, 0), jnp.where(side == 1, 30, 0))
        base = NODES * (slot >> 2) + first
        return base, step

    def spread_over(values, matrix, dims):
        high = (values >> 6).astype(F32).astype(BF16)
        low = (values & 63).astype(F32).astype(BF16)
        go = lambda x: lax.dot_general(x, matrix, (dims, ((), ())), preferred_element_type=F32)
        return (go(high) * 64.0 + go(low)).astype(jnp.int32)

    rim_base, rim_step = bases(rim[...], None)
    natural = ((1,), (0,))
    node_r = lane_marks[2:3, 0:LANES].astype(jnp.int32)
    rim_index = spread_over(rim_base, rim_spread[...], natural) + node_r * spread_over(
        rim_step, rim_spread[...], natural
    )

    slot = neighbour[...]
    turn = orient[...]
    remote = slot >= 4 * elems
    base, step = bases(slot, None)
    row = slot - 4 * elems
    base = jnp.where(remote, state_tiles * LANES + LANES * (row >> 4) + 6 * (row & 15), base)
    step = jnp.where(remote, 1, step)
    base = jnp.where(turn == 1, base + 5 * step, base)
    step = jnp.where(turn == 1, -step, step)
    over = ((0,), (0,))
    matrix = spread[...]
    base_l = spread_over(base, matrix, over)
    step_l = spread_over(step + 64, matrix, over) - 64
    wall_l = spread_over(wall[...], matrix, over)
    node_l = lane_marks[0:1, :].astype(jnp.int32)
    second = lane_marks[1:2, :] > 0.5
    used = spread_over(jnp.ones_like(slot), matrix, over)[0:1] > 0
    for axis in range(2):
        pick = lambda x: jnp.where(second, x[2 * axis + 1 : 2 * axis + 2], x[2 * axis : 2 * axis + 1])
        lanes_at = jnp.where(used, pick(base_l) + pick(step_l) * node_l, 0)
        walls = 1.0 - 2.0 * pick(wall_l).astype(F32)
        for t in range(index.shape[1]):
            cut = slice(t * LANES, (t + 1) * LANES)
            index[axis, t] = jnp.broadcast_to(lanes_at[:, cut], (8, LANES))
            flip[axis, t] = jnp.broadcast_to(walls[:, cut], (8, LANES))

    def gather(at, start, tiles):
        low = at & (LANES - 1)
        high = at >> 7
        totals = list(start)
        for k in tiles:
            here = high == k
            for v in range(4):
                tile = (
                    state[v, :, k * LANES : (k + 1) * LANES]
                    if k < state_tiles
                    else rim_recv[k - state_tiles, v]
                )
                got = jnp.take_along_axis(tile, low, axis=1, mode="promise_in_bounds")
                totals[v] = jnp.where(here, got, totals[v])
        return totals

    zero = [jnp.zeros((8, LANES), F32)] * 4
    for way in range(2):
        at = jnp.broadcast_to(rim_index[way : way + 1], (8, LANES))
        got = gather(at, zero, range(state_tiles))
        for v in range(4):
            rim_send[way, v] = got[v]

    pl.semaphore_wait(barrier, span + 1)

    rim_copies = [
        pltpu.make_async_remote_copy(
            rim_send.at[way], rim_recv.at[1 - way], rim_sems.at[way], rim_sems.at[3 - way],
            device_id=(to, me), device_id_type=MESH,
        )
        for way, to in ((0, lower), (1, upper))
    ]
    for copy in rim_copies:
        copy.start()

    lane = lax.broadcasted_iota(jnp.int32, (8, LANES), 1)

    def gather_axis(axis, tiles, first):
        def one(t, carry):
            at = index[axis, t]
            start = zero if first else [others[axis, v, t] for v in range(4)]
            got = gather(at, start, tiles)
            for v in range(4):
                others[axis, v, t] = got[v]
            return carry

        lax.fori_loop(0, index.shape[1], one, 0)

    gather_axis(1, range(state_tiles), True)

    def reflected(axis, v, t):
        tile = others[axis, v, t]
        return tile * flip[axis, t] if v < 3 else tile

    for d in range(span):
        b = Builder(lane)
        for v in range(4):
            b.add(
                ("own", v),
                lambda k, v=v: state[v, :, k * LANES : (k + 1) * LANES],
                PAIR * d, 96 * v, PAIR,
            )
            b.add(("other", v), lambda k, v=v: reflected(1, v, k), 32 * d, 96 * v + PAIR, 24)
        for k in range(3):
            send_a[d, :, k * LANES : (k + 1) * LANES] = b.tiles[k]

    def exchange(src, dst, sems):
        def one(k, carry):
            to = lax.rem(me + k, span)
            pltpu.make_async_remote_copy(
                src(to), dst(me), sems.at[0], sems.at[1],
                device_id=(group, to), device_id_type=MESH,
            ).start()
            return carry

        lax.fori_loop(1, span, one, 0)
        pltpu.make_async_copy(src(me), dst(me), sems.at[1]).start()

    mode_rows = lambda who: pl.ds(pl.multiple_of(8 * who, 8), 8)
    exchange(lambda to: send_a.at[to], lambda who: recv_a.at[mode_rows(who), :], a_sems)

    gather_axis(0, range(state_tiles), True)
    for copy in rim_copies:
        copy.wait()
    gather_axis(0, range(state_tiles, state_tiles + 2), False)
    for d in range(span):
        b = Builder(lane)
        for v in range(4):
            b.add(("other", v), lambda k, v=v: reflected(0, v, k), 32 * d, 24 * v, 24)
        send_b[d] = b.tiles[0]
    exchange(lambda to: send_b.at[to], lambda who: recv_b.at[mode_rows(who), :], b_sems)

    at = lax.broadcasted_iota(jnp.int32, (2, elems), 1)
    scale = metric[...]
    first = jnp.sum(jnp.where(at == 2 * me, scale, 0.0), axis=1, keepdims=True)
    last = jnp.sum(jnp.where(at == 2 * me + 1, scale, 0.0), axis=1, keepdims=True)

    def per_row(rows, which):
        e = lax.broadcasted_iota(jnp.int32, (rows, 1), 0)
        return jnp.where(e < rows // 2, first[which : which + 1], last[which : which + 1])

    rx, ry = per_row(PAIR, 0), per_row(PAIR, 1)
    marks = node_marks[...]
    coef_u = 7.5 * rx * marks[:, 0:1]
    coef_v = 7.5 * ry * marks[:, 1:2]
    coef_c = 7.5 * (jnp.abs(rx) * marks[:, 2:3] + jnp.abs(ry) * marks[:, 3:4])
    operator = split(rx * node_tab[0] + ry * node_tab[1] + node_tab[2])
    side = lax.broadcasted_iota(jnp.int32, (24, 1), 0)
    low_side = (side < 6) | ((side >= 12) & (side < 18))
    toward = jnp.where(low_side, 7.5, -7.5)
    ox, oy = per_row(24, 0), per_row(24, 1)

    over0 = ((0,), (0,))
    pltpu.make_async_copy(recv_a, recv_a, a_sems.at[1]).wait()
    basis = (both_high[:, 0:modes], both_low[:, 0:modes])
    planes_a = dot3(split(recv_a[...]), basis, over0)
    own = [planes_a[96 * v : 96 * v + PAIR] for v in range(4)]
    facing_y = [planes_a[96 * v + PAIR : 96 * v + 96] for v in range(4)]
    own_coef = coef_u * own[0] + coef_v * own[1] - coef_c
    facing_y_coef = (toward * oy) * facing_y[1] + 7.5 * jnp.abs(oy)
    for v in range(4):
        fields[v, 0:72] = own[0] * own[v]
        fields[v, 72:144] = own[1] * own[v]
        fields[v, 144:168] = facing_y_coef * facing_y[v]
        rows_r[72 * v : 72 * v + 72, modes : 2 * modes] = own[2] * own[v]
        rows_r[72 * v : 72 * v + 72, 0:modes] = own_coef * own[v]

    pltpu.make_async_copy(recv_b, recv_b, b_sems.at[1]).wait()
    planes_b = dot3(split(recv_b[...]), basis, over0)
    facing_x = [planes_b[24 * v : 24 * v + 24] for v in range(4)]
    facing_x_coef = (toward * ox) * facing_x[0] + 7.5 * jnp.abs(ox)
    for v in range(4):
        fields[v, 168:192] = facing_x_coef * facing_x[v]
        rows_r[72 * v : 72 * v + 72, 0:modes] += dot3(operator, split(fields[v]), ((1,), (0,)))

    back_send[:, 0:288] = dot3(
        (both_high[...], both_low[...]), split(rows_r[...]), ((1,), (1,))
    )
    exchange(lambda to: back_send.at[mode_rows(to), :], lambda who: back_recv.at[who], back_sems)
    pltpu.make_async_copy(back_recv, back_recv, back_sems.at[1]).wait()

    mode = 8 * me + lax.broadcasted_iota(jnp.int32, (8, LANES), 0)
    k = jnp.where(mode == 1, modes // 2, mode >> 1).astype(F32)
    shrink = 1.0 / (1.0 + TIME_STEP * VISCOSITY * k * k)
    builders = [Builder(lane) for _ in range(4)]
    for d in range(span):
        for v in range(4):
            builders[v].add(
                d, lambda t, d=d: back_recv[d, :, t * LANES : (t + 1) * LANES],
                PAIR * v, PAIR * d, PAIR,
            )
    for v in range(4):
        for t in range(state_tiles):
            cut = slice(t * LANES, (t + 1) * LANES)
            out[v, :, cut] = (state[v, :, cut] + TIME_STEP * builders[v].tiles[t]) * shrink

    pltpu.make_async_copy(send_a.at[0 : span - 1], send_a.at[0 : span - 1], a_sems.at[0]).wait()
    pltpu.make_async_copy(send_b.at[0 : span - 1], send_b.at[0 : span - 1], b_sems.at[0]).wait()
    sent = back_send.at[0 : 8 * (span - 1), :]
    pltpu.make_async_copy(sent, sent, back_sems.at[0]).wait()


def body(groups, span, state, metric, neighbour, orient, wall, rim):
    elems = metric.shape[1]
    modes = span * 8
    tables, marks = node_tables()
    spread, rim_spread, lane_marks = lookup_tables(elems, rim.shape[1])
    both_high, both_low = basis_tables(modes)
    constants = [both_high, both_low, tables, marks, spread, rim_spread, lane_marks]
    constants = [jnp.asarray(c) for c in constants]
    vmem = pl.BlockSpec(memory_space=pltpu.VMEM)
    gathered = elems // 2 * 32 // LANES
    scratch = [
        pltpu.VMEM((2, gathered, 8, LANES), jnp.int32),
        pltpu.VMEM((2, gathered, 8, LANES), F32),
        pltpu.VMEM((2, 4, gathered, 8, LANES), F32),
        pltpu.VMEM((2, 4, 8, LANES), F32),
        pltpu.VMEM((2, 4, 8, LANES), F32),
        pltpu.VMEM((span, 8, 384), F32),
        pltpu.VMEM((span, 8, LANES), F32),
        pltpu.VMEM((modes, 384), F32),
        pltpu.VMEM((modes, LANES), F32),
        pltpu.VMEM((4, 192, modes), F32),
        pltpu.VMEM((288, 2 * modes), F32),
        pltpu.VMEM((modes, 384), F32),
        pltpu.VMEM((span, 8, 384), F32),
        pltpu.SemaphoreType.DMA((4,)),
        pltpu.SemaphoreType.DMA((2,)),
        pltpu.SemaphoreType.DMA((2,)),
        pltpu.SemaphoreType.DMA((2,)),
    ]
    return pl.pallas_call(
        functools.partial(kernel, groups, span),
        out_shape=jax.ShapeDtypeStruct(state.shape, F32),
        in_specs=[vmem] * 13,
        out_specs=vmem,
        scratch_shapes=scratch,
        compiler_params=pltpu.CompilerParams(
            collective_id=0, has_side_effects=True, vmem_limit_bytes=40 << 20
        ),
        name="section",
    )(state, metric, neighbour, orient, wall, rim, *constants)


def solution(mesh):
    specs = (
        P(None, "span", "elem"), P(None, "elem"), P("elem", None),
        P("elem", None), P("elem", None), P(None, "elem"),
    )
    return jax.shard_map(
        functools.partial(body, mesh.shape["elem"], mesh.shape["span"]),
        mesh=mesh, in_specs=specs, out_specs=P(None, "span", "elem"), check_vma=False,
    )
```

```python
import functools
import math

import jax
import jax.numpy as jnp
import numpy as np
from jax import lax
from jax.experimental import pallas as pl
from jax.experimental.pallas import tpu as pltpu
from jax.sharding import PartitionSpec as P

TIME_STEP = 0.001
VISCOSITY = 0.02
MESH = pl.DeviceIdType.MESH
F32 = jnp.float32
BF16 = jnp.bfloat16
NODES = 36
PAIR = 72
LANES = 128


def differentiation():
    near = math.sqrt(1.0 / 3.0 - 2.0 * math.sqrt(7.0) / 21.0)
    far = math.sqrt(1.0 / 3.0 + 2.0 * math.sqrt(7.0) / 21.0)
    points = np.array([-1.0, -far, -near, near, far, 1.0])
    weights = np.array(
        [1.0 / np.prod([points[c] - points[s] for s in range(6) if s != c]) for c in range(6)]
    )
    deriv = np.zeros((6, 6))
    for t in range(6):
        for s in range(6):
            if s != t:
                deriv[t, s] = weights[s] / weights[t] / (points[t] - points[s])
        deriv[t, t] = -np.sum(deriv[t])
    return deriv


def split_np(x):
    high = x.astype(jnp.bfloat16)
    low = (x - high.astype(np.float64)).astype(jnp.bfloat16)
    return high, low


def basis_tables(count):
    m = np.arange(count)[:, None]
    n = np.arange(count)[None, :]
    angle = (m // 2 * n % count) * (2.0 * math.pi / count)
    basis = np.where(m % 2 == 1, np.sin(angle), np.cos(angle)) * math.sqrt(2.0 / count)
    basis[0] = 1.0 / math.sqrt(count)
    basis[1] = (1.0 - 2.0 * (np.arange(count) % 2)) / math.sqrt(count)
    minus = np.zeros_like(basis)
    k = np.arange(count // 2)[:, None]
    minus[0::2] = -k * basis[1::2]
    minus[1::2] = k * basis[0::2]
    both = np.concatenate([basis, minus], axis=1)
    return split_np(both)


def node_tables():
    deriv = differentiation()
    ident = np.eye(6)
    two = np.eye(2)
    along_x = np.zeros((PAIR, 168))
    along_y = np.zeros((PAIR, 168))
    lift = np.zeros((PAIR, 168))
    lift_x = np.zeros((PAIR, 24))
    along_x[:, 0:72] = -np.kron(two, np.kron(deriv, ident))
    along_y[:, 72:144] = -np.kron(two, np.kron(ident, deriv))
    for e in range(2):
        for s2 in range(2):
            for j in range(6):
                lane = e * 12 + s2 * 6 + j
                lift[e * 36 + 6 * j + 5 * s2, 144 + lane] = 1.0
                lift_x[e * 36 + 30 * s2 + j, lane] = 1.0
    tables = np.stack([along_x, along_y, lift]).astype(np.float32)
    marks = np.zeros((PAIR, 8), np.float32)
    p = np.arange(PAIR) % 36
    marks[:, 0] = 1.0 * (p // 6 == 5) - 1.0 * (p // 6 == 0)
    marks[:, 1] = 1.0 * (p % 6 == 5) - 1.0 * (p % 6 == 0)
    marks[:, 2] = np.abs(marks[:, 0])
    marks[:, 3] = np.abs(marks[:, 1])
    return tables, np.kron(np.eye(4), lift_x).astype(jnp.bfloat16), marks


def lookup_tables(elems, rows):
    spread = np.zeros((elems, elems // 2 * 32))
    marks = np.zeros((8, elems // 2 * 32), np.float32)
    lane = np.arange(elems // 2 * 32)
    r = lane % 32
    used = r < 24
    e = 2 * (lane // 32) + r % 24 // 12
    spread[e[used], lane[used]] = 1.0
    marks[0] = np.where(used, r % 6, 0)
    marks[1] = np.where(used, r // 6 % 2, 0)
    marks[3] = used
    rim_spread = np.zeros((rows, LANES))
    rim_lane = np.arange(6 * rows)
    rim_spread[rim_lane // 6, rim_lane] = 1.0
    marks[2, : 6 * rows] = rim_lane % 6
    return spread.astype(jnp.bfloat16), rim_spread.astype(jnp.bfloat16), marks


def split(x):
    high = x.astype(BF16)
    low = (x - high.astype(F32)).astype(BF16)
    return high, low


def dot3(a, b, dims):
    go = lambda x, y: lax.dot_general(x, y, (dims, ((), ())), preferred_element_type=F32)
    return go(a[0], b[0]) + (go(a[0], b[1]) + go(a[1], b[0]))


def pieces(src, dst, length):
    out = []
    done = 0
    while done < length:
        s, d = src + done, dst + done
        size = min(length - done, LANES - s % LANES, LANES - d % LANES)
        out.append((s // LANES, d // LANES, (d - s) % LANES, d % LANES, d % LANES + size))
        done += size
    return out


class Builder:
    def __init__(self, lane):
        self.lane = lane
        self.tiles = {}
        self.turned = {}

    def add(self, key, load, src, dst, length):
        for st, dt, shift, lo, hi in pieces(src, dst, length):
            name = (key, st, shift)
            if name not in self.turned:
                tile = load(st)
                self.turned[name] = pltpu.roll(tile, shift, 1) if shift else tile
            value = self.turned[name]
            if dt in self.tiles:
                value = jnp.where((self.lane >= lo) & (self.lane < hi), value, self.tiles[dt])
            self.tiles[dt] = value


def kernel(groups, span, *refs):
    given, refs = refs[:14], refs[14:]
    out, refs = refs[0], refs[1:]
    held, refs = refs[:14], refs[14:]
    (
        index, flip, others, rim_send, rim_recv, send_a, send_b, recv_a, recv_b,
        fields, rows_r, back_sum, back_send, back_recv,
        load_sems, rim_sems, a_sems, b_sems, back_sems, hello,
    ) = refs
    (
        state, neighbour, orient, wall, rim, spread, rim_spread, lane_marks,
        metric, node_tab, node_marks, lift_x, both_high, both_low,
    ) = held
    me = lax.axis_index("span")
    group = lax.axis_index("elem")
    lower = lax.rem(group + groups - 1, groups)
    upper = lax.rem(group + 1, groups)
    elems = metric.shape[1]
    modes = span * 8
    state_tiles = elems * NODES // LANES

    loads = [pltpu.make_async_copy(a, b, load_sems.at[i]) for i, (a, b) in enumerate(zip(given, held))]
    for load in loads[:8]:
        load.start()

    barrier = pltpu.get_barrier_semaphore()

    def greet(k, carry):
        pl.semaphore_signal(
            barrier, 1, device_id=(group, lax.rem(me + k, span)), device_id_type=MESH
        )
        return carry

    lax.fori_loop(1, span, greet, 0)
    pl.semaphore_signal(barrier, 1, device_id=(lower, me), device_id_type=MESH)
    for load in loads[8:]:
        load.start()
    for load in loads[1:8]:
        load.wait()

    def bases(slot):
        side = slot & 3
        vertical = side >= 2
        step = jnp.where(vertical, 6, 1)
        first = jnp.where(vertical, jnp.where(side == 3, 5, 0), jnp.where(side == 1, 30, 0))
        return NODES * (slot >> 2) + first, step

    def spread_over(values, matrix):
        high = (values >> 6).astype(F32).astype(BF16)
        low = (values & 63).astype(F32).astype(BF16)
        go = lambda x: jnp.dot(x, matrix, preferred_element_type=F32)
        return (go(high) * 64.0 + go(low)).astype(jnp.int32)

    rim_base, rim_step = bases(rim[...])
    node_r = lane_marks[2:3, 0:LANES].astype(jnp.int32)
    rim_index = spread_over(rim_base, rim_spread[...]) + node_r * spread_over(
        rim_step, rim_spread[...]
    )

    slot = neighbour[...]
    turn = orient[...]
    remote = slot >= 4 * elems
    base, step = bases(slot)
    row = slot - 4 * elems
    base = jnp.where(remote, state_tiles * LANES + LANES * (row >> 4) + 6 * (row & 15), base)
    step = jnp.where(remote, 1, step)
    base = jnp.where(turn == 1, base + 5 * step, base)
    step = jnp.where(turn == 1, -step, step)
    matrix = spread[...]
    base_l = spread_over(base, matrix)
    step_l = spread_over(step + 8, matrix) - 8
    wall_l = spread_over(wall[...], matrix)
    node_l = lane_marks[0:1, :].astype(jnp.int32)
    second = lane_marks[1:2, :] > 0.5
    used = lane_marks[3:4, :] > 0.5
    for axis in range(2):
        pick = lambda x: jnp.where(second, x[2 * axis + 1 : 2 * axis + 2], x[2 * axis : 2 * axis + 1])
        lanes_at = jnp.where(used, pick(base_l) + pick(step_l) * node_l, 0)
        walls = 1.0 - 2.0 * pick(wall_l).astype(F32)
        for t in range(index.shape[1]):
            cut = slice(t * LANES, (t + 1) * LANES)
            index[axis, t] = jnp.broadcast_to(lanes_at[:, cut], (8, LANES))
            flip[axis, t] = jnp.broadcast_to(walls[:, cut], (8, LANES))

    def gather(at, start, tiles):
        low = at & (LANES - 1)
        high = at >> 7
        totals = list(start)
        for k in tiles:
            here = high == k
            for v in range(4):
                tile = (
                    state[v, :, k * LANES : (k + 1) * LANES]
                    if k < state_tiles
                    else rim_recv[k - state_tiles, v]
                )
                got = jnp.take_along_axis(tile, low, axis=1, mode="promise_in_bounds")
                totals[v] = jnp.where(here, got, totals[v])
        return totals

    loads[0].wait()
    zero = [jnp.zeros((8, LANES), F32)] * 4
    for way in range(2):
        at = jnp.broadcast_to(rim_index[way : way + 1], (8, LANES))
        got = gather(at, zero, range(state_tiles))
        for v in range(4):
            rim_send[way, v] = got[v]

    def rim_copy(way, to):
        return pltpu.make_async_remote_copy(
            rim_send.at[way], rim_recv.at[1 - way], rim_sems.at[way], rim_sems.at[3 - way],
            device_id=(to, me), device_id_type=MESH,
        )

    rim_up, rim_down = rim_copy(1, upper), rim_copy(0, lower)
    lane = lax.broadcasted_iota(jnp.int32, (8, LANES), 1)
    row8 = lax.broadcasted_iota(jnp.int32, (8, LANES), 0)

    def gather_axis(axis, tiles, first):
        def one(t, carry):
            at = index[axis, t]
            start = zero if first else [others[axis, v, t] for v in range(4)]
            got = gather(at, start, tiles)
            for v in range(4):
                others[axis, v, t] = got[v]
            return carry

        lax.fori_loop(0, index.shape[1], one, 0)

    gather_axis(1, range(state_tiles), True)

    def reflected(axis, v, t):
        tile = others[axis, v, t]
        return tile * flip[axis, t] if v < 3 else tile

    for d in range(span):
        b = Builder(lane)
        for v in range(4):
            b.add(
                ("own", v),
                lambda k, v=v: state[v, :, k * LANES : (k + 1) * LANES],
                PAIR * d, 96 * v, PAIR,
            )
            b.add(("other", v), lambda k, v=v: reflected(1, v, k), 32 * d, 96 * v + PAIR, 24)
        for k in range(3):
            send_a[d, :, k * LANES : (k + 1) * LANES] = b.tiles[k]

    def exchange(src, dst, sems):
        def one(k, carry):
            to = lax.rem(me + k, span)
            pltpu.make_async_remote_copy(
                src(to), dst(me), sems.at[0], sems.at[1],
                device_id=(group, to), device_id_type=MESH,
            ).start()
            return carry

        lax.fori_loop(1, span, one, 0)
        pltpu.make_async_copy(src(me), dst(me), sems.at[1]).start()

    mode_rows = lambda who: pl.ds(pl.multiple_of(8 * who, 8), 8)

    pl.semaphore_wait(barrier, span)
    pl.semaphore_signal(hello, 1, device_id=(upper, me), device_id_type=MESH)
    rim_up.start()
    exchange(lambda to: send_a.at[to], lambda who: recv_a.at[mode_rows(who), :], a_sems)

    gather_axis(0, range(state_tiles), True)
    pl.semaphore_wait(hello, 1)
    rim_down.start()

    for load in loads[8:]:
        load.wait()
    at = lax.broadcasted_iota(jnp.int32, (2, elems), 1)
    scale = metric[...]
    first = jnp.sum(jnp.where(at == 2 * me, scale, 0.0), axis=1, keepdims=True)
    last = jnp.sum(jnp.where(at == 2 * me + 1, scale, 0.0), axis=1, keepdims=True)

    def per_row(rows, which):
        e = lax.broadcasted_iota(jnp.int32, (rows, 1), 0)
        return jnp.where(e < rows // 2, first[which : which + 1], last[which : which + 1])

    rx, ry = per_row(PAIR, 0), per_row(PAIR, 1)
    marks = node_marks[...]
    coef_u = 7.5 * rx * marks[:, 0:1]
    coef_v = 7.5 * ry * marks[:, 1:2]
    coef_c = 7.5 * (jnp.abs(rx) * marks[:, 2:3] + jnp.abs(ry) * marks[:, 3:4])
    operator = split(rx * node_tab[0] + ry * node_tab[1] + node_tab[2])
    side = lax.broadcasted_iota(jnp.int32, (24, 1), 0)
    low_side = (side < 6) | ((side >= 12) & (side < 18))
    toward = jnp.where(low_side, 7.5, -7.5)
    ox, oy = per_row(24, 0), per_row(24, 1)

    rim_up.wait()
    rim_down.wait()
    gather_axis(0, range(state_tiles, state_tiles + 2), False)
    for d in range(span):
        b = Builder(lane)
        for v in range(4):
            b.add(("other", v), lambda k, v=v: reflected(0, v, k), 32 * d, 24 * v, 24)
        send_b[d] = b.tiles[0]
    exchange(lambda to: send_b.at[to], lambda who: recv_b.at[mode_rows(who), :], b_sems)

    over0, over1 = ((0,), (0,)), ((1,), (1,))
    pltpu.make_async_copy(recv_a, recv_a, a_sems.at[1]).wait()
    basis = (both_high[:, 0:modes], both_low[:, 0:modes])
    planes_a = dot3(split(recv_a[...]), basis, over0)
    own = [planes_a[96 * v : 96 * v + PAIR] for v in range(4)]
    facing_y = [planes_a[96 * v + PAIR : 96 * v + 96] for v in range(4)]
    own_coef = coef_u * own[0] + coef_v * own[1] - coef_c
    facing_y_coef = (toward * oy) * facing_y[1] + 7.5 * jnp.abs(oy)
    for v in range(4):
        fields[v, 0:72] = own[0] * own[v]
        fields[v, 72:144] = own[1] * own[v]
        fields[v, 144:168] = facing_y_coef * facing_y[v]
        rows_r[72 * v : 72 * v + 72, modes : 2 * modes] = own[2] * own[v]
        rows_r[72 * v : 72 * v + 72, 0:modes] = own_coef * own[v] + dot3(
            operator, split(fields[v]), ((1,), (0,))
        )
    back_sum[:, 0:288] = dot3((both_high[...], both_low[...]), split(rows_r[...]), over1)

    pltpu.make_async_copy(recv_b, recv_b, b_sems.at[1]).wait()
    planes_b = dot3(split(recv_b[:, 0:96]), basis, over0)
    facing_x_coef = (toward * ox) * planes_b[0:24] + 7.5 * jnp.abs(ox)
    jump_high, jump_low = split(jnp.concatenate([facing_x_coef] * 4, axis=0) * planes_b)
    lifted = [
        jnp.dot(lift_x[...], part, preferred_element_type=F32).astype(BF16)
        for part in (jump_high, jump_low)
    ]
    back_sum[:, 0:288] += dot3(basis, lifted, over1)

    for d in range(span):
        mine = back_sum[8 * d : 8 * d + 8, :]
        back_send[18 * d : 18 * d + 8, :] = mine[:, 0:LANES]
        back_send[18 * d + 8 : 18 * d + 16, :] = mine[:, LANES : 2 * LANES]
        rest = jnp.take_along_axis(mine[:, 2 * LANES :], lane & 31, axis=1, mode="promise_in_bounds")
        rest = jnp.where((lane >> 5) == (row8 & 3), rest, 0.0)
        for a in range(2):
            back_send[18 * d + 16 + a : 18 * d + 17 + a, :] = jnp.sum(
                rest[4 * a : 4 * a + 4], axis=0, keepdims=True
            )
    message = lambda who: pl.ds(18 * who, 18)
    exchange(
        lambda to: back_send.at[message(to), :], lambda who: back_recv.at[message(who), :], back_sems
    )
    pltpu.make_async_copy(back_recv, back_recv, back_sems.at[1]).wait()

    mode = 8 * me + row8
    k = jnp.where(mode == 1, modes // 2, mode >> 1).astype(F32)
    shrink = 1.0 / (1.0 + TIME_STEP * VISCOSITY * k * k)
    top = row8 < 4
    unfold = (lane & 31) + 32 * (row8 & 3)

    def unfolded(s, t):
        if t < 2:
            return back_recv[18 * s + 8 * t : 18 * s + 8 * t + 8, :]
        rest = jnp.where(
            top, back_recv[18 * s + 16 : 18 * s + 17, :], back_recv[18 * s + 17 : 18 * s + 18, :]
        )
        return jnp.take_along_axis(rest, unfold, axis=1, mode="promise_in_bounds")

    builders = [Builder(lane) for _ in range(4)]
    for s in range(span):
        for v in range(4):
            builders[v].add(s, lambda t, s=s: unfolded(s, t), PAIR * v, PAIR * s, PAIR)
    for v in range(4):
        for t in range(state_tiles):
            cut = slice(t * LANES, (t + 1) * LANES)
            out[v, :, cut] = (state[v, :, cut] + TIME_STEP * builders[v].tiles[t]) * shrink

    pltpu.make_async_copy(send_a.at[0 : span - 1], send_a.at[0 : span - 1], a_sems.at[0]).wait()
    pltpu.make_async_copy(send_b.at[0 : span - 1], send_b.at[0 : span - 1], b_sems.at[0]).wait()
    sent = back_send.at[0 : 18 * (span - 1), :]
    pltpu.make_async_copy(sent, sent, back_sems.at[0]).wait()


def body(groups, span, state, metric, neighbour, orient, wall, rim):
    elems = metric.shape[1]
    modes = span * 8
    tables, lift_x, marks = node_tables()
    spread, rim_spread, lane_marks = lookup_tables(elems, rim.shape[1])
    both_high, both_low = basis_tables(modes)
    given = [
        state, neighbour.T, orient.T, wall.T, rim, spread, rim_spread, lane_marks,
        metric, tables, marks, lift_x, both_high, both_low,
    ]
    given = [jnp.asarray(x) for x in given]
    gathered = elems // 2 * 32 // LANES
    scratch = [pltpu.VMEM(x.shape, x.dtype) for x in given] + [
        pltpu.VMEM((2, gathered, 8, LANES), jnp.int32),
        pltpu.VMEM((2, gathered, 8, LANES), F32),
        pltpu.VMEM((2, 4, gathered, 8, LANES), F32),
        pltpu.VMEM((2, 4, 8, LANES), F32),
        pltpu.VMEM((2, 4, 8, LANES), F32),
        pltpu.VMEM((span, 8, 384), F32),
        pltpu.VMEM((span, 8, LANES), F32),
        pltpu.VMEM((modes, 384), F32),
        pltpu.VMEM((modes, LANES), F32),
        pltpu.VMEM((4, 168, modes), F32),
        pltpu.VMEM((288, 2 * modes), F32),
        pltpu.VMEM((modes, 384), F32),
        pltpu.VMEM((18 * span, LANES), F32),
        pltpu.VMEM((18 * span, LANES), F32),
        pltpu.SemaphoreType.DMA((len(given),)),
        pltpu.SemaphoreType.DMA((4,)),
        pltpu.SemaphoreType.DMA((2,)),
        pltpu.SemaphoreType.DMA((2,)),
        pltpu.SemaphoreType.DMA((2,)),
        pltpu.SemaphoreType.REGULAR,
    ]
    return pl.pallas_call(
        functools.partial(kernel, groups, span),
        out_shape=jax.ShapeDtypeStruct(state.shape, F32),
        in_specs=[pl.BlockSpec(memory_space=pltpu.HBM)] * len(given),
        out_specs=pl.BlockSpec(memory_space=pltpu.VMEM),
        scratch_shapes=scratch,
        compiler_params=pltpu.CompilerParams(
            collective_id=0, has_side_effects=True, vmem_limit_bytes=60 << 20
        ),
        name="section",
    )(*given)


def solution(mesh):
    specs = (
        P(None, "span", "elem"), P(None, "elem"), P("elem", None),
        P("elem", None), P("elem", None), P(None, "elem"),
    )
    return jax.shard_map(
        functools.partial(body, mesh.shape["elem"], mesh.shape["span"]),
        mesh=mesh, in_specs=specs, out_specs=P(None, "span", "elem"), check_vma=False,
    )
```

```python
import functools
import math

import jax
import jax.numpy as jnp
import numpy as np
from jax import lax
from jax.experimental import pallas as pl
from jax.experimental.pallas import tpu as pltpu
from jax.sharding import PartitionSpec as P

TIME_STEP = 0.001
VISCOSITY = 0.02
MESH = pl.DeviceIdType.MESH
F32 = jnp.float32
BF16 = jnp.bfloat16
NODES = 36
PAIR = 72
LANES = 128


def differentiation():
    near = math.sqrt(1.0 / 3.0 - 2.0 * math.sqrt(7.0) / 21.0)
    far = math.sqrt(1.0 / 3.0 + 2.0 * math.sqrt(7.0) / 21.0)
    points = np.array([-1.0, -far, -near, near, far, 1.0])
    weights = np.array(
        [1.0 / np.prod([points[c] - points[s] for s in range(6) if s != c]) for c in range(6)]
    )
    deriv = np.zeros((6, 6))
    for t in range(6):
        for s in range(6):
            if s != t:
                deriv[t, s] = weights[s] / weights[t] / (points[t] - points[s])
        deriv[t, t] = -np.sum(deriv[t])
    return deriv


def split_np(x):
    high = x.astype(jnp.bfloat16)
    low = (x - high.astype(np.float64)).astype(jnp.bfloat16)
    return high, low


def basis_tables(count):
    m = np.arange(count)[:, None]
    n = np.arange(count)[None, :]
    angle = (m // 2 * n % count) * (2.0 * math.pi / count)
    basis = np.where(m % 2 == 1, np.sin(angle), np.cos(angle)) * math.sqrt(2.0 / count)
    basis[0] = 1.0 / math.sqrt(count)
    basis[1] = (1.0 - 2.0 * (np.arange(count) % 2)) / math.sqrt(count)
    minus = np.zeros_like(basis)
    k = np.arange(count // 2)[:, None]
    minus[0::2] = -k * basis[1::2]
    minus[1::2] = k * basis[0::2]
    both = np.concatenate([basis, minus], axis=1)
    return split_np(both)


def node_tables():
    deriv = differentiation()
    ident = np.eye(6)
    two = np.eye(2)
    along_x = np.zeros((PAIR, 144))
    along_y = np.zeros((PAIR, 144))
    lift = np.zeros((PAIR, 48))
    along_x[:, 0:72] = -np.kron(two, np.kron(deriv, ident))
    along_y[:, 72:144] = -np.kron(two, np.kron(ident, deriv))
    for e in range(2):
        for s2 in range(2):
            for j in range(6):
                lane = e * 12 + s2 * 6 + j
                lift[e * 36 + 6 * j + 5 * s2, lane] = 1.0
                lift[e * 36 + 30 * s2 + j, 24 + lane] = 1.0
    tables = np.stack([along_x, along_y]).astype(np.float32)
    marks = np.zeros((PAIR, 8), np.float32)
    p = np.arange(PAIR) % 36
    marks[:, 0] = 1.0 * (p // 6 == 5) - 1.0 * (p // 6 == 0)
    marks[:, 1] = 1.0 * (p % 6 == 5) - 1.0 * (p % 6 == 0)
    marks[:, 2] = np.abs(marks[:, 0])
    marks[:, 3] = np.abs(marks[:, 1])
    return tables, np.kron(np.eye(4), lift).astype(jnp.bfloat16), marks


def lookup_tables(elems, rows):
    spread = np.zeros((elems, elems // 2 * 32))
    marks = np.zeros((8, elems // 2 * 32), np.float32)
    lane = np.arange(elems // 2 * 32)
    r = lane % 32
    used = r < 24
    e = 2 * (lane // 32) + r % 24 // 12
    spread[e[used], lane[used]] = 1.0
    marks[0] = np.where(used, r % 6, 0)
    marks[1] = np.where(used, r // 6 % 2, 0)
    marks[3] = used
    rim_spread = np.zeros((rows, LANES))
    rim_lane = np.arange(6 * rows)
    rim_spread[rim_lane // 6, rim_lane] = 1.0
    marks[2, : 6 * rows] = rim_lane % 6
    return spread.astype(jnp.bfloat16), rim_spread.astype(jnp.bfloat16), marks


def split(x):
    high = x.astype(BF16)
    low = (x - high.astype(F32)).astype(BF16)
    return high, low


def dot3(a, b, dims):
    go = lambda x, y: lax.dot_general(x, y, (dims, ((), ())), preferred_element_type=F32)
    return go(a[0], b[0]) + (go(a[0], b[1]) + go(a[1], b[0]))


def pieces(src, dst, length):
    out = []
    done = 0
    while done < length:
        s, d = src + done, dst + done
        size = min(length - done, LANES - s % LANES, LANES - d % LANES)
        out.append((s // LANES, d // LANES, (d - s) % LANES, d % LANES, d % LANES + size))
        done += size
    return out


class Builder:
    def __init__(self, lane):
        self.lane = lane
        self.tiles = {}
        self.turned = {}

    def add(self, key, load, src, dst, length):
        for st, dt, shift, lo, hi in pieces(src, dst, length):
            name = (key, st, shift)
            if name not in self.turned:
                tile = load(st)
                self.turned[name] = pltpu.roll(tile, shift, 1) if shift else tile
            value = self.turned[name]
            if dt in self.tiles:
                value = jnp.where((self.lane >= lo) & (self.lane < hi), value, self.tiles[dt])
            self.tiles[dt] = value


OWN_ROWS = 18
FACING_ROWS = 12


def kernel(groups, span, *refs):
    given, refs = refs[:14], refs[14:]
    out, refs = refs[0], refs[1:]
    held, refs = refs[:14], refs[14:]
    (
        index, flip, others, rim_send, rim_recv, send_a, send_b, recv_a, recv_b, coef_a, coef_b,
        fields, rows_r, back_sum, back_send, back_recv,
        load_sems, rim_sems, a_sems, b_sems, back_sems, hello,
    ) = refs
    (
        state, rim, rim_spread, lane_marks, neighbour, orient, wall, spread,
        metric, node_tab, node_marks, lift, both_high, both_low,
    ) = held
    me = lax.axis_index("span")
    group = lax.axis_index("elem")
    lower = lax.rem(group + groups - 1, groups)
    upper = lax.rem(group + 1, groups)
    elems = metric.shape[1]
    modes = span * 8
    state_tiles = elems * NODES // LANES

    loads = [pltpu.make_async_copy(a, b, load_sems.at[i]) for i, (a, b) in enumerate(zip(given, held))]
    for load in loads[:4]:
        load.start()

    barrier = pltpu.get_barrier_semaphore()

    def greet(k, carry):
        pl.semaphore_signal(
            barrier, 1, device_id=(group, lax.rem(me + k, span)), device_id_type=MESH
        )
        return carry

    pl.semaphore_signal(barrier, 1, device_id=(lower, me), device_id_type=MESH)
    lax.fori_loop(1, span, greet, 0)
    for load in loads[4:]:
        load.start()

    lane = lax.broadcasted_iota(jnp.int32, (8, LANES), 1)
    row8 = lax.broadcasted_iota(jnp.int32, (8, LANES), 0)

    def bases(slot):
        side = slot & 3
        vertical = side >= 2
        step = jnp.where(vertical, 6, 1)
        first = jnp.where(vertical, jnp.where(side == 3, 5, 0), jnp.where(side == 1, 30, 0))
        return NODES * (slot >> 2) + first, step

    def spread_over(values, matrix):
        high = (values >> 6).astype(F32).astype(BF16)
        low = (values & 63).astype(F32).astype(BF16)
        go = lambda x: jnp.dot(x, matrix, preferred_element_type=F32)
        return (go(high) * 64.0 + go(low)).astype(jnp.int32)

    def picked(tile, at):
        return jnp.take_along_axis(tile, at, axis=1, mode="promise_in_bounds")

    def gather(at, start, tiles):
        low = at & (LANES - 1)
        high = at >> 7
        totals = list(start)
        for k in tiles:
            here = high == k
            for v in range(4):
                tile = (
                    state[v, :, k * LANES : (k + 1) * LANES]
                    if k < state_tiles
                    else rim_recv[k - state_tiles, v]
                )
                totals[v] = jnp.where(here, picked(tile, low), totals[v])
        return totals

    def fold(tile, width, store):
        every = LANES // width
        tile = jnp.where(lane // width == (row8 & (every - 1)), picked(tile, lane & (width - 1)), 0.0)
        for a in range(8 // every):
            store(a, jnp.sum(tile[every * a : every * (a + 1)], axis=0, keepdims=True))

    def unfold(load, width):
        every = LANES // width
        tile = load(0)
        for a in range(1, 8 // every):
            tile = jnp.where(row8 < every * a, tile, load(a))
        return picked(jnp.broadcast_to(tile, (8, LANES)), (lane & (width - 1)) + width * (row8 & (every - 1)))

    for load in loads[1:4]:
        load.wait()
    rim_base, rim_step = bases(rim[...])
    node_r = lane_marks[2:3, 0:LANES].astype(jnp.int32)
    rim_index = spread_over(rim_base, rim_spread[...]) + node_r * spread_over(
        rim_step, rim_spread[...]
    )
    loads[0].wait()
    zero = [jnp.zeros((8, LANES), F32)] * 4
    for way in range(2):
        at = jnp.broadcast_to(rim_index[way : way + 1], (8, LANES))
        got = gather(at, zero, range(state_tiles))
        for v in range(4):
            rim_send[way, v] = got[v]

    def rim_copy(way, to):
        return pltpu.make_async_remote_copy(
            rim_send.at[way], rim_recv.at[1 - way], rim_sems.at[way], rim_sems.at[3 - way],
            device_id=(to, me), device_id_type=MESH,
        )

    rim_up, rim_down = rim_copy(1, upper), rim_copy(0, lower)
    pl.semaphore_wait(barrier, span)
    pl.semaphore_signal(hello, 1, device_id=(upper, me), device_id_type=MESH)
    rim_up.start()

    def exchange(send, recv, rows, sems, near=None):
        arrived = sems.at[1] if near is None else sems.at[1 + near]
        at = lambda who: pl.ds(rows * who, rows)

        def one(k, carry):
            to = lax.rem(me + k, span)
            pltpu.make_async_remote_copy(
                send.at[at(to), :], recv.at[at(me), :], sems.at[0], arrived,
                device_id=(group, to), device_id_type=MESH,
            ).start()
            return carry

        lax.fori_loop(1, span, one, 0)
        pltpu.make_async_copy(send.at[at(me), :], recv.at[at(me), :], arrived).start()

    for d in range(span):
        b = Builder(lane)
        for v in range(4):
            b.add(v, lambda k, v=v: state[v, :, k * LANES : (k + 1) * LANES], PAIR * d, PAIR * v, PAIR)
        top = OWN_ROWS * d
        send_a[top : top + 8, :] = b.tiles[0]
        send_a[top + 8 : top + 16, :] = b.tiles[1]

        def store(a, row, top=top):
            send_a[top + 16 + a : top + 17 + a, :] = row

        fold(b.tiles[2], 32, store)

    @pl.when(group > 0)
    def _():
        pl.semaphore_wait(hello, 1)
        rim_down.start()

    exchange(send_a, recv_a, OWN_ROWS, a_sems)

    for load in loads[4:8]:
        load.wait()
    slot = neighbour[...]
    turn = orient[...]
    remote = slot >= 4 * elems
    base, step = bases(slot)
    row = slot - 4 * elems
    base = jnp.where(remote, state_tiles * LANES + LANES * (row >> 4) + 6 * (row & 15), base)
    step = jnp.where(remote, 1, step)
    base = jnp.where(turn == 1, base + 5 * step, base)
    step = jnp.where(turn == 1, -step, step)
    matrix = spread[...]
    base_l = spread_over(base, matrix)
    step_l = spread_over(step + 8, matrix) - 8
    wall_l = spread_over(wall[...], matrix)
    node_l = lane_marks[0:1, :].astype(jnp.int32)
    second = lane_marks[1:2, :] > 0.5
    used = lane_marks[3:4, :] > 0.5
    for axis in range(2):
        pick = lambda x: jnp.where(second, x[2 * axis + 1 : 2 * axis + 2], x[2 * axis : 2 * axis + 1])
        lanes_at = jnp.where(used, pick(base_l) + pick(step_l) * node_l, 0)
        walls = 1.0 - 2.0 * pick(wall_l).astype(F32)
        for t in range(index.shape[1]):
            cut = slice(t * LANES, (t + 1) * LANES)
            index[axis, t] = jnp.broadcast_to(lanes_at[:, cut], (8, LANES))
            flip[axis, t] = jnp.broadcast_to(walls[:, cut], (8, LANES))

    def gather_axis(axis, tiles, first):
        def one(t, carry):
            at = index[axis, t]
            start = zero if first else [others[axis, v, t] for v in range(4)]
            got = gather(at, start, tiles)
            for v in range(4):
                others[axis, v, t] = got[v]
            return carry

        lax.fori_loop(0, index.shape[1], one, 0)

    gather_axis(0, range(state_tiles), True)
    gather_axis(1, range(state_tiles), True)

    @pl.when(group == 0)
    def _():
        pl.semaphore_wait(hello, 1)
        rim_down.start()

    rim_up.wait()
    rim_down.wait()
    gather_axis(0, range(state_tiles, state_tiles + 2), False)

    def reflected(axis, v, t):
        tile = others[axis, v, t]
        return tile * flip[axis, t] if v < 3 else tile

    for d in range(span):
        b = Builder(lane)
        for v in range(4):
            for axis in range(2):
                b.add(
                    (axis, v), lambda k, a=axis, v=v: reflected(a, v, k),
                    32 * d, 48 * v + 24 * (1 - axis), 24,
                )
        top = FACING_ROWS * d
        send_b[top : top + 8, :] = b.tiles[0]

        def store(a, row, top=top):
            send_b[top + 8 + a : top + 9 + a, :] = row

        fold(b.tiles[1], 64, store)
    exchange(send_b, recv_b, FACING_ROWS, b_sems)

    for load in loads[8:]:
        load.wait()
    at = lax.broadcasted_iota(jnp.int32, (2, elems), 1)
    scale = metric[...]
    first = jnp.sum(jnp.where(at == 2 * me, scale, 0.0), axis=1, keepdims=True)
    last = jnp.sum(jnp.where(at == 2 * me + 1, scale, 0.0), axis=1, keepdims=True)

    def per_row(rows, which):
        e = lax.broadcasted_iota(jnp.int32, (rows, 1), 0)
        return jnp.where(e < rows // 2, first[which : which + 1], last[which : which + 1])

    rx, ry = per_row(PAIR, 0), per_row(PAIR, 1)
    marks = node_marks[...]
    coef_u = 7.5 * rx * marks[:, 0:1]
    coef_v = 7.5 * ry * marks[:, 1:2]
    coef_c = 7.5 * (jnp.abs(rx) * marks[:, 2:3] + jnp.abs(ry) * marks[:, 3:4])
    operator = split(rx * node_tab[0] + ry * node_tab[1])
    side = lax.broadcasted_iota(jnp.int32, (24, 1), 0)
    low_side = (side < 6) | ((side >= 12) & (side < 18))
    toward = jnp.where(low_side, 7.5, -7.5)
    ox, oy = per_row(24, 0), per_row(24, 1)

    over0, over1 = ((0,), (0,)), ((1,), (1,))
    basis = (both_high[:, 0:modes], both_low[:, 0:modes])
    pltpu.make_async_copy(recv_a, recv_a, a_sems.at[1]).wait()
    for s in range(span):
        top = OWN_ROWS * s
        cut = slice(8 * s, 8 * s + 8)
        coef_a[cut, 0:LANES] = recv_a[top : top + 8, :]
        coef_a[cut, LANES : 2 * LANES] = recv_a[top + 8 : top + 16, :]
        coef_a[cut, 2 * LANES :] = unfold(lambda a: recv_a[top + 16 + a : top + 17 + a, :], 32)
    planes_a = dot3(split(coef_a[:, 0:288]), basis, over0)
    own = [planes_a[PAIR * v : PAIR * (v + 1)] for v in range(4)]
    own_coef = coef_u * own[0] + coef_v * own[1] - coef_c
    for v in range(4):
        fields[v, 0:72] = own[0] * own[v]
        fields[v, 72:144] = own[1] * own[v]
        rows_r[72 * v : 72 * v + 72, modes : 2 * modes] = own[2] * own[v]
        rows_r[72 * v : 72 * v + 72, 0:modes] = own_coef * own[v] + dot3(
            operator, split(fields[v]), ((1,), (0,))
        )
    back_sum[:, 0:288] = dot3((both_high[...], both_low[...]), split(rows_r[...]), over1)

    pltpu.make_async_copy(recv_b, recv_b, b_sems.at[1]).wait()
    for s in range(span):
        top = FACING_ROWS * s
        cut = slice(8 * s, 8 * s + 8)
        coef_b[cut, 0:LANES] = recv_b[top : top + 8, :]
        coef_b[cut, LANES:] = unfold(lambda a: recv_b[top + 8 + a : top + 9 + a, :], 64)
    planes_b = dot3(split(coef_b[:, 0:192]), basis, over0)
    facing_coef = jnp.concatenate(
        [
            (toward * oy) * planes_b[48:72] + 7.5 * jnp.abs(oy),
            (toward * ox) * planes_b[24:48] + 7.5 * jnp.abs(ox),
        ],
        axis=0,
    )
    jump_high, jump_low = split(jnp.concatenate([facing_coef] * 4, axis=0) * planes_b)
    lifted = split(
        jnp.dot(lift[...], jump_high, preferred_element_type=F32)
        + jnp.dot(lift[...], jump_low, preferred_element_type=F32)
    )
    back_sum[:, 0:288] += dot3(basis, lifted, over1)

    for d in range(span):
        top = OWN_ROWS * d
        mine = back_sum[8 * d : 8 * d + 8, :]
        back_send[top : top + 8, :] = mine[:, 0:LANES]
        back_send[top + 8 : top + 16, :] = mine[:, LANES : 2 * LANES]

        def store(a, row, top=top):
            back_send[top + 16 + a : top + 17 + a, :] = row

        fold(mine[:, 2 * LANES :], 32, store)
    half = span // 2
    near = me // half
    exchange(back_send, back_recv, OWN_ROWS, back_sems, near)

    mode = 8 * me + row8
    k = jnp.where(mode == 1, modes // 2, mode >> 1).astype(F32)
    shrink = 1.0 / (1.0 + TIME_STEP * VISCOSITY * k * k)

    def finish(i, carry):
        h = lax.rem(near + i, 2)
        part = back_recv.at[pl.ds(pl.multiple_of(OWN_ROWS * half * h, 8), OWN_ROWS * half), :]
        pltpu.make_async_copy(part, part, back_sems.at[1 + h]).wait()
        builders = [Builder(lane) for _ in range(4)]

        def back(s, t):
            top = OWN_ROWS * s
            if t < 2:
                return part[top + 8 * t : top + 8 * t + 8, :]
            return unfold(lambda a: part[top + 16 + a : top + 17 + a, :], 32)

        for s in range(half):
            for v in range(4):
                builders[v].add(s, lambda t, s=s: back(s, t), PAIR * v, PAIR * s, PAIR)
        for v in range(4):
            for t in range(state_tiles // 2):
                cut = pl.ds(pl.multiple_of((state_tiles // 2 * h + t) * LANES, LANES), LANES)
                out[v, :, cut] = (state[v, :, cut] + TIME_STEP * builders[v].tiles[t]) * shrink
        return carry

    lax.fori_loop(0, 2, finish, 0)

    for send, rows, sems in (
        (send_a, OWN_ROWS, a_sems), (send_b, FACING_ROWS, b_sems), (back_send, OWN_ROWS, back_sems),
    ):
        sent = send.at[0 : rows * (span - 1), :]
        pltpu.make_async_copy(sent, sent, sems.at[0]).wait()


def body(groups, span, state, metric, neighbour, orient, wall, rim):
    elems = metric.shape[1]
    modes = span * 8
    tables, lift, marks = node_tables()
    spread, rim_spread, lane_marks = lookup_tables(elems, rim.shape[1])
    both_high, both_low = basis_tables(modes)
    given = [
        state, rim, rim_spread, lane_marks, neighbour.T, orient.T, wall.T, spread,
        metric, tables, marks, lift, both_high, both_low,
    ]
    given = [jnp.asarray(x) for x in given]
    gathered = elems // 2 * 32 // LANES
    scratch = [pltpu.VMEM(x.shape, x.dtype) for x in given] + [
        pltpu.VMEM((2, gathered, 8, LANES), jnp.int32),
        pltpu.VMEM((2, gathered, 8, LANES), F32),
        pltpu.VMEM((2, 4, gathered, 8, LANES), F32),
        pltpu.VMEM((2, 4, 8, LANES), F32),
        pltpu.VMEM((2, 4, 8, LANES), F32),
        pltpu.VMEM((OWN_ROWS * span, LANES), F32),
        pltpu.VMEM((FACING_ROWS * span, LANES), F32),
        pltpu.VMEM((OWN_ROWS * span, LANES), F32),
        pltpu.VMEM((FACING_ROWS * span, LANES), F32),
        pltpu.VMEM((modes, 384), F32),
        pltpu.VMEM((modes, 256), F32),
        pltpu.VMEM((4, 144, modes), F32),
        pltpu.VMEM((288, 2 * modes), F32),
        pltpu.VMEM((modes, 384), F32),
        pltpu.VMEM((OWN_ROWS * span, LANES), F32),
        pltpu.VMEM((OWN_ROWS * span, LANES), F32),
        pltpu.SemaphoreType.DMA((len(given),)),
        pltpu.SemaphoreType.DMA((4,)),
        pltpu.SemaphoreType.DMA((2,)),
        pltpu.SemaphoreType.DMA((2,)),
        pltpu.SemaphoreType.DMA((3,)),
        pltpu.SemaphoreType.REGULAR,
    ]
    return pl.pallas_call(
        functools.partial(kernel, groups, span),
        out_shape=jax.ShapeDtypeStruct(state.shape, F32),
        in_specs=[pl.BlockSpec(memory_space=pltpu.HBM)] * len(given),
        out_specs=pl.BlockSpec(memory_space=pltpu.VMEM),
        scratch_shapes=scratch,
        compiler_params=pltpu.CompilerParams(
            collective_id=0, has_side_effects=True, vmem_limit_bytes=60 << 20
        ),
        name="section",
    )(*given)


def solution(mesh):
    specs = (
        P(None, "span", "elem"), P(None, "elem"), P("elem", None),
        P("elem", None), P("elem", None), P(None, "elem"),
    )
    return jax.shard_map(
        functools.partial(body, mesh.shape["elem"], mesh.shape["span"]),
        mesh=mesh, in_specs=specs, out_specs=P(None, "span", "elem"), check_vma=False,
    )
```

```python
import functools
import math

import jax
import jax.numpy as jnp
import numpy as np
from jax import lax
from jax.experimental import pallas as pl
from jax.experimental.pallas import tpu as pltpu
from jax.sharding import PartitionSpec as P

TIME_STEP = 0.001
VISCOSITY = 0.02
MESH = pl.DeviceIdType.MESH
F32 = jnp.float32
BF16 = jnp.bfloat16
NODES = 36
PAIR = 72
LANES = 128
INNER = ((6, 30), (42, 66))
OUTER = ((0, 6), (30, 36), (36, 42), (66, 72))


def differentiation():
    near = math.sqrt(1.0 / 3.0 - 2.0 * math.sqrt(7.0) / 21.0)
    far = math.sqrt(1.0 / 3.0 + 2.0 * math.sqrt(7.0) / 21.0)
    points = np.array([-1.0, -far, -near, near, far, 1.0])
    weights = np.array(
        [1.0 / np.prod([points[c] - points[s] for s in range(6) if s != c]) for c in range(6)]
    )
    deriv = np.zeros((6, 6))
    for t in range(6):
        for s in range(6):
            if s != t:
                deriv[t, s] = weights[s] / weights[t] / (points[t] - points[s])
        deriv[t, t] = -np.sum(deriv[t])
    return deriv


def split_np(x):
    high = x.astype(jnp.bfloat16)
    low = (x - high.astype(np.float64)).astype(jnp.bfloat16)
    return high, low


def basis_tables(count):
    m = np.arange(count)[:, None]
    n = np.arange(count)[None, :]
    angle = (m // 2 * n % count) * (2.0 * math.pi / count)
    basis = np.where(m % 2 == 1, np.sin(angle), np.cos(angle)) * math.sqrt(2.0 / count)
    basis[0] = 1.0 / math.sqrt(count)
    basis[1] = (1.0 - 2.0 * (np.arange(count) % 2)) / math.sqrt(count)
    minus = np.zeros_like(basis)
    k = np.arange(count // 2)[:, None]
    minus[0::2] = -k * basis[1::2]
    minus[1::2] = k * basis[0::2]
    both = np.concatenate([basis, minus], axis=1)
    return split_np(both)


def node_tables():
    deriv = differentiation()
    ident = np.eye(6)
    two = np.eye(2)
    along_x = np.zeros((PAIR, 168))
    along_y = np.zeros((PAIR, 168))
    lift = np.zeros((PAIR, 168))
    order = np.concatenate([np.arange(a, b) for a, b in INNER + OUTER])
    along_x[:, 0:72] = -np.kron(two, np.kron(deriv, ident))[order][:, order]
    along_y[:, 72:144] = -np.kron(two, np.kron(ident, deriv))[order][:, order]
    for e in range(2):
        for s2 in range(2):
            for j in range(6):
                lift[e * 36 + 6 * j + 5 * s2, 144 + e * 12 + s2 * 6 + j] = 1.0
    lift = lift[order]
    tables = np.stack([along_x, along_y, lift]).astype(np.float32)
    marks = np.zeros((PAIR, 8), np.float32)
    p = order % 36
    marks[:, 0] = 1.0 * (p // 6 == 5) - 1.0 * (p // 6 == 0)
    marks[:, 1] = 1.0 * (p % 6 == 5) - 1.0 * (p % 6 == 0)
    marks[:, 2] = np.abs(marks[:, 0])
    marks[:, 3] = np.abs(marks[:, 1])
    marks[:, 4] = order >= 36
    return tables, marks


def lookup_tables(elems, rows):
    spread = np.zeros((elems, elems // 2 * 32))
    marks = np.zeros((8, elems // 2 * 32), np.float32)
    lane = np.arange(elems // 2 * 32)
    r = lane % 32
    used = r < 24
    e = 2 * (lane // 32) + r % 24 // 12
    spread[e[used], lane[used]] = 1.0
    marks[0] = np.where(used, r % 6, 0)
    marks[1] = np.where(used, r // 6 % 2, 0)
    marks[3] = used
    rim_spread = np.zeros((rows, LANES))
    rim_lane = np.arange(6 * rows)
    rim_spread[rim_lane // 6, rim_lane] = 1.0
    marks[2, : 6 * rows] = rim_lane % 6
    return spread.astype(jnp.bfloat16), rim_spread.astype(jnp.bfloat16), marks


def split(x):
    high = x.astype(BF16)
    low = (x - high.astype(F32)).astype(BF16)
    return high, low


def dot3(a, b, dims):
    go = lambda x, y: lax.dot_general(x, y, (dims, ((), ())), preferred_element_type=F32)
    return go(a[0], b[0]) + (go(a[0], b[1]) + go(a[1], b[0]))


def pieces(src, dst, length):
    out = []
    done = 0
    while done < length:
        s, d = src + done, dst + done
        size = min(length - done, LANES - s % LANES, LANES - d % LANES)
        out.append((s // LANES, d // LANES, (d - s) % LANES, d % LANES, d % LANES + size))
        done += size
    return out


class Builder:
    def __init__(self, lane):
        self.lane = lane
        self.tiles = {}
        self.turned = {}

    def add(self, key, load, src, dst, length):
        for st, dt, shift, lo, hi in pieces(src, dst, length):
            name = (key, st, shift)
            if name not in self.turned:
                tile = load(st)
                self.turned[name] = pltpu.roll(tile, shift, 1) if shift else tile
            value = self.turned[name]
            if dt in self.tiles:
                value = jnp.where((self.lane >= lo) & (self.lane < hi), value, self.tiles[dt])
            self.tiles[dt] = value


INNER_ROWS = 12
OUTER_ROWS = 6


def kernel(groups, span, *refs):
    given, refs = refs[:13], refs[13:]
    out, refs = refs[0], refs[1:]
    held, refs = refs[:13], refs[13:]
    (
        index, flip, others, rim_send, rim_recv, send_a, send_b, send_c, recv_a, recv_b, recv_c,
        modal_c, fields, rows_r, inner_sum, outer_sum, inner_send, outer_send, inner_recv, outer_recv, change,
        load_sems, rim_sems, a_sems, b_sems, c_sems, inner_sems, outer_sems, hello,
    ) = refs
    (
        state, rim, rim_spread, lane_marks, neighbour, orient, wall, spread,
        metric, node_tab, node_marks, both_high, both_low,
    ) = held
    me = lax.axis_index("span")
    group = lax.axis_index("elem")
    lower = lax.rem(group + groups - 1, groups)
    upper = lax.rem(group + 1, groups)
    elems = metric.shape[1]
    modes = span * 8
    state_tiles = elems * NODES // LANES

    loads = [pltpu.make_async_copy(a, b, load_sems.at[i]) for i, (a, b) in enumerate(zip(given, held))]
    for load in loads[:4]:
        load.start()

    barrier = pltpu.get_barrier_semaphore()

    def greet(k, carry):
        pl.semaphore_signal(
            barrier, 1, device_id=(group, lax.rem(me + k, span)), device_id_type=MESH
        )
        return carry

    pl.semaphore_signal(barrier, 1, device_id=(lower, me), device_id_type=MESH)
    lax.fori_loop(1, span, greet, 0)
    for load in loads[4:]:
        load.start()

    lane = lax.broadcasted_iota(jnp.int32, (8, LANES), 1)
    row8 = lax.broadcasted_iota(jnp.int32, (8, LANES), 0)

    def bases(slot):
        side = slot & 3
        vertical = side >= 2
        step = jnp.where(vertical, 6, 1)
        first = jnp.where(vertical, jnp.where(side == 3, 5, 0), jnp.where(side == 1, 30, 0))
        return NODES * (slot >> 2) + first, step

    def spread_over(values, matrix):
        high = (values >> 6).astype(F32).astype(BF16)
        low = (values & 63).astype(F32).astype(BF16)
        go = lambda x: jnp.dot(x, matrix, preferred_element_type=F32)
        return (go(high) * 64.0 + go(low)).astype(jnp.int32)

    def picked(tile, at):
        return jnp.take_along_axis(tile, at, axis=1, mode="promise_in_bounds")

    def gather(at, start, tiles):
        low = at & (LANES - 1)
        high = at >> 7
        totals = list(start)
        for k in tiles:
            here = high == k
            for v in range(4):
                tile = (
                    state[v, :, k * LANES : (k + 1) * LANES]
                    if k < state_tiles
                    else rim_recv[k - state_tiles, v]
                )
                totals[v] = jnp.where(here, picked(tile, low), totals[v])
        return totals

    def fold(tile, start, width, store):
        every = LANES // width
        tile = picked(tile, start + (lane & (width - 1)))
        tile = jnp.where(lane // width == (row8 & (every - 1)), tile, 0.0)
        for a in range(8 // every):
            store(a, jnp.sum(tile[every * a : every * (a + 1)], axis=0, keepdims=True))

    def unfold(load, width):
        every = LANES // width
        tile = load(0)
        for a in range(1, 8 // every):
            tile = jnp.where(row8 < every * a, tile, load(a))
        return picked(jnp.broadcast_to(tile, (8, LANES)), (lane & (width - 1)) + width * (row8 & (every - 1)))

    def fold_96(tile, store):
        fold(tile, 0, 64, store)
        fold(tile, 64, 32, lambda a, row: store(4 + a, row))

    def unfold_96(load):
        return jnp.where(lane < 64, unfold(load, 64), unfold(lambda a: load(4 + a), 32))

    def rows_of(ref, top):
        def store(a, row):
            ref[top + a : top + a + 1, :] = row

        return store, lambda a: ref[top + a : top + a + 1, :]

    for load in loads[1:4]:
        load.wait()
    rim_base, rim_step = bases(rim[...])
    node_r = lane_marks[2:3, 0:LANES].astype(jnp.int32)
    rim_index = spread_over(rim_base, rim_spread[...]) + node_r * spread_over(
        rim_step, rim_spread[...]
    )
    loads[0].wait()
    zero = [jnp.zeros((8, LANES), F32)] * 4
    for way in range(2):
        at = jnp.broadcast_to(rim_index[way : way + 1], (8, LANES))
        got = gather(at, zero, range(state_tiles))
        for v in range(4):
            rim_send[way, v] = got[v]

    def rim_copy(way, to):
        return pltpu.make_async_remote_copy(
            rim_send.at[way], rim_recv.at[1 - way], rim_sems.at[way], rim_sems.at[3 - way],
            device_id=(to, me), device_id_type=MESH,
        )

    rim_up, rim_down = rim_copy(1, upper), rim_copy(0, lower)
    for d in range(span):
        b = Builder(lane)
        for v in range(4):
            b.add(v, lambda k, v=v: state[v, :, k * LANES : (k + 1) * LANES], PAIR * d, PAIR * v, PAIR)
        rows = slice(8 * d, 8 * d + 8)
        send_a[rows, 0:LANES] = b.tiles[0]
        send_a[rows, LANES:] = b.tiles[1]
        send_b[rows, :] = b.tiles[2]

    pl.semaphore_wait(barrier, span)
    pl.semaphore_signal(hello, 1, device_id=(upper, me), device_id_type=MESH)
    rim_up.start()

    def exchange(send, recv, rows, sems):
        arrived = sems.at[1]
        at = lambda who: pl.ds(pl.multiple_of(rows * who, 8) if rows == 8 else rows * who, rows)

        def one(k, carry):
            to = lax.rem(me + k, span)
            pltpu.make_async_remote_copy(
                send.at[at(to), :], recv.at[at(me), :], sems.at[0], arrived,
                device_id=(group, to), device_id_type=MESH,
            ).start()
            return carry

        lax.fori_loop(1, span, one, 0)
        pltpu.make_async_copy(send.at[at(me), :], recv.at[at(me), :], arrived).start()

    @pl.when(group > 0)
    def _():
        pl.semaphore_wait(hello, 1)
        rim_down.start()

    exchange(send_a, recv_a, 8, a_sems)

    for load in loads[4:8]:
        load.wait()
    slot = neighbour[...]
    turn = orient[...]
    remote = slot >= 4 * elems
    base, step = bases(slot)
    row = slot - 4 * elems
    base = jnp.where(remote, state_tiles * LANES + LANES * (row >> 4) + 6 * (row & 15), base)
    step = jnp.where(remote, 1, step)
    base = jnp.where(turn == 1, base + 5 * step, base)
    step = jnp.where(turn == 1, -step, step)
    matrix = spread[...]
    base_l = spread_over(base, matrix)
    step_l = spread_over(step + 8, matrix) - 8
    wall_l = spread_over(wall[...], matrix)
    node_l = lane_marks[0:1, :].astype(jnp.int32)
    second = lane_marks[1:2, :] > 0.5
    used = lane_marks[3:4, :] > 0.5
    for axis in range(2):
        pick = lambda x: jnp.where(second, x[2 * axis + 1 : 2 * axis + 2], x[2 * axis : 2 * axis + 1])
        lanes_at = jnp.where(used, pick(base_l) + pick(step_l) * node_l, 0)
        walls = 1.0 - 2.0 * pick(wall_l).astype(F32)
        for t in range(index.shape[1]):
            cut = slice(t * LANES, (t + 1) * LANES)
            index[axis, t] = jnp.broadcast_to(lanes_at[:, cut], (8, LANES))
            flip[axis, t] = jnp.broadcast_to(walls[:, cut], (8, LANES))

    def gather_axis(axis, tiles, first):
        def one(t, carry):
            at = index[axis, t]
            start = zero if first else [others[axis, v, t] for v in range(4)]
            got = gather(at, start, tiles)
            for v in range(4):
                others[axis, v, t] = got[v]
            return carry

        lax.fori_loop(0, index.shape[1], one, 0)

    def reflected(axis, v, t):
        tile = others[axis, v, t]
        return tile * flip[axis, t] if v < 3 else tile

    gather_axis(1, range(state_tiles), True)
    for d in range(span):
        b = Builder(lane)
        b.tiles[0] = send_b[8 * d : 8 * d + 8, :]
        for v in range(4):
            b.add(v, lambda k, v=v: reflected(1, v, k), 32 * d, 32 + 24 * v, 24)
        send_b[8 * d : 8 * d + 8, :] = b.tiles[0]
    exchange(send_b, recv_b, 8, b_sems)
    gather_axis(0, range(state_tiles), True)

    @pl.when(group == 0)
    def _():
        pl.semaphore_wait(hello, 1)
        rim_down.start()

    rim_up.wait()
    rim_down.wait()
    gather_axis(0, range(state_tiles, state_tiles + 2), False)

    for d in range(span):
        b = Builder(lane)
        for v in range(4):
            b.add(v, lambda k, v=v: reflected(0, v, k), 32 * d, 24 * v, 24)
        fold_96(b.tiles[0], rows_of(send_c, OUTER_ROWS * d)[0])
    exchange(send_c, recv_c, OUTER_ROWS, c_sems)

    for load in loads[8:]:
        load.wait()
    at = lax.broadcasted_iota(jnp.int32, (2, elems), 1)
    scale = metric[...]
    first = jnp.sum(jnp.where(at == 2 * me, scale, 0.0), axis=1, keepdims=True)
    last = jnp.sum(jnp.where(at == 2 * me + 1, scale, 0.0), axis=1, keepdims=True)

    def per_row(on_first, which):
        return jnp.where(on_first, first[which : which + 1], last[which : which + 1])

    marks = node_marks[...]
    on_first = marks[:, 4:5] < 0.5
    rx, ry = per_row(on_first, 0), per_row(on_first, 1)
    coef_u = 7.5 * rx * marks[:, 0:1]
    coef_v = 7.5 * ry * marks[:, 1:2]
    coef_c = 7.5 * (jnp.abs(rx) * marks[:, 2:3] + jnp.abs(ry) * marks[:, 3:4])
    operator = split(rx * node_tab[0] + ry * node_tab[1] + node_tab[2])
    side = lax.broadcasted_iota(jnp.int32, (24, 1), 0)
    low_side = (side < 6) | ((side >= 12) & (side < 18))
    toward = jnp.where(low_side, 7.5, -7.5)
    ox, oy = per_row(side < 12, 0), per_row(side < 12, 1)

    over0, over1 = ((0,), (0,)), ((1,), (1,))
    basis = (both_high[:, 0:modes], both_low[:, 0:modes])
    pltpu.make_async_copy(recv_a, recv_a, a_sems.at[1]).wait()
    planes_a = dot3(split(recv_a[...]), basis, over0)
    pltpu.make_async_copy(recv_b, recv_b, b_sems.at[1]).wait()
    planes_b = dot3(split(recv_b[...]), basis, over0)
    own = [planes_a[PAIR * v : PAIR * (v + 1)] for v in range(3)]
    own.append(jnp.concatenate([planes_a[3 * PAIR :], planes_b[0:32]], axis=0))
    own = [jnp.concatenate([x[a:b] for a, b in INNER + OUTER], axis=0) for x in own]
    facing_y = [planes_b[32 + 24 * v : 56 + 24 * v] for v in range(4)]
    own_coef = coef_u * own[0] + coef_v * own[1] - coef_c
    facing_y_coef = (toward * oy) * facing_y[1] + 7.5 * jnp.abs(oy)
    for v in range(4):
        fields[v, 0:72] = own[0] * own[v]
        fields[v, 72:144] = own[1] * own[v]
        fields[v, 144:168] = facing_y_coef * facing_y[v]
        along_z = own[2] * own[v]
        planar = own_coef * own[v] + dot3(operator, split(fields[v]), ((1,), (0,)))
        for part, at in ((planar, slice(0, modes)), (along_z, slice(modes, 2 * modes))):
            rows_r[48 * v : 48 * v + 48, at] = part[0:48]
            rows_r[192 + 24 * v : 216 + 24 * v, at] = part[48:72]
    both = (both_high[...], both_low[...])

    inner_sum[:, 0:192] = dot3(both, split(rows_r[0:192, :]), over1)
    for d in range(span):
        mine = inner_sum[8 * d : 8 * d + 8, :]
        top = INNER_ROWS * d
        inner_send[top : top + 8, :] = mine[:, 0:LANES]
        fold(mine[:, LANES:], 0, 64, rows_of(inner_send, top + 8)[0])
    exchange(inner_send, inner_recv, INNER_ROWS, inner_sems)
    outer_sum[:, 0:96] = dot3(both, split(rows_r[192:288, :]), over1)

    pltpu.make_async_copy(recv_c, recv_c, c_sems.at[1]).wait()
    for s in range(span):
        modal_c[8 * s : 8 * s + 8, :] = unfold_96(rows_of(recv_c, OUTER_ROWS * s)[1])
    planes_c = dot3(split(modal_c[:, 0:96]), basis, over0)
    facing_x_coef = (toward * ox) * planes_c[0:24] + 7.5 * jnp.abs(ox)
    jump = split(jnp.concatenate([facing_x_coef] * 4, axis=0) * planes_c)
    outer_sum[:, 0:96] += dot3(basis, jump, over1)
    for d in range(span):
        fold_96(outer_sum[8 * d : 8 * d + 8, :], rows_of(outer_send, OUTER_ROWS * d)[0])
    exchange(outer_send, outer_recv, OUTER_ROWS, outer_sems)

    mode = 8 * me + row8
    k = jnp.where(mode == 1, modes // 2, mode >> 1).astype(F32)
    shrink = 1.0 / (1.0 + TIME_STEP * VISCOSITY * k * k)

    pltpu.make_async_copy(inner_recv, inner_recv, inner_sems.at[1]).wait()
    builders = [Builder(lane) for _ in range(4)]
    for s in range(span):
        top = INNER_ROWS * s

        def inner(t, top=top):
            if t == 0:
                return inner_recv[top : top + 8, :]
            return unfold(rows_of(inner_recv, top + 8)[1], 64)

        tiles = [inner(0), inner(1)]
        for v in range(4):
            for e, (a, b) in enumerate(INNER):
                builders[v].add((s, e), lambda t, x=tiles: x[t], 48 * v + 24 * e, PAIR * s + a, 24)
    for v in range(4):
        for t in range(state_tiles):
            cut = slice(t * LANES, (t + 1) * LANES)
            change[v, :, cut] = builders[v].tiles[t]

    pltpu.make_async_copy(outer_recv, outer_recv, outer_sems.at[1]).wait()
    builders = [Builder(lane) for _ in range(4)]
    for v in range(4):
        for t in range(state_tiles):
            builders[v].tiles[t] = change[v, :, t * LANES : (t + 1) * LANES]
    for s in range(span):
        tile = unfold_96(rows_of(outer_recv, OUTER_ROWS * s)[1])
        for v in range(4):
            for src, dst, length in ((0, 0, 6), (6, 30, 12), (18, 66, 6)):
                builders[v].add((s, src), lambda t, x=tile: x, 24 * v + src, PAIR * s + dst, length)
    for v in range(4):
        for t in range(state_tiles):
            cut = slice(t * LANES, (t + 1) * LANES)
            out[v, :, cut] = (state[v, :, cut] + TIME_STEP * builders[v].tiles[t]) * shrink

    for send, rows, sems in (
        (send_a, 8, a_sems), (send_b, 8, b_sems), (send_c, OUTER_ROWS, c_sems),
        (inner_send, INNER_ROWS, inner_sems), (outer_send, OUTER_ROWS, outer_sems),
    ):
        sent = send.at[0 : rows * (span - 1), :]
        pltpu.make_async_copy(sent, sent, sems.at[0]).wait()


def body(groups, span, state, metric, neighbour, orient, wall, rim):
    elems = metric.shape[1]
    modes = span * 8
    tables, marks = node_tables()
    spread, rim_spread, lane_marks = lookup_tables(elems, rim.shape[1])
    both_high, both_low = basis_tables(modes)
    given = [
        state, rim, rim_spread, lane_marks, neighbour.T, orient.T, wall.T, spread,
        metric, tables, marks, both_high, both_low,
    ]
    given = [jnp.asarray(x) for x in given]
    gathered = elems // 2 * 32 // LANES
    scratch = [pltpu.VMEM(x.shape, x.dtype) for x in given] + [
        pltpu.VMEM((2, gathered, 8, LANES), jnp.int32),
        pltpu.VMEM((2, gathered, 8, LANES), F32),
        pltpu.VMEM((2, 4, gathered, 8, LANES), F32),
        pltpu.VMEM((2, 4, 8, LANES), F32),
        pltpu.VMEM((2, 4, 8, LANES), F32),
        pltpu.VMEM((modes, 256), F32),
        pltpu.VMEM((modes, LANES), F32),
        pltpu.VMEM((OUTER_ROWS * span, LANES), F32),
        pltpu.VMEM((modes, 256), F32),
        pltpu.VMEM((modes, LANES), F32),
        pltpu.VMEM((OUTER_ROWS * span, LANES), F32),
        pltpu.VMEM((modes, LANES), F32),
        pltpu.VMEM((4, 168, modes), F32),
        pltpu.VMEM((288, 2 * modes), F32),
        pltpu.VMEM((modes, 256), F32),
        pltpu.VMEM((modes, LANES), F32),
        pltpu.VMEM((INNER_ROWS * span, LANES), F32),
        pltpu.VMEM((OUTER_ROWS * span, LANES), F32),
        pltpu.VMEM((INNER_ROWS * span, LANES), F32),
        pltpu.VMEM((OUTER_ROWS * span, LANES), F32),
        pltpu.VMEM(state.shape, F32),
        pltpu.SemaphoreType.DMA((len(given),)),
        pltpu.SemaphoreType.DMA((4,)),
        pltpu.SemaphoreType.DMA((2,)),
        pltpu.SemaphoreType.DMA((2,)),
        pltpu.SemaphoreType.DMA((2,)),
        pltpu.SemaphoreType.DMA((2,)),
        pltpu.SemaphoreType.DMA((2,)),
        pltpu.SemaphoreType.REGULAR,
    ]
    return pl.pallas_call(
        functools.partial(kernel, groups, span),
        out_shape=jax.ShapeDtypeStruct(state.shape, F32),
        in_specs=[pl.BlockSpec(memory_space=pltpu.HBM)] * len(given),
        out_specs=pl.BlockSpec(memory_space=pltpu.VMEM),
        scratch_shapes=scratch,
        compiler_params=pltpu.CompilerParams(
            collective_id=0, has_side_effects=True, vmem_limit_bytes=60 << 20
        ),
        name="section",
    )(*given)


def solution(mesh):
    specs = (
        P(None, "span", "elem"), P(None, "elem"), P("elem", None),
        P("elem", None), P("elem", None), P(None, "elem"),
    )
    return jax.shard_map(
        functools.partial(body, mesh.shape["elem"], mesh.shape["span"]),
        mesh=mesh, in_specs=specs, out_specs=P(None, "span", "elem"), check_vma=False,
    )
```

```python
import functools
import math

import jax
import jax.numpy as jnp
import numpy as np
from jax import lax
from jax.experimental import pallas as pl
from jax.experimental.pallas import tpu as pltpu
from jax.sharding import PartitionSpec as P

TIME_STEP = 0.001
VISCOSITY = 0.02
MESH = pl.DeviceIdType.MESH
F32 = jnp.float32
BF16 = jnp.bfloat16
NODES = 36
PAIR = 72
LANES = 128
INNER = ((6, 30), (42, 66))
OUTER = ((0, 6), (30, 36), (36, 42), (66, 72))


def differentiation():
    near = math.sqrt(1.0 / 3.0 - 2.0 * math.sqrt(7.0) / 21.0)
    far = math.sqrt(1.0 / 3.0 + 2.0 * math.sqrt(7.0) / 21.0)
    points = np.array([-1.0, -far, -near, near, far, 1.0])
    weights = np.array(
        [1.0 / np.prod([points[c] - points[s] for s in range(6) if s != c]) for c in range(6)]
    )
    deriv = np.zeros((6, 6))
    for t in range(6):
        for s in range(6):
            if s != t:
                deriv[t, s] = weights[s] / weights[t] / (points[t] - points[s])
        deriv[t, t] = -np.sum(deriv[t])
    return deriv


def split_np(x):
    high = x.astype(jnp.bfloat16)
    low = (x - high.astype(np.float64)).astype(jnp.bfloat16)
    return high, low


def basis_tables(count):
    m = np.arange(count)[:, None]
    n = np.arange(count)[None, :]
    angle = (m // 2 * n % count) * (2.0 * math.pi / count)
    basis = np.where(m % 2 == 1, np.sin(angle), np.cos(angle)) * math.sqrt(2.0 / count)
    basis[0] = 1.0 / math.sqrt(count)
    basis[1] = (1.0 - 2.0 * (np.arange(count) % 2)) / math.sqrt(count)
    minus = np.zeros_like(basis)
    k = np.arange(count // 2)[:, None]
    minus[0::2] = -k * basis[1::2]
    minus[1::2] = k * basis[0::2]
    both = np.concatenate([basis, minus], axis=1)
    return split_np(both)


def node_tables():
    deriv = differentiation()
    ident = np.eye(6)
    two = np.eye(2)
    along_x = np.zeros((PAIR, 168))
    along_y = np.zeros((PAIR, 168))
    lift = np.zeros((PAIR, 168))
    order = np.concatenate([np.arange(a, b) for a, b in INNER + OUTER])
    along_x[:, 0:72] = -np.kron(two, np.kron(deriv, ident))[order][:, order]
    along_y[:, 72:144] = -np.kron(two, np.kron(ident, deriv))[order][:, order]
    for e in range(2):
        for s2 in range(2):
            for j in range(6):
                lift[e * 36 + 6 * j + 5 * s2, 144 + e * 12 + s2 * 6 + j] = 1.0
    lift = lift[order]
    tables = np.stack([along_x, along_y, lift]).astype(np.float32)
    marks = np.zeros((PAIR, 8), np.float32)
    p = order % 36
    marks[:, 0] = 1.0 * (p // 6 == 5) - 1.0 * (p // 6 == 0)
    marks[:, 1] = 1.0 * (p % 6 == 5) - 1.0 * (p % 6 == 0)
    marks[:, 2] = np.abs(marks[:, 0])
    marks[:, 3] = np.abs(marks[:, 1])
    marks[:, 4] = order >= 36
    return tables, marks


def lookup_tables(elems, rows):
    spread = np.zeros((elems, elems // 2 * 32))
    marks = np.zeros((8, elems // 2 * 32), np.float32)
    lane = np.arange(elems // 2 * 32)
    r = lane % 32
    used = r < 24
    e = 2 * (lane // 32) + r % 24 // 12
    spread[e[used], lane[used]] = 1.0
    marks[0] = np.where(used, r % 6, 0)
    marks[1] = np.where(used, r // 6 % 2, 0)
    marks[3] = used
    rim_spread = np.zeros((rows, LANES))
    rim_lane = np.arange(6 * rows)
    rim_spread[rim_lane // 6, rim_lane] = 1.0
    marks[2, : 6 * rows] = rim_lane % 6
    return spread.astype(jnp.bfloat16), rim_spread.astype(jnp.bfloat16), marks


def split(x):
    high = x.astype(BF16)
    low = (x - high.astype(F32)).astype(BF16)
    return high, low


def dot3(a, b, dims):
    go = lambda x, y: lax.dot_general(x, y, (dims, ((), ())), preferred_element_type=F32)
    return go(a[0], b[0]) + (go(a[0], b[1]) + go(a[1], b[0]))


def pieces(src, dst, length):
    out = []
    done = 0
    while done < length:
        s, d = src + done, dst + done
        size = min(length - done, LANES - s % LANES, LANES - d % LANES)
        out.append((s // LANES, d // LANES, (d - s) % LANES, d % LANES, d % LANES + size))
        done += size
    return out


class Builder:
    def __init__(self, lane):
        self.lane = lane
        self.tiles = {}
        self.turned = {}

    def add(self, key, load, src, dst, length):
        for st, dt, shift, lo, hi in pieces(src, dst, length):
            name = (key, st, shift)
            if name not in self.turned:
                tile = load(st)
                self.turned[name] = pltpu.roll(tile, shift, 1) if shift else tile
            value = self.turned[name]
            if dt in self.tiles:
                value = jnp.where((self.lane >= lo) & (self.lane < hi), value, self.tiles[dt])
            self.tiles[dt] = value


def picked(tile, at):
    return jnp.take_along_axis(tile, at, axis=1, mode="promise_in_bounds")


def tile_indices():
    return tuple(lax.broadcasted_iota(jnp.int32, (8, LANES), dim) for dim in range(2))


def fold(tile, start, width, store):
    row8, lane = tile_indices()
    every = LANES // width
    tile = picked(tile, start + (lane & (width - 1)))
    tile = jnp.where(lane // width == (row8 & (every - 1)), tile, 0.0)
    for a in range(8 // every):
        store(a, jnp.sum(tile[every * a : every * (a + 1)], axis=0, keepdims=True))


def unfold(load, width):
    row8, lane = tile_indices()
    every = LANES // width
    tile = load(0)
    for a in range(1, 8 // every):
        tile = jnp.where(row8 < every * a, tile, load(a))
    return picked(jnp.broadcast_to(tile, (8, LANES)), (lane & (width - 1)) + width * (row8 & (every - 1)))


def fold_96(tile, store):
    fold(tile, 0, 64, store)
    fold(tile, 64, 32, lambda a, row: store(4 + a, row))


def unfold_96(load):
    lane = tile_indices()[1]
    return jnp.where(lane < 64, unfold(load, 64), unfold(lambda a: load(4 + a), 32))


def rows_of(ref, top):
    def store(a, row):
        ref[top + a : top + a + 1, :] = row

    return store, lambda a: ref[top + a : top + a + 1, :]


INNER_ROWS = 12
OUTER_ROWS = 6


def kernel(groups, span, *refs):
    given, refs = refs[:13], refs[13:]
    (result, outer_recv), refs = refs[:2], refs[2:]
    held, refs = refs[:13], refs[13:]
    (
        index, flip, others, rim_send, rim_recv, send_a, send_b, send_c, recv_a, recv_b, recv_c,
        modal_c, fields, rows_r, inner_sum, outer_sum, inner_send, outer_send, inner_recv, settled,
        load_sems, rim_sems, a_sems, b_sems, c_sems, inner_sems, outer_sems, result_sem, hello,
    ) = refs
    (
        state, rim, rim_spread, lane_marks, neighbour, orient, wall, spread,
        metric, node_tab, node_marks, both_high, both_low,
    ) = held
    me = lax.axis_index("span")
    group = lax.axis_index("elem")
    lower = lax.rem(group + groups - 1, groups)
    upper = lax.rem(group + 1, groups)
    elems = metric.shape[1]
    modes = span * 8
    state_tiles = elems * NODES // LANES

    loads = [pltpu.make_async_copy(a, b, load_sems.at[i]) for i, (a, b) in enumerate(zip(given, held))]
    for load in loads[:4]:
        load.start()

    barrier = pltpu.get_barrier_semaphore()

    def greet(k, carry):
        pl.semaphore_signal(
            barrier, 1, device_id=(group, lax.rem(me + k, span)), device_id_type=MESH
        )
        return carry

    pl.semaphore_signal(barrier, 1, device_id=(lower, me), device_id_type=MESH)
    lax.fori_loop(1, span, greet, 0)
    for load in loads[4:]:
        load.start()

    lane = lax.broadcasted_iota(jnp.int32, (8, LANES), 1)
    row8 = lax.broadcasted_iota(jnp.int32, (8, LANES), 0)

    def bases(slot):
        side = slot & 3
        vertical = side >= 2
        step = jnp.where(vertical, 6, 1)
        first = jnp.where(vertical, jnp.where(side == 3, 5, 0), jnp.where(side == 1, 30, 0))
        return NODES * (slot >> 2) + first, step

    def spread_over(values, matrix):
        high = (values >> 6).astype(F32).astype(BF16)
        low = (values & 63).astype(F32).astype(BF16)
        go = lambda x: jnp.dot(x, matrix, preferred_element_type=F32)
        return (go(high) * 64.0 + go(low)).astype(jnp.int32)

    def gather(at, start, tiles):
        low = at & (LANES - 1)
        high = at >> 7
        totals = list(start)
        for k in tiles:
            here = high == k
            for v in range(4):
                tile = (
                    state[v, :, k * LANES : (k + 1) * LANES]
                    if k < state_tiles
                    else rim_recv[k - state_tiles, v]
                )
                totals[v] = jnp.where(here, picked(tile, low), totals[v])
        return totals

    for load in loads[1:4]:
        load.wait()
    rim_base, rim_step = bases(rim[...])
    node_r = lane_marks[2:3, 0:LANES].astype(jnp.int32)
    rim_index = spread_over(rim_base, rim_spread[...]) + node_r * spread_over(
        rim_step, rim_spread[...]
    )
    loads[0].wait()
    zero = [jnp.zeros((8, LANES), F32)] * 4
    for way in range(2):
        at = jnp.broadcast_to(rim_index[way : way + 1], (8, LANES))
        got = gather(at, zero, range(state_tiles))
        for v in range(4):
            rim_send[way, v] = got[v]

    def rim_copy(way, to):
        return pltpu.make_async_remote_copy(
            rim_send.at[way], rim_recv.at[1 - way], rim_sems.at[way], rim_sems.at[3 - way],
            device_id=(to, me), device_id_type=MESH,
        )

    rim_up, rim_down = rim_copy(1, upper), rim_copy(0, lower)
    for d in range(span):
        b = Builder(lane)
        for v in range(4):
            b.add(v, lambda k, v=v: state[v, :, k * LANES : (k + 1) * LANES], PAIR * d, PAIR * v, PAIR)
        rows = slice(8 * d, 8 * d + 8)
        send_a[rows, 0:LANES] = b.tiles[0]
        send_a[rows, LANES:] = b.tiles[1]
        send_b[rows, :] = b.tiles[2]

    pl.semaphore_wait(barrier, span)
    pl.semaphore_signal(hello, 1, device_id=(upper, me), device_id_type=MESH)
    rim_up.start()

    def exchange(send, recv, rows, sems):
        arrived = sems.at[1]
        at = lambda who: pl.ds(pl.multiple_of(rows * who, 8) if rows == 8 else rows * who, rows)

        def one(k, carry):
            to = lax.rem(me + k, span)
            pltpu.make_async_remote_copy(
                send.at[at(to), :], recv.at[at(me), :], sems.at[0], arrived,
                device_id=(group, to), device_id_type=MESH,
            ).start()
            return carry

        lax.fori_loop(1, span, one, 0)
        pltpu.make_async_copy(send.at[at(me), :], recv.at[at(me), :], arrived).start()

    @pl.when(group > 0)
    def _():
        pl.semaphore_wait(hello, 1)
        rim_down.start()

    exchange(send_a, recv_a, 8, a_sems)

    for load in loads[4:8]:
        load.wait()
    slot = neighbour[...]
    turn = orient[...]
    remote = slot >= 4 * elems
    base, step = bases(slot)
    row = slot - 4 * elems
    base = jnp.where(remote, state_tiles * LANES + LANES * (row >> 4) + 6 * (row & 15), base)
    step = jnp.where(remote, 1, step)
    base = jnp.where(turn == 1, base + 5 * step, base)
    step = jnp.where(turn == 1, -step, step)
    matrix = spread[...]
    base_l = spread_over(base, matrix)
    step_l = spread_over(step + 8, matrix) - 8
    wall_l = spread_over(wall[...], matrix)
    node_l = lane_marks[0:1, :].astype(jnp.int32)
    second = lane_marks[1:2, :] > 0.5
    used = lane_marks[3:4, :] > 0.5
    for axis in range(2):
        pick = lambda x: jnp.where(second, x[2 * axis + 1 : 2 * axis + 2], x[2 * axis : 2 * axis + 1])
        lanes_at = jnp.where(used, pick(base_l) + pick(step_l) * node_l, 0)
        walls = 1.0 - 2.0 * pick(wall_l).astype(F32)
        for t in range(index.shape[1]):
            cut = slice(t * LANES, (t + 1) * LANES)
            index[axis, t] = jnp.broadcast_to(lanes_at[:, cut], (8, LANES))
            flip[axis, t] = jnp.broadcast_to(walls[:, cut], (8, LANES))

    def gather_axis(axis, tiles, first):
        def one(t, carry):
            at = index[axis, t]
            start = zero if first else [others[axis, v, t] for v in range(4)]
            got = gather(at, start, tiles)
            for v in range(4):
                others[axis, v, t] = got[v]
            return carry

        lax.fori_loop(0, index.shape[1], one, 0)

    def reflected(axis, v, t):
        tile = others[axis, v, t]
        return tile * flip[axis, t] if v < 3 else tile

    gather_axis(1, range(state_tiles), True)
    for d in range(span):
        b = Builder(lane)
        b.tiles[0] = send_b[8 * d : 8 * d + 8, :]
        for v in range(4):
            b.add(v, lambda k, v=v: reflected(1, v, k), 32 * d, 32 + 24 * v, 24)
        send_b[8 * d : 8 * d + 8, :] = b.tiles[0]
    exchange(send_b, recv_b, 8, b_sems)
    gather_axis(0, range(state_tiles), True)

    @pl.when(group == 0)
    def _():
        pl.semaphore_wait(hello, 1)
        rim_down.start()

    rim_up.wait()
    rim_down.wait()
    gather_axis(0, range(state_tiles, state_tiles + 2), False)

    for d in range(span):
        b = Builder(lane)
        for v in range(4):
            b.add(v, lambda k, v=v: reflected(0, v, k), 32 * d, 24 * v, 24)
        fold_96(b.tiles[0], rows_of(send_c, OUTER_ROWS * d)[0])
    exchange(send_c, recv_c, OUTER_ROWS, c_sems)

    for load in loads[8:]:
        load.wait()
    at = lax.broadcasted_iota(jnp.int32, (2, elems), 1)
    scale = metric[...]
    first = jnp.sum(jnp.where(at == 2 * me, scale, 0.0), axis=1, keepdims=True)
    last = jnp.sum(jnp.where(at == 2 * me + 1, scale, 0.0), axis=1, keepdims=True)

    def per_row(on_first, which):
        return jnp.where(on_first, first[which : which + 1], last[which : which + 1])

    marks = node_marks[...]
    on_first = marks[:, 4:5] < 0.5
    rx, ry = per_row(on_first, 0), per_row(on_first, 1)
    coef_u = 7.5 * rx * marks[:, 0:1]
    coef_v = 7.5 * ry * marks[:, 1:2]
    coef_c = 7.5 * (jnp.abs(rx) * marks[:, 2:3] + jnp.abs(ry) * marks[:, 3:4])
    operator = split(rx * node_tab[0] + ry * node_tab[1] + node_tab[2])
    side = lax.broadcasted_iota(jnp.int32, (24, 1), 0)
    low_side = (side < 6) | ((side >= 12) & (side < 18))
    toward = jnp.where(low_side, 7.5, -7.5)
    ox, oy = per_row(side < 12, 0), per_row(side < 12, 1)

    over0, over1 = ((0,), (0,)), ((1,), (1,))
    basis = (both_high[:, 0:modes], both_low[:, 0:modes])
    pltpu.make_async_copy(recv_a, recv_a, a_sems.at[1]).wait()
    planes_a = dot3(split(recv_a[...]), basis, over0)
    pltpu.make_async_copy(recv_b, recv_b, b_sems.at[1]).wait()
    planes_b = dot3(split(recv_b[...]), basis, over0)
    own = [planes_a[PAIR * v : PAIR * (v + 1)] for v in range(3)]
    own.append(jnp.concatenate([planes_a[3 * PAIR :], planes_b[0:32]], axis=0))
    own = [jnp.concatenate([x[a:b] for a, b in INNER + OUTER], axis=0) for x in own]
    facing_y = [planes_b[32 + 24 * v : 56 + 24 * v] for v in range(4)]
    own_coef = coef_u * own[0] + coef_v * own[1] - coef_c
    facing_y_coef = (toward * oy) * facing_y[1] + 7.5 * jnp.abs(oy)
    for v in range(4):
        fields[v, 0:72] = own[0] * own[v]
        fields[v, 72:144] = own[1] * own[v]
        fields[v, 144:168] = facing_y_coef * facing_y[v]
        along_z = own[2] * own[v]
        planar = own_coef * own[v] + dot3(operator, split(fields[v]), ((1,), (0,)))
        for part, at in ((planar, slice(0, modes)), (along_z, slice(modes, 2 * modes))):
            rows_r[48 * v : 48 * v + 48, at] = part[0:48]
            rows_r[192 + 24 * v : 216 + 24 * v, at] = part[48:72]
    both = (both_high[...], both_low[...])

    def damped(mode):
        k = jnp.where(mode == 1, modes // 2, mode >> 1).astype(F32)
        return 1.0 / (1.0 + TIME_STEP * VISCOSITY * k * k)

    step_of = TIME_STEP * damped(lax.broadcasted_iota(jnp.int32, (modes, 1), 0))

    inner_sum[:, 0:192] = step_of * dot3(both, split(rows_r[0:192, :]), over1)
    for d in range(span):
        mine = inner_sum[8 * d : 8 * d + 8, :]
        top = INNER_ROWS * d
        inner_send[top : top + 8, :] = mine[:, 0:LANES]
        fold(mine[:, LANES:], 0, 64, rows_of(inner_send, top + 8)[0])
    exchange(inner_send, inner_recv, INNER_ROWS, inner_sems)
    outer_sum[:, 0:96] = dot3(both, split(rows_r[192:288, :]), over1)

    pltpu.make_async_copy(recv_c, recv_c, c_sems.at[1]).wait()
    for s in range(span):
        modal_c[8 * s : 8 * s + 8, :] = unfold_96(rows_of(recv_c, OUTER_ROWS * s)[1])
    planes_c = dot3(split(modal_c[:, 0:96]), basis, over0)
    facing_x_coef = (toward * ox) * planes_c[0:24] + 7.5 * jnp.abs(ox)
    jump = split(jnp.concatenate([facing_x_coef] * 4, axis=0) * planes_c)
    outer_sum[:, 0:96] = step_of * (outer_sum[:, 0:96] + dot3(basis, jump, over1))
    for d in range(span):
        fold_96(outer_sum[8 * d : 8 * d + 8, :], rows_of(outer_send, OUTER_ROWS * d)[0])
    exchange(outer_send, outer_recv, OUTER_ROWS, outer_sems)

    shrink = damped(8 * me + row8)
    pltpu.make_async_copy(inner_recv, inner_recv, inner_sems.at[1]).wait()
    nothing = jnp.zeros((8, LANES), F32)
    builders = [Builder(lane) for _ in range(4)]
    for v in range(4):
        builders[v].tiles = {t: nothing for t in range(state_tiles)}
    for s in range(span):
        top = INNER_ROWS * s

        def inner(t, top=top):
            if t == 0:
                return inner_recv[top : top + 8, :]
            return unfold(rows_of(inner_recv, top + 8)[1], 64)

        tiles = [inner(0), inner(1)]
        for v in range(4):
            for e, (a, b) in enumerate(INNER):
                builders[v].add((s, e), lambda t, x=tiles: x[t], 48 * v + 24 * e, PAIR * s + a, 24)
    for v in range(4):
        for t in range(state_tiles):
            cut = slice(t * LANES, (t + 1) * LANES)
            settled[v, :, cut] = state[v, :, cut] * shrink + builders[v].tiles[t]
    put = pltpu.make_async_copy(settled, result, result_sem)
    put.start()
    pltpu.make_async_copy(outer_recv, outer_recv, outer_sems.at[1]).wait()
    put.wait()

    for send, rows, sems in (
        (send_a, 8, a_sems), (send_b, 8, b_sems), (send_c, OUTER_ROWS, c_sems),
        (inner_send, INNER_ROWS, inner_sems), (outer_send, OUTER_ROWS, outer_sems),
    ):
        sent = send.at[0 : rows * (span - 1), :]
        pltpu.make_async_copy(sent, sent, sems.at[0]).wait()


def finish(span, base, outer, out, base_v, outer_v, out_v, load_sems, store_sems):
    loads = [
        pltpu.make_async_copy(a, b, load_sems.at[i])
        for i, (a, b) in enumerate(((outer, outer_v), (base, base_v)))
    ]
    for load in loads:
        load.start()
    loads[0].wait()
    lane = tile_indices()[1]
    tiles = [unfold_96(rows_of(outer_v, OUTER_ROWS * s)[1]) for s in range(span)]
    loads[1].wait()
    stores = []
    for v in range(4):
        b = Builder(lane)
        for t in range(base.shape[2] // LANES):
            b.tiles[t] = jnp.zeros((8, LANES), F32)
        for s in range(span):
            for src, dst, length in ((0, 0, 6), (6, 30, 12), (18, 66, 6)):
                b.add((s, src), lambda t, x=tiles[s]: x, 24 * v + src, PAIR * s + dst, length)
        for t in range(base.shape[2] // LANES):
            cut = slice(t * LANES, (t + 1) * LANES)
            out_v[v, :, cut] = base_v[v, :, cut] + b.tiles[t]
        store = pltpu.make_async_copy(out_v.at[v], out.at[v], store_sems.at[v])
        store.start()
        stores.append(store)
    for store in stores:
        store.wait()


def body(groups, span, state, metric, neighbour, orient, wall, rim):
    elems = metric.shape[1]
    modes = span * 8
    tables, marks = node_tables()
    spread, rim_spread, lane_marks = lookup_tables(elems, rim.shape[1])
    both_high, both_low = basis_tables(modes)
    given = [
        state, rim, rim_spread, lane_marks, neighbour.T, orient.T, wall.T, spread,
        metric, tables, marks, both_high, both_low,
    ]
    given = [jnp.asarray(x) for x in given]
    gathered = elems // 2 * 32 // LANES
    scratch = [pltpu.VMEM(x.shape, x.dtype) for x in given] + [
        pltpu.VMEM((2, gathered, 8, LANES), jnp.int32),
        pltpu.VMEM((2, gathered, 8, LANES), F32),
        pltpu.VMEM((2, 4, gathered, 8, LANES), F32),
        pltpu.VMEM((2, 4, 8, LANES), F32),
        pltpu.VMEM((2, 4, 8, LANES), F32),
        pltpu.VMEM((modes, 256), F32),
        pltpu.VMEM((modes, LANES), F32),
        pltpu.VMEM((OUTER_ROWS * span, LANES), F32),
        pltpu.VMEM((modes, 256), F32),
        pltpu.VMEM((modes, LANES), F32),
        pltpu.VMEM((OUTER_ROWS * span, LANES), F32),
        pltpu.VMEM((modes, LANES), F32),
        pltpu.VMEM((4, 168, modes), F32),
        pltpu.VMEM((288, 2 * modes), F32),
        pltpu.VMEM((modes, 256), F32),
        pltpu.VMEM((modes, LANES), F32),
        pltpu.VMEM((INNER_ROWS * span, LANES), F32),
        pltpu.VMEM((OUTER_ROWS * span, LANES), F32),
        pltpu.VMEM((INNER_ROWS * span, LANES), F32),
        pltpu.VMEM(state.shape, F32),
        pltpu.SemaphoreType.DMA((len(given),)),
        pltpu.SemaphoreType.DMA((4,)),
        pltpu.SemaphoreType.DMA((2,)),
        pltpu.SemaphoreType.DMA((2,)),
        pltpu.SemaphoreType.DMA((2,)),
        pltpu.SemaphoreType.DMA((2,)),
        pltpu.SemaphoreType.DMA((2,)),
        pltpu.SemaphoreType.DMA,
        pltpu.SemaphoreType.REGULAR,
    ]
    hbm = pl.BlockSpec(memory_space=pltpu.HBM)
    outer = jax.ShapeDtypeStruct((OUTER_ROWS * span, LANES), F32)
    whole = jax.ShapeDtypeStruct(state.shape, F32)
    base, outer_rows = pl.pallas_call(
        functools.partial(kernel, groups, span),
        out_shape=(whole, outer),
        in_specs=[hbm] * len(given),
        out_specs=(hbm, hbm),
        scratch_shapes=scratch,
        compiler_params=pltpu.CompilerParams(
            collective_id=0, has_side_effects=True, vmem_limit_bytes=60 << 20
        ),
        name="section",
    )(*given)
    return pl.pallas_call(
        functools.partial(finish, span),
        out_shape=whole,
        in_specs=[hbm, hbm],
        out_specs=hbm,
        scratch_shapes=[
            pltpu.VMEM(whole.shape, F32), pltpu.VMEM(outer.shape, F32), pltpu.VMEM(whole.shape, F32),
            pltpu.SemaphoreType.DMA((2,)), pltpu.SemaphoreType.DMA((4,)),
        ],
        compiler_params=pltpu.CompilerParams(vmem_limit_bytes=60 << 20),
        name="finish",
    )(base, outer_rows)


def solution(mesh):
    specs = (
        P(None, "span", "elem"), P(None, "elem"), P("elem", None),
        P("elem", None), P("elem", None), P(None, "elem"),
    )
    return jax.shard_map(
        functools.partial(body, mesh.shape["elem"], mesh.shape["span"]),
        mesh=mesh, in_specs=specs, out_specs=P(None, "span", "elem"), check_vma=False,
    )
```

```python
import functools
import math

import jax
import jax.numpy as jnp
import numpy as np
from jax import lax
from jax.experimental import pallas as pl
from jax.experimental.pallas import tpu as pltpu
from jax.sharding import PartitionSpec as P

TIME_STEP = 0.001
VISCOSITY = 0.02
MESH = pl.DeviceIdType.MESH
F32 = jnp.float32
BF16 = jnp.bfloat16
NODES = 36
PAIR = 72
LANES = 128
INNER = ((6, 30), (42, 66))
OUTER = ((0, 6), (30, 36), (36, 42), (66, 72))


def differentiation():
    near = math.sqrt(1.0 / 3.0 - 2.0 * math.sqrt(7.0) / 21.0)
    far = math.sqrt(1.0 / 3.0 + 2.0 * math.sqrt(7.0) / 21.0)
    points = np.array([-1.0, -far, -near, near, far, 1.0])
    weights = np.array(
        [1.0 / np.prod([points[c] - points[s] for s in range(6) if s != c]) for c in range(6)]
    )
    deriv = np.zeros((6, 6))
    for t in range(6):
        for s in range(6):
            if s != t:
                deriv[t, s] = weights[s] / weights[t] / (points[t] - points[s])
        deriv[t, t] = -np.sum(deriv[t])
    return deriv


def split_np(x):
    high = x.astype(jnp.bfloat16)
    low = (x - high.astype(np.float64)).astype(jnp.bfloat16)
    return high, low


def basis_tables(count):
    m = np.arange(count)[:, None]
    n = np.arange(count)[None, :]
    angle = (m // 2 * n % count) * (2.0 * math.pi / count)
    basis = np.where(m % 2 == 1, np.sin(angle), np.cos(angle)) * math.sqrt(2.0 / count)
    basis[0] = 1.0 / math.sqrt(count)
    basis[1] = (1.0 - 2.0 * (np.arange(count) % 2)) / math.sqrt(count)
    minus = np.zeros_like(basis)
    k = np.arange(count // 2)[:, None]
    minus[0::2] = -k * basis[1::2]
    minus[1::2] = k * basis[0::2]
    both = np.concatenate([basis, minus], axis=1)
    return split_np(both)


def node_tables():
    deriv = differentiation()
    ident = np.eye(6)
    two = np.eye(2)
    along_x = np.zeros((PAIR, 168))
    along_y = np.zeros((PAIR, 168))
    lift = np.zeros((PAIR, 168))
    order = np.concatenate([np.arange(a, b) for a, b in INNER + OUTER])
    along_x[:, 0:72] = -np.kron(two, np.kron(deriv, ident))[order][:, order]
    along_y[:, 72:144] = -np.kron(two, np.kron(ident, deriv))[order][:, order]
    for e in range(2):
        for s2 in range(2):
            for j in range(6):
                lift[e * 36 + 6 * j + 5 * s2, 144 + e * 12 + s2 * 6 + j] = 1.0
    lift = lift[order]
    tables = np.stack([along_x, along_y, lift]).astype(np.float32)
    marks = np.zeros((PAIR, 8), np.float32)
    p = order % 36
    marks[:, 0] = 1.0 * (p // 6 == 5) - 1.0 * (p // 6 == 0)
    marks[:, 1] = 1.0 * (p % 6 == 5) - 1.0 * (p % 6 == 0)
    marks[:, 2] = np.abs(marks[:, 0])
    marks[:, 3] = np.abs(marks[:, 1])
    marks[:, 4] = order >= 36
    return tables, marks


def lookup_tables(elems, rows):
    spread = np.zeros((elems, elems // 2 * 32))
    marks = np.zeros((8, elems // 2 * 32), np.float32)
    lane = np.arange(elems // 2 * 32)
    r = lane % 32
    used = r < 24
    e = 2 * (lane // 32) + r % 24 // 12
    spread[e[used], lane[used]] = 1.0
    marks[0] = np.where(used, r % 6, 0)
    marks[1] = np.where(used, r // 6 % 2, 0)
    marks[3] = used
    rim_spread = np.zeros((rows, LANES))
    rim_lane = np.arange(6 * rows)
    rim_spread[rim_lane // 6, rim_lane] = 1.0
    marks[2, : 6 * rows] = rim_lane % 6
    return spread.astype(jnp.bfloat16), rim_spread.astype(jnp.bfloat16), marks


def split(x):
    high = x.astype(BF16)
    low = (x - high.astype(F32)).astype(BF16)
    return high, low


def dot3(a, b, dims):
    go = lambda x, y: lax.dot_general(x, y, (dims, ((), ())), preferred_element_type=F32)
    return go(a[0], b[0]) + (go(a[0], b[1]) + go(a[1], b[0]))


def pieces(src, dst, length):
    out = []
    done = 0
    while done < length:
        s, d = src + done, dst + done
        size = min(length - done, LANES - s % LANES, LANES - d % LANES)
        out.append((s // LANES, d // LANES, (d - s) % LANES, d % LANES, d % LANES + size))
        done += size
    return out


class Builder:
    def __init__(self, lane):
        self.lane = lane
        self.tiles = {}
        self.turned = {}

    def add(self, key, load, src, dst, length):
        for st, dt, shift, lo, hi in pieces(src, dst, length):
            name = (key, st, shift)
            if name not in self.turned:
                tile = load(st)
                self.turned[name] = pltpu.roll(tile, shift, 1) if shift else tile
            value = self.turned[name]
            if dt in self.tiles:
                value = jnp.where((self.lane >= lo) & (self.lane < hi), value, self.tiles[dt])
            self.tiles[dt] = value


def picked(tile, at):
    return jnp.take_along_axis(tile, at, axis=1, mode="promise_in_bounds")


def tile_indices():
    return tuple(lax.broadcasted_iota(jnp.int32, (8, LANES), dim) for dim in range(2))


def fold(tile, start, width, store):
    row8, lane = tile_indices()
    every = LANES // width
    tile = picked(tile, start + (lane & (width - 1)))
    tile = jnp.where(lane // width == (row8 & (every - 1)), tile, 0.0)
    for a in range(8 // every):
        store(a, jnp.sum(tile[every * a : every * (a + 1)], axis=0, keepdims=True))


def unfold(load, width):
    row8, lane = tile_indices()
    every = LANES // width
    tile = load(0)
    for a in range(1, 8 // every):
        tile = jnp.where(row8 < every * a, tile, load(a))
    return picked(jnp.broadcast_to(tile, (8, LANES)), (lane & (width - 1)) + width * (row8 & (every - 1)))


def fold_96(tile, store):
    fold(tile, 0, 64, store)
    fold(tile, 64, 32, lambda a, row: store(4 + a, row))


def unfold_96(load):
    lane = tile_indices()[1]
    return jnp.where(lane < 64, unfold(load, 64), unfold(lambda a: load(4 + a), 32))


def rows_of(ref, top):
    def store(a, row):
        ref[top + a : top + a + 1, :] = row

    return store, lambda a: ref[top + a : top + a + 1, :]


INNER_ROWS = 12
OUTER_ROWS = 6


def kernel(groups, span, *refs):
    given, refs = refs[:13], refs[13:]
    (result, outer_recv), refs = refs[:2], refs[2:]
    held, refs = refs[:13], refs[13:]
    (
        index, flip, others, rim_send, rim_recv, send_a, send_b, send_c, recv_a, recv_b, recv_c,
        modal_c, fields, rows_r, inner_sum, outer_sum, inner_send, outer_send, inner_recv, settled,
        load_sems, rim_sems, a_sems, b_sems, c_sems, inner_sems, outer_sems, result_sem, hello,
    ) = refs
    (
        state, rim, rim_spread, lane_marks, neighbour, orient, wall, spread,
        metric, node_tab, node_marks, both_high, both_low,
    ) = held
    me = lax.axis_index("span")
    group = lax.axis_index("elem")
    lower = lax.rem(group + groups - 1, groups)
    upper = lax.rem(group + 1, groups)
    elems = metric.shape[1]
    modes = span * 8
    state_tiles = elems * NODES // LANES

    loads = [pltpu.make_async_copy(a, b, load_sems.at[i]) for i, (a, b) in enumerate(zip(given, held))]
    for load in loads[:4]:
        load.start()

    barrier = pltpu.get_barrier_semaphore()

    def greet(k, carry):
        pl.semaphore_signal(
            barrier, 1, device_id=(group, lax.rem(me + k, span)), device_id_type=MESH
        )
        return carry

    pl.semaphore_signal(barrier, 1, device_id=(lower, me), device_id_type=MESH)
    lax.fori_loop(1, span, greet, 0)
    for load in loads[4:]:
        load.start()

    lane = lax.broadcasted_iota(jnp.int32, (8, LANES), 1)
    row8 = lax.broadcasted_iota(jnp.int32, (8, LANES), 0)

    def bases(slot):
        side = slot & 3
        vertical = side >= 2
        step = jnp.where(vertical, 6, 1)
        first = jnp.where(vertical, jnp.where(side == 3, 5, 0), jnp.where(side == 1, 30, 0))
        return NODES * (slot >> 2) + first, step

    def spread_over(values, matrix):
        high = (values >> 6).astype(F32).astype(BF16)
        low = (values & 63).astype(F32).astype(BF16)
        go = lambda x: jnp.dot(x, matrix, preferred_element_type=F32)
        return (go(high) * 64.0 + go(low)).astype(jnp.int32)

    def gather(at, start, tiles):
        low = at & (LANES - 1)
        high = at >> 7
        totals = list(start)
        for k in tiles:
            here = high == k
            for v in range(4):
                tile = (
                    state[v, :, k * LANES : (k + 1) * LANES]
                    if k < state_tiles
                    else rim_recv[k - state_tiles, v]
                )
                totals[v] = jnp.where(here, picked(tile, low), totals[v])
        return totals

    for load in loads[1:4]:
        load.wait()
    rim_base, rim_step = bases(rim[...])
    node_r = lane_marks[2:3, 0:LANES].astype(jnp.int32)
    rim_index = spread_over(rim_base, rim_spread[...]) + node_r * spread_over(
        rim_step, rim_spread[...]
    )
    loads[0].wait()
    zero = [jnp.zeros((8, LANES), F32)] * 4
    for way in range(2):
        at = jnp.broadcast_to(rim_index[way : way + 1], (8, LANES))
        got = gather(at, zero, range(state_tiles))
        for v in range(4):
            rim_send[way, v] = got[v]

    def rim_copy(way, to):
        return pltpu.make_async_remote_copy(
            rim_send.at[way], rim_recv.at[1 - way], rim_sems.at[way], rim_sems.at[3 - way],
            device_id=(to, me), device_id_type=MESH,
        )

    rim_up, rim_down = rim_copy(1, upper), rim_copy(0, lower)
    for d in range(span):
        b = Builder(lane)
        for v in range(4):
            b.add(v, lambda k, v=v: state[v, :, k * LANES : (k + 1) * LANES], PAIR * d, PAIR * v, PAIR)
        rows = slice(8 * d, 8 * d + 8)
        send_a[rows, 0:LANES] = b.tiles[0]
        send_a[rows, LANES:] = b.tiles[1]
        send_b[rows, :] = b.tiles[2]

    pl.semaphore_wait(barrier, span)
    pl.semaphore_signal(hello, 1, device_id=(upper, me), device_id_type=MESH)
    rim_up.start()

    def exchange(send, recv, rows, sems):
        arrived = sems.at[1]
        at = lambda who: pl.ds(pl.multiple_of(rows * who, 8) if rows == 8 else rows * who, rows)

        def one(k, carry):
            to = lax.rem(me + k, span)
            pltpu.make_async_remote_copy(
                send.at[at(to), :], recv.at[at(me), :], sems.at[0], arrived,
                device_id=(group, to), device_id_type=MESH,
            ).start()
            return carry

        lax.fori_loop(1, span, one, 0)
        pltpu.make_async_copy(send.at[at(me), :], recv.at[at(me), :], arrived).start()

    exchange(send_a, recv_a, 8, a_sems)

    @pl.when(group > 0)
    def _():
        pl.semaphore_wait(hello, 1)
        rim_down.start()


    for load in loads[4:8]:
        load.wait()
    slot = neighbour[...]
    turn = orient[...]
    remote = slot >= 4 * elems
    base, step = bases(slot)
    row = slot - 4 * elems
    base = jnp.where(remote, state_tiles * LANES + LANES * (row >> 4) + 6 * (row & 15), base)
    step = jnp.where(remote, 1, step)
    base = jnp.where(turn == 1, base + 5 * step, base)
    step = jnp.where(turn == 1, -step, step)
    matrix = spread[...]
    base_l = spread_over(base, matrix)
    step_l = spread_over(step + 8, matrix) - 8
    wall_l = spread_over(wall[...], matrix)
    node_l = lane_marks[0:1, :].astype(jnp.int32)
    second = lane_marks[1:2, :] > 0.5
    used = lane_marks[3:4, :] > 0.5
    for axis in range(2):
        pick = lambda x: jnp.where(second, x[2 * axis + 1 : 2 * axis + 2], x[2 * axis : 2 * axis + 1])
        lanes_at = jnp.where(used, pick(base_l) + pick(step_l) * node_l, 0)
        walls = 1.0 - 2.0 * pick(wall_l).astype(F32)
        for t in range(index.shape[1]):
            cut = slice(t * LANES, (t + 1) * LANES)
            index[axis, t] = jnp.broadcast_to(lanes_at[:, cut], (8, LANES))
            flip[axis, t] = jnp.broadcast_to(walls[:, cut], (8, LANES))

    def gather_axis(axis, tiles, first):
        def one(t, carry):
            at = index[axis, t]
            start = zero if first else [others[axis, v, t] for v in range(4)]
            got = gather(at, start, tiles)
            for v in range(4):
                others[axis, v, t] = got[v]
            return carry

        lax.fori_loop(0, index.shape[1], one, 0)

    def reflected(axis, v, t):
        tile = others[axis, v, t]
        return tile * flip[axis, t] if v < 3 else tile

    gather_axis(1, range(state_tiles), True)
    for d in range(span):
        b = Builder(lane)
        b.tiles[0] = send_b[8 * d : 8 * d + 8, :]
        for v in range(4):
            b.add(v, lambda k, v=v: reflected(1, v, k), 32 * d, 32 + 24 * v, 24)
        send_b[8 * d : 8 * d + 8, :] = b.tiles[0]
    exchange(send_b, recv_b, 8, b_sems)
    gather_axis(0, range(state_tiles), True)

    @pl.when(group == 0)
    def _():
        pl.semaphore_wait(hello, 1)
        rim_down.start()

    rim_up.wait()
    rim_down.wait()
    gather_axis(0, range(state_tiles, state_tiles + 2), False)

    for d in range(span):
        b = Builder(lane)
        for v in range(4):
            b.add(v, lambda k, v=v: reflected(0, v, k), 32 * d, 24 * v, 24)
        fold_96(b.tiles[0], rows_of(send_c, OUTER_ROWS * d)[0])
    exchange(send_c, recv_c, OUTER_ROWS, c_sems)

    for load in loads[8:]:
        load.wait()
    at = lax.broadcasted_iota(jnp.int32, (2, elems), 1)
    scale = metric[...]
    first = jnp.sum(jnp.where(at == 2 * me, scale, 0.0), axis=1, keepdims=True)
    last = jnp.sum(jnp.where(at == 2 * me + 1, scale, 0.0), axis=1, keepdims=True)

    def per_row(on_first, which):
        return jnp.where(on_first, first[which : which + 1], last[which : which + 1])

    marks = node_marks[...]
    on_first = marks[:, 4:5] < 0.5
    rx, ry = per_row(on_first, 0), per_row(on_first, 1)
    coef_u = 7.5 * rx * marks[:, 0:1]
    coef_v = 7.5 * ry * marks[:, 1:2]
    coef_c = 7.5 * (jnp.abs(rx) * marks[:, 2:3] + jnp.abs(ry) * marks[:, 3:4])
    operator = split(rx * node_tab[0] + ry * node_tab[1] + node_tab[2])
    side = lax.broadcasted_iota(jnp.int32, (24, 1), 0)
    low_side = (side < 6) | ((side >= 12) & (side < 18))
    toward = jnp.where(low_side, 7.5, -7.5)
    ox, oy = per_row(side < 12, 0), per_row(side < 12, 1)

    over0, over1 = ((0,), (0,)), ((1,), (1,))
    basis = (both_high[:, 0:modes], both_low[:, 0:modes])
    pltpu.make_async_copy(recv_a, recv_a, a_sems.at[1]).wait()
    planes_a = dot3(split(recv_a[...]), basis, over0)
    pltpu.make_async_copy(recv_b, recv_b, b_sems.at[1]).wait()
    planes_b = dot3(split(recv_b[...]), basis, over0)
    own = [planes_a[PAIR * v : PAIR * (v + 1)] for v in range(3)]
    own.append(jnp.concatenate([planes_a[3 * PAIR :], planes_b[0:32]], axis=0))
    own = [jnp.concatenate([x[a:b] for a, b in INNER + OUTER], axis=0) for x in own]
    facing_y = [planes_b[32 + 24 * v : 56 + 24 * v] for v in range(4)]
    own_coef = coef_u * own[0] + coef_v * own[1] - coef_c
    facing_y_coef = (toward * oy) * facing_y[1] + 7.5 * jnp.abs(oy)
    for v in range(4):
        fields[v, 0:72] = own[0] * own[v]
        fields[v, 72:144] = own[1] * own[v]
        fields[v, 144:168] = facing_y_coef * facing_y[v]
        along_z = own[2] * own[v]
        planar = own_coef * own[v] + dot3(operator, split(fields[v]), ((1,), (0,)))
        for part, at in ((planar, slice(0, modes)), (along_z, slice(modes, 2 * modes))):
            rows_r[48 * v : 48 * v + 48, at] = part[0:48]
            rows_r[192 + 24 * v : 216 + 24 * v, at] = part[48:72]
    both = (both_high[...], both_low[...])

    def damped(mode):
        k = jnp.where(mode == 1, modes // 2, mode >> 1).astype(F32)
        return 1.0 / (1.0 + TIME_STEP * VISCOSITY * k * k)

    step_of = TIME_STEP * damped(lax.broadcasted_iota(jnp.int32, (modes, 1), 0))

    inner_sum[:, 0:192] = step_of * dot3(both, split(rows_r[0:192, :]), over1)
    for d in range(span):
        mine = inner_sum[8 * d : 8 * d + 8, :]
        top = INNER_ROWS * d
        inner_send[top : top + 8, :] = mine[:, 0:LANES]
        fold(mine[:, LANES:], 0, 64, rows_of(inner_send, top + 8)[0])
    exchange(inner_send, inner_recv, INNER_ROWS, inner_sems)
    outer_sum[:, 0:96] = dot3(both, split(rows_r[192:288, :]), over1)

    pltpu.make_async_copy(recv_c, recv_c, c_sems.at[1]).wait()
    for s in range(span):
        modal_c[8 * s : 8 * s + 8, :] = unfold_96(rows_of(recv_c, OUTER_ROWS * s)[1])
    planes_c = dot3(split(modal_c[:, 0:96]), basis, over0)
    facing_x_coef = (toward * ox) * planes_c[0:24] + 7.5 * jnp.abs(ox)
    jump = split(jnp.concatenate([facing_x_coef] * 4, axis=0) * planes_c)
    outer_sum[:, 0:96] = step_of * (outer_sum[:, 0:96] + dot3(basis, jump, over1))
    for d in range(span):
        fold_96(outer_sum[8 * d : 8 * d + 8, :], rows_of(outer_send, OUTER_ROWS * d)[0])
    exchange(outer_send, outer_recv, OUTER_ROWS, outer_sems)

    shrink = damped(8 * me + row8)
    pltpu.make_async_copy(inner_recv, inner_recv, inner_sems.at[1]).wait()
    nothing = jnp.zeros((8, LANES), F32)
    builders = [Builder(lane) for _ in range(4)]
    for v in range(4):
        builders[v].tiles = {t: nothing for t in range(state_tiles)}
    for s in range(span):
        top = INNER_ROWS * s

        def inner(t, top=top):
            if t == 0:
                return inner_recv[top : top + 8, :]
            return unfold(rows_of(inner_recv, top + 8)[1], 64)

        tiles = [inner(0), inner(1)]
        for v in range(4):
            for e, (a, b) in enumerate(INNER):
                builders[v].add((s, e), lambda t, x=tiles: x[t], 48 * v + 24 * e, PAIR * s + a, 24)
    for v in range(4):
        for t in range(state_tiles):
            cut = slice(t * LANES, (t + 1) * LANES)
            settled[v, :, cut] = state[v, :, cut] * shrink + builders[v].tiles[t]
    put = pltpu.make_async_copy(settled, result, result_sem)
    put.start()
    pltpu.make_async_copy(outer_recv, outer_recv, outer_sems.at[1]).wait()
    put.wait()

    for send, rows, sems in (
        (send_a, 8, a_sems), (send_b, 8, b_sems), (send_c, OUTER_ROWS, c_sems),
        (inner_send, INNER_ROWS, inner_sems), (outer_send, OUTER_ROWS, outer_sems),
    ):
        sent = send.at[0 : rows * (span - 1), :]
        pltpu.make_async_copy(sent, sent, sems.at[0]).wait()


def finish(span, base, outer, out, base_v, outer_v, out_v, load_sems, store_sems):
    loads = [
        pltpu.make_async_copy(a, b, load_sems.at[i])
        for i, (a, b) in enumerate(((outer, outer_v), (base, base_v)))
    ]
    for load in loads:
        load.start()
    loads[0].wait()
    lane = tile_indices()[1]
    tiles = [unfold_96(rows_of(outer_v, OUTER_ROWS * s)[1]) for s in range(span)]
    loads[1].wait()
    stores = []
    for v in range(4):
        b = Builder(lane)
        for t in range(base.shape[2] // LANES):
            b.tiles[t] = jnp.zeros((8, LANES), F32)
        for s in range(span):
            for src, dst, length in ((0, 0, 6), (6, 30, 12), (18, 66, 6)):
                b.add((s, src), lambda t, x=tiles[s]: x, 24 * v + src, PAIR * s + dst, length)
        for t in range(base.shape[2] // LANES):
            cut = slice(t * LANES, (t + 1) * LANES)
            out_v[v, :, cut] = base_v[v, :, cut] + b.tiles[t]
        store = pltpu.make_async_copy(out_v.at[v], out.at[v], store_sems.at[v])
        store.start()
        stores.append(store)
    for store in stores:
        store.wait()


def body(groups, span, state, metric, neighbour, orient, wall, rim):
    elems = metric.shape[1]
    modes = span * 8
    tables, marks = node_tables()
    spread, rim_spread, lane_marks = lookup_tables(elems, rim.shape[1])
    both_high, both_low = basis_tables(modes)
    given = [
        state, rim, rim_spread, lane_marks, neighbour.T, orient.T, wall.T, spread,
        metric, tables, marks, both_high, both_low,
    ]
    given = [jnp.asarray(x) for x in given]
    gathered = elems // 2 * 32 // LANES
    scratch = [pltpu.VMEM(x.shape, x.dtype) for x in given] + [
        pltpu.VMEM((2, gathered, 8, LANES), jnp.int32),
        pltpu.VMEM((2, gathered, 8, LANES), F32),
        pltpu.VMEM((2, 4, gathered, 8, LANES), F32),
        pltpu.VMEM((2, 4, 8, LANES), F32),
        pltpu.VMEM((2, 4, 8, LANES), F32),
        pltpu.VMEM((modes, 256), F32),
        pltpu.VMEM((modes, LANES), F32),
        pltpu.VMEM((OUTER_ROWS * span, LANES), F32),
        pltpu.VMEM((modes, 256), F32),
        pltpu.VMEM((modes, LANES), F32),
        pltpu.VMEM((OUTER_ROWS * span, LANES), F32),
        pltpu.VMEM((modes, LANES), F32),
        pltpu.VMEM((4, 168, modes), F32),
        pltpu.VMEM((288, 2 * modes), F32),
        pltpu.VMEM((modes, 256), F32),
        pltpu.VMEM((modes, LANES), F32),
        pltpu.VMEM((INNER_ROWS * span, LANES), F32),
        pltpu.VMEM((OUTER_ROWS * span, LANES), F32),
        pltpu.VMEM((INNER_ROWS * span, LANES), F32),
        pltpu.VMEM(state.shape, F32),
        pltpu.SemaphoreType.DMA((len(given),)),
        pltpu.SemaphoreType.DMA((4,)),
        pltpu.SemaphoreType.DMA((2,)),
        pltpu.SemaphoreType.DMA((2,)),
        pltpu.SemaphoreType.DMA((2,)),
        pltpu.SemaphoreType.DMA((2,)),
        pltpu.SemaphoreType.DMA((2,)),
        pltpu.SemaphoreType.DMA,
        pltpu.SemaphoreType.REGULAR,
    ]
    hbm = pl.BlockSpec(memory_space=pltpu.HBM)
    outer = jax.ShapeDtypeStruct((OUTER_ROWS * span, LANES), F32)
    whole = jax.ShapeDtypeStruct(state.shape, F32)
    base, outer_rows = pl.pallas_call(
        functools.partial(kernel, groups, span),
        out_shape=(whole, outer),
        in_specs=[hbm] * len(given),
        out_specs=(hbm, hbm),
        scratch_shapes=scratch,
        compiler_params=pltpu.CompilerParams(
            collective_id=0, has_side_effects=True, vmem_limit_bytes=60 << 20
        ),
        name="section",
    )(*given)
    return pl.pallas_call(
        functools.partial(finish, span),
        out_shape=whole,
        in_specs=[hbm, hbm],
        out_specs=hbm,
        scratch_shapes=[
            pltpu.VMEM(whole.shape, F32), pltpu.VMEM(outer.shape, F32), pltpu.VMEM(whole.shape, F32),
            pltpu.SemaphoreType.DMA((2,)), pltpu.SemaphoreType.DMA((4,)),
        ],
        compiler_params=pltpu.CompilerParams(vmem_limit_bytes=60 << 20),
        name="finish",
    )(base, outer_rows)


def solution(mesh):
    specs = (
        P(None, "span", "elem"), P(None, "elem"), P("elem", None),
        P("elem", None), P("elem", None), P(None, "elem"),
    )
    return jax.shard_map(
        functools.partial(body, mesh.shape["elem"], mesh.shape["span"]),
        mesh=mesh, in_specs=specs, out_specs=P(None, "span", "elem"), check_vma=False,
    )
```

```python
import functools
import math

import jax
import jax.numpy as jnp
import numpy as np
from jax import lax
from jax.experimental import pallas as pl
from jax.experimental.pallas import tpu as pltpu
from jax.sharding import PartitionSpec as P

TIME_STEP = 0.001
VISCOSITY = 0.02
MESH = pl.DeviceIdType.MESH
F32 = jnp.float32
BF16 = jnp.bfloat16
NODES = 36
PAIR = 72
LANES = 128
INNER = ((6, 30), (42, 66))
OUTER = ((0, 6), (30, 36), (36, 42), (66, 72))


def differentiation():
    near = math.sqrt(1.0 / 3.0 - 2.0 * math.sqrt(7.0) / 21.0)
    far = math.sqrt(1.0 / 3.0 + 2.0 * math.sqrt(7.0) / 21.0)
    points = np.array([-1.0, -far, -near, near, far, 1.0])
    weights = np.array(
        [1.0 / np.prod([points[c] - points[s] for s in range(6) if s != c]) for c in range(6)]
    )
    deriv = np.zeros((6, 6))
    for t in range(6):
        for s in range(6):
            if s != t:
                deriv[t, s] = weights[s] / weights[t] / (points[t] - points[s])
        deriv[t, t] = -np.sum(deriv[t])
    return deriv


def split_np(x):
    high = x.astype(jnp.bfloat16)
    low = (x - high.astype(np.float64)).astype(jnp.bfloat16)
    return high, low


def basis_tables(count):
    m = np.arange(count)[:, None]
    n = np.arange(count)[None, :]
    angle = (m // 2 * n % count) * (2.0 * math.pi / count)
    basis = np.where(m % 2 == 1, np.sin(angle), np.cos(angle)) * math.sqrt(2.0 / count)
    basis[0] = 1.0 / math.sqrt(count)
    basis[1] = (1.0 - 2.0 * (np.arange(count) % 2)) / math.sqrt(count)
    minus = np.zeros_like(basis)
    k = np.arange(count // 2)[:, None]
    minus[0::2] = -k * basis[1::2]
    minus[1::2] = k * basis[0::2]
    both = np.concatenate([basis, minus], axis=1)
    return split_np(both)


def node_tables():
    deriv = differentiation()
    ident = np.eye(6)
    two = np.eye(2)
    along_x = np.zeros((PAIR, 168))
    along_y = np.zeros((PAIR, 168))
    lift = np.zeros((PAIR, 168))
    order = np.concatenate([np.arange(a, b) for a, b in INNER + OUTER])
    along_x[:, 0:72] = -np.kron(two, np.kron(deriv, ident))[order][:, order]
    along_y[:, 72:144] = -np.kron(two, np.kron(ident, deriv))[order][:, order]
    for e in range(2):
        for s2 in range(2):
            for j in range(6):
                lift[e * 36 + 6 * j + 5 * s2, 144 + e * 12 + s2 * 6 + j] = 1.0
    lift = lift[order]
    tables = np.stack([along_x, along_y, lift]).astype(np.float32)
    marks = np.zeros((PAIR, 8), np.float32)
    p = order % 36
    marks[:, 0] = 1.0 * (p // 6 == 5) - 1.0 * (p // 6 == 0)
    marks[:, 1] = 1.0 * (p % 6 == 5) - 1.0 * (p % 6 == 0)
    marks[:, 2] = np.abs(marks[:, 0])
    marks[:, 3] = np.abs(marks[:, 1])
    marks[:, 4] = order >= 36
    return tables, marks


def lookup_tables(elems, rows):
    spread = np.zeros((elems, elems // 2 * 32))
    marks = np.zeros((8, elems // 2 * 32), np.float32)
    lane = np.arange(elems // 2 * 32)
    r = lane % 32
    used = r < 24
    e = 2 * (lane // 32) + r % 24 // 12
    spread[e[used], lane[used]] = 1.0
    marks[0] = np.where(used, r % 6, 0)
    marks[1] = np.where(used, r // 6 % 2, 0)
    marks[3] = used
    rim_spread = np.zeros((rows, LANES))
    rim_lane = np.arange(6 * rows)
    rim_spread[rim_lane // 6, rim_lane] = 1.0
    marks[2, : 6 * rows] = rim_lane % 6
    return spread.astype(jnp.bfloat16), rim_spread.astype(jnp.bfloat16), marks


def split(x):
    high = x.astype(BF16)
    low = (x - high.astype(F32)).astype(BF16)
    return high, low


def dot3(a, b, dims):
    go = lambda x, y: lax.dot_general(x, y, (dims, ((), ())), preferred_element_type=F32)
    return go(a[0], b[0]) + (go(a[0], b[1]) + go(a[1], b[0]))


def pieces(src, dst, length):
    out = []
    done = 0
    while done < length:
        s, d = src + done, dst + done
        size = min(length - done, LANES - s % LANES, LANES - d % LANES)
        out.append((s // LANES, d // LANES, (d - s) % LANES, d % LANES, d % LANES + size))
        done += size
    return out


class Builder:
    def __init__(self, lane):
        self.lane = lane
        self.tiles = {}
        self.turned = {}

    def add(self, key, load, src, dst, length):
        for st, dt, shift, lo, hi in pieces(src, dst, length):
            name = (key, st, shift)
            if name not in self.turned:
                tile = load(st)
                self.turned[name] = pltpu.roll(tile, shift, 1) if shift else tile
            value = self.turned[name]
            if dt in self.tiles:
                value = jnp.where((self.lane >= lo) & (self.lane < hi), value, self.tiles[dt])
            self.tiles[dt] = value


def picked(tile, at):
    return jnp.take_along_axis(tile, at, axis=1, mode="promise_in_bounds")


def tile_indices():
    return tuple(lax.broadcasted_iota(jnp.int32, (8, LANES), dim) for dim in range(2))


def fold(tile, start, width, store):
    row8, lane = tile_indices()
    every = LANES // width
    tile = picked(tile, start + (lane & (width - 1)))
    tile = jnp.where(lane // width == (row8 & (every - 1)), tile, 0.0)
    for a in range(8 // every):
        store(a, jnp.sum(tile[every * a : every * (a + 1)], axis=0, keepdims=True))


def unfold(load, width):
    row8, lane = tile_indices()
    every = LANES // width
    tile = load(0)
    for a in range(1, 8 // every):
        tile = jnp.where(row8 < every * a, tile, load(a))
    return picked(jnp.broadcast_to(tile, (8, LANES)), (lane & (width - 1)) + width * (row8 & (every - 1)))


def fold_96(tile, store):
    fold(tile, 0, 64, store)
    fold(tile, 64, 32, lambda a, row: store(4 + a, row))


def unfold_96(load):
    lane = tile_indices()[1]
    return jnp.where(lane < 64, unfold(load, 64), unfold(lambda a: load(4 + a), 32))


def rows_of(ref, top):
    def store(a, row):
        ref[top + a : top + a + 1, :] = row

    return store, lambda a: ref[top + a : top + a + 1, :]


INNER_ROWS = 12
OUTER_ROWS = 6


def kernel(groups, span, *refs):
    given, refs = refs[:13], refs[13:]
    (result, outer_recv), refs = refs[:2], refs[2:]
    held, refs = refs[:13], refs[13:]
    (
        index, flip, others, rim_send, rim_recv, send_a, send_b, send_c, recv_a, recv_b, recv_c,
        modal_c, fields, rows_r, inner_sum, outer_sum, inner_send, outer_send, inner_recv, settled,
        load_sems, rim_sems, a_sems, b_sems, c_sems, inner_sems, outer_sems, result_sem, hello,
    ) = refs
    (
        state, rim, rim_spread, lane_marks, neighbour, orient, wall, spread,
        metric, node_tab, node_marks, both_high, both_low,
    ) = held
    me = lax.axis_index("span")
    group = lax.axis_index("elem")
    lower = lax.rem(group + groups - 1, groups)
    upper = lax.rem(group + 1, groups)
    elems = metric.shape[1]
    modes = span * 8
    state_tiles = elems * NODES // LANES

    loads = [pltpu.make_async_copy(a, b, load_sems.at[i]) for i, (a, b) in enumerate(zip(given, held))]
    for load in loads[:4]:
        load.start()

    barrier = pltpu.get_barrier_semaphore()

    def greet(k, carry):
        pl.semaphore_signal(
            barrier, 1, device_id=(group, lax.rem(me + k, span)), device_id_type=MESH
        )
        return carry

    pl.semaphore_signal(barrier, 1, device_id=(lower, me), device_id_type=MESH)
    lax.fori_loop(1, span, greet, 0)
    for load in loads[4:]:
        load.start()

    lane = lax.broadcasted_iota(jnp.int32, (8, LANES), 1)
    row8 = lax.broadcasted_iota(jnp.int32, (8, LANES), 0)

    def bases(slot):
        side = slot & 3
        vertical = side >= 2
        step = jnp.where(vertical, 6, 1)
        first = jnp.where(vertical, jnp.where(side == 3, 5, 0), jnp.where(side == 1, 30, 0))
        return NODES * (slot >> 2) + first, step

    def spread_over(values, matrix):
        high = (values >> 6).astype(F32).astype(BF16)
        low = (values & 63).astype(F32).astype(BF16)
        go = lambda x: jnp.dot(x, matrix, preferred_element_type=F32)
        return (go(high) * 64.0 + go(low)).astype(jnp.int32)

    def gather(at, start, tiles):
        low = at & (LANES - 1)
        high = at >> 7
        totals = list(start)
        for k in tiles:
            here = high == k
            for v in range(4):
                tile = (
                    state[v, :, k * LANES : (k + 1) * LANES]
                    if k < state_tiles
                    else rim_recv[k - state_tiles, v]
                )
                totals[v] = jnp.where(here, picked(tile, low), totals[v])
        return totals

    for load in loads[1:4]:
        load.wait()
    rim_base, rim_step = bases(rim[...])
    node_r = lane_marks[2:3, 0:LANES].astype(jnp.int32)
    rim_index = spread_over(rim_base, rim_spread[...]) + node_r * spread_over(
        rim_step, rim_spread[...]
    )
    loads[0].wait()
    zero = [jnp.zeros((8, LANES), F32)] * 4
    for way in range(2):
        at = jnp.broadcast_to(rim_index[way : way + 1], (8, LANES))
        got = gather(at, zero, range(state_tiles))
        for v in range(4):
            rim_send[way, v] = got[v]

    def rim_copy(way, to):
        return pltpu.make_async_remote_copy(
            rim_send.at[way], rim_recv.at[1 - way], rim_sems.at[way], rim_sems.at[3 - way],
            device_id=(to, me), device_id_type=MESH,
        )

    rim_up, rim_down = rim_copy(1, upper), rim_copy(0, lower)
    for d in range(span):
        b = Builder(lane)
        for v in range(4):
            b.add(v, lambda k, v=v: state[v, :, k * LANES : (k + 1) * LANES], PAIR * d, PAIR * v, PAIR)
        rows = slice(8 * d, 8 * d + 8)
        send_a[rows, 0:LANES] = b.tiles[0]
        send_a[rows, LANES:] = b.tiles[1]
        send_b[rows, :] = b.tiles[2]

    pl.semaphore_wait(barrier, span)
    pl.semaphore_signal(hello, 1, device_id=(upper, me), device_id_type=MESH)
    rim_up.start()

    def exchange(send, recv, rows, sems):
        arrived = sems.at[1]
        at = lambda who: pl.ds(pl.multiple_of(rows * who, 8) if rows == 8 else rows * who, rows)

        def one(k, carry):
            to = lax.rem(me + k, span)
            pltpu.make_async_remote_copy(
                send.at[at(to), :], recv.at[at(me), :], sems.at[0], arrived,
                device_id=(group, to), device_id_type=MESH,
            ).start()
            return carry

        lax.fori_loop(1, span, one, 0)
        pltpu.make_async_copy(send.at[at(me), :], recv.at[at(me), :], arrived).start()

    exchange(send_a, recv_a, 8, a_sems)

    @pl.when(group > 0)
    def _():
        pl.semaphore_wait(hello, 1)
        rim_down.start()


    for load in loads[4:8]:
        load.wait()
    slot = neighbour[...]
    turn = orient[...]
    remote = slot >= 4 * elems
    base, step = bases(slot)
    row = slot - 4 * elems
    base = jnp.where(remote, state_tiles * LANES + LANES * (row >> 4) + 6 * (row & 15), base)
    step = jnp.where(remote, 1, step)
    base = jnp.where(turn == 1, base + 5 * step, base)
    step = jnp.where(turn == 1, -step, step)
    matrix = spread[...]
    base_l = spread_over(base, matrix)
    step_l = spread_over(step + 8, matrix) - 8
    wall_l = spread_over(wall[...], matrix)
    node_l = lane_marks[0:1, :].astype(jnp.int32)
    second = lane_marks[1:2, :] > 0.5
    used = lane_marks[3:4, :] > 0.5
    for axis in range(2):
        pick = lambda x: jnp.where(second, x[2 * axis + 1 : 2 * axis + 2], x[2 * axis : 2 * axis + 1])
        lanes_at = jnp.where(used, pick(base_l) + pick(step_l) * node_l, 0)
        walls = 1.0 - 2.0 * pick(wall_l).astype(F32)
        for t in range(index.shape[1]):
            cut = slice(t * LANES, (t + 1) * LANES)
            index[axis, t] = jnp.broadcast_to(lanes_at[:, cut], (8, LANES))
            flip[axis, t] = jnp.broadcast_to(walls[:, cut], (8, LANES))

    def gather_axis(axis, tiles, first):
        def one(t, carry):
            at = index[axis, t]
            start = zero if first else [others[axis, v, t] for v in range(4)]
            got = gather(at, start, tiles)
            for v in range(4):
                others[axis, v, t] = got[v]
            return carry

        lax.fori_loop(0, index.shape[1], one, 0)

    def reflected(axis, v, t):
        tile = others[axis, v, t]
        return tile * flip[axis, t] if v < 3 else tile

    gather_axis(1, range(state_tiles), True)
    for d in range(span):
        b = Builder(lane)
        b.tiles[0] = send_b[8 * d : 8 * d + 8, :]
        for v in range(4):
            b.add(v, lambda k, v=v: reflected(1, v, k), 32 * d, 32 + 24 * v, 24)
        send_b[8 * d : 8 * d + 8, :] = b.tiles[0]
    exchange(send_b, recv_b, 8, b_sems)
    gather_axis(0, range(state_tiles), True)

    @pl.when(group == 0)
    def _():
        pl.semaphore_wait(hello, 1)
        rim_down.start()

    rim_up.wait()
    rim_down.wait()
    gather_axis(0, range(state_tiles, state_tiles + 2), False)

    for d in range(span):
        b = Builder(lane)
        for v in range(4):
            b.add(v, lambda k, v=v: reflected(0, v, k), 32 * d, 24 * v, 24)
        fold_96(b.tiles[0], rows_of(send_c, OUTER_ROWS * d)[0])
    exchange(send_c, recv_c, OUTER_ROWS, c_sems)

    for load in loads[8:]:
        load.wait()
    at = lax.broadcasted_iota(jnp.int32, (2, elems), 1)
    scale = metric[...]
    first = jnp.sum(jnp.where(at == 2 * me, scale, 0.0), axis=1, keepdims=True)
    last = jnp.sum(jnp.where(at == 2 * me + 1, scale, 0.0), axis=1, keepdims=True)

    def per_row(on_first, which):
        return jnp.where(on_first, first[which : which + 1], last[which : which + 1])

    marks = node_marks[...]
    on_first = marks[:, 4:5] < 0.5
    rx, ry = per_row(on_first, 0), per_row(on_first, 1)
    coef_u = 7.5 * rx * marks[:, 0:1]
    coef_v = 7.5 * ry * marks[:, 1:2]
    coef_c = 7.5 * (jnp.abs(rx) * marks[:, 2:3] + jnp.abs(ry) * marks[:, 3:4])
    operator = split(rx * node_tab[0, :, 0:144] + ry * node_tab[1, :, 0:144])
    lift_y = node_tab[2, :, 144:168].astype(BF16)
    over1_0 = ((1,), (0,))
    side = lax.broadcasted_iota(jnp.int32, (24, 1), 0)
    low_side = (side < 6) | ((side >= 12) & (side < 18))
    toward = jnp.where(low_side, 7.5, -7.5)
    ox, oy = per_row(side < 12, 0), per_row(side < 12, 1)

    over0, over1 = ((0,), (0,)), ((1,), (1,))
    basis = (both_high[:, 0:modes], both_low[:, 0:modes])
    pltpu.make_async_copy(recv_a, recv_a, a_sems.at[1]).wait()
    planes_a = dot3(split(recv_a[...]), basis, over0)
    reorder = lambda x: jnp.concatenate([x[a:b] for a, b in INNER + OUTER], axis=0)
    own = [reorder(planes_a[PAIR * v : PAIR * (v + 1)]) for v in range(3)]
    own_coef = coef_u * own[0] + coef_v * own[1] - coef_c

    def own_terms(v):
        fields[v, 0:72] = own[0] * own[v]
        fields[v, 72:144] = own[1] * own[v]
        planar = own_coef * own[v] + dot3(operator, split(fields[v]), over1_0)
        for part, at in ((planar, slice(0, modes)), (own[2] * own[v], slice(modes, 2 * modes))):
            rows_r[48 * v : 48 * v + 48, at] = part[0:48]
            rows_r[192 + 24 * v : 216 + 24 * v, at] = part[48:72]

    for v in range(3):
        own_terms(v)
    pltpu.make_async_copy(recv_b, recv_b, b_sems.at[1]).wait()
    planes_b = dot3(split(recv_b[...]), basis, over0)
    own.append(reorder(jnp.concatenate([planes_a[3 * PAIR :], planes_b[0:32]], axis=0)))
    facing_y_coef = (toward * oy) * planes_b[56:80] + 7.5 * jnp.abs(oy)
    facing_y = [split(facing_y_coef * planes_b[32 + 24 * v : 56 + 24 * v]) for v in range(4)]
    own_terms(3)
    for v in range(4):
        lifted = sum(jnp.dot(lift_y, part, preferred_element_type=F32) for part in facing_y[v])
        rows_r[48 * v : 48 * v + 48, 0:modes] += lifted[0:48]
        rows_r[192 + 24 * v : 216 + 24 * v, 0:modes] += lifted[48:72]
    both = (both_high[...], both_low[...])

    def damped(mode):
        k = jnp.where(mode == 1, modes // 2, mode >> 1).astype(F32)
        return 1.0 / (1.0 + TIME_STEP * VISCOSITY * k * k)

    step_of = TIME_STEP * damped(lax.broadcasted_iota(jnp.int32, (modes, 1), 0))

    inner_sum[:, 0:192] = step_of * dot3(both, split(rows_r[0:192, :]), over1)
    for d in range(span):
        mine = inner_sum[8 * d : 8 * d + 8, :]
        top = INNER_ROWS * d
        inner_send[top : top + 8, :] = mine[:, 0:LANES]
        fold(mine[:, LANES:], 0, 64, rows_of(inner_send, top + 8)[0])
    exchange(inner_send, inner_recv, INNER_ROWS, inner_sems)
    outer_sum[:, 0:96] = dot3(both, split(rows_r[192:288, :]), over1)

    pltpu.make_async_copy(recv_c, recv_c, c_sems.at[1]).wait()
    for s in range(span):
        modal_c[8 * s : 8 * s + 8, :] = unfold_96(rows_of(recv_c, OUTER_ROWS * s)[1])
    planes_c = dot3(split(modal_c[:, 0:96]), basis, over0)
    facing_x_coef = (toward * ox) * planes_c[0:24] + 7.5 * jnp.abs(ox)
    jump = split(jnp.concatenate([facing_x_coef] * 4, axis=0) * planes_c)
    outer_sum[:, 0:96] = step_of * (outer_sum[:, 0:96] + dot3(basis, jump, over1))
    for d in range(span):
        fold_96(outer_sum[8 * d : 8 * d + 8, :], rows_of(outer_send, OUTER_ROWS * d)[0])
    exchange(outer_send, outer_recv, OUTER_ROWS, outer_sems)

    shrink = damped(8 * me + row8)
    pltpu.make_async_copy(inner_recv, inner_recv, inner_sems.at[1]).wait()
    nothing = jnp.zeros((8, LANES), F32)
    builders = [Builder(lane) for _ in range(4)]
    for v in range(4):
        builders[v].tiles = {t: nothing for t in range(state_tiles)}
    for s in range(span):
        top = INNER_ROWS * s

        def inner(t, top=top):
            if t == 0:
                return inner_recv[top : top + 8, :]
            return unfold(rows_of(inner_recv, top + 8)[1], 64)

        tiles = [inner(0), inner(1)]
        for v in range(4):
            for e, (a, b) in enumerate(INNER):
                builders[v].add((s, e), lambda t, x=tiles: x[t], 48 * v + 24 * e, PAIR * s + a, 24)
    for v in range(4):
        for t in range(state_tiles):
            cut = slice(t * LANES, (t + 1) * LANES)
            settled[v, :, cut] = state[v, :, cut] * shrink + builders[v].tiles[t]
    put = pltpu.make_async_copy(settled, result, result_sem)
    put.start()
    pltpu.make_async_copy(outer_recv, outer_recv, outer_sems.at[1]).wait()
    put.wait()

    for send, rows, sems in (
        (send_a, 8, a_sems), (send_b, 8, b_sems), (send_c, OUTER_ROWS, c_sems),
        (inner_send, INNER_ROWS, inner_sems), (outer_send, OUTER_ROWS, outer_sems),
    ):
        sent = send.at[0 : rows * (span - 1), :]
        pltpu.make_async_copy(sent, sent, sems.at[0]).wait()


def finish(span, base, outer, out, base_v, outer_v, out_v, load_sems, store_sems):
    loads = [
        pltpu.make_async_copy(a, b, load_sems.at[i])
        for i, (a, b) in enumerate(((outer, outer_v), (base, base_v)))
    ]
    for load in loads:
        load.start()
    loads[0].wait()
    lane = tile_indices()[1]
    tiles = [unfold_96(rows_of(outer_v, OUTER_ROWS * s)[1]) for s in range(span)]
    loads[1].wait()
    stores = []
    for v in range(4):
        b = Builder(lane)
        for t in range(base.shape[2] // LANES):
            b.tiles[t] = jnp.zeros((8, LANES), F32)
        for s in range(span):
            for src, dst, length in ((0, 0, 6), (6, 30, 12), (18, 66, 6)):
                b.add((s, src), lambda t, x=tiles[s]: x, 24 * v + src, PAIR * s + dst, length)
        for t in range(base.shape[2] // LANES):
            cut = slice(t * LANES, (t + 1) * LANES)
            out_v[v, :, cut] = base_v[v, :, cut] + b.tiles[t]
        store = pltpu.make_async_copy(out_v.at[v], out.at[v], store_sems.at[v])
        store.start()
        stores.append(store)
    for store in stores:
        store.wait()


def body(groups, span, state, metric, neighbour, orient, wall, rim):
    elems = metric.shape[1]
    modes = span * 8
    tables, marks = node_tables()
    spread, rim_spread, lane_marks = lookup_tables(elems, rim.shape[1])
    both_high, both_low = basis_tables(modes)
    given = [
        state, rim, rim_spread, lane_marks, neighbour.T, orient.T, wall.T, spread,
        metric, tables, marks, both_high, both_low,
    ]
    given = [jnp.asarray(x) for x in given]
    gathered = elems // 2 * 32 // LANES
    scratch = [pltpu.VMEM(x.shape, x.dtype) for x in given] + [
        pltpu.VMEM((2, gathered, 8, LANES), jnp.int32),
        pltpu.VMEM((2, gathered, 8, LANES), F32),
        pltpu.VMEM((2, 4, gathered, 8, LANES), F32),
        pltpu.VMEM((2, 4, 8, LANES), F32),
        pltpu.VMEM((2, 4, 8, LANES), F32),
        pltpu.VMEM((modes, 256), F32),
        pltpu.VMEM((modes, LANES), F32),
        pltpu.VMEM((OUTER_ROWS * span, LANES), F32),
        pltpu.VMEM((modes, 256), F32),
        pltpu.VMEM((modes, LANES), F32),
        pltpu.VMEM((OUTER_ROWS * span, LANES), F32),
        pltpu.VMEM((modes, LANES), F32),
        pltpu.VMEM((4, 144, modes), F32),
        pltpu.VMEM((288, 2 * modes), F32),
        pltpu.VMEM((modes, 256), F32),
        pltpu.VMEM((modes, LANES), F32),
        pltpu.VMEM((INNER_ROWS * span, LANES), F32),
        pltpu.VMEM((OUTER_ROWS * span, LANES), F32),
        pltpu.VMEM((INNER_ROWS * span, LANES), F32),
        pltpu.VMEM(state.shape, F32),
        pltpu.SemaphoreType.DMA((len(given),)),
        pltpu.SemaphoreType.DMA((4,)),
        pltpu.SemaphoreType.DMA((2,)),
        pltpu.SemaphoreType.DMA((2,)),
        pltpu.SemaphoreType.DMA((2,)),
        pltpu.SemaphoreType.DMA((2,)),
        pltpu.SemaphoreType.DMA((2,)),
        pltpu.SemaphoreType.DMA,
        pltpu.SemaphoreType.REGULAR,
    ]
    hbm = pl.BlockSpec(memory_space=pltpu.HBM)
    outer = jax.ShapeDtypeStruct((OUTER_ROWS * span, LANES), F32)
    whole = jax.ShapeDtypeStruct(state.shape, F32)
    base, outer_rows = pl.pallas_call(
        functools.partial(kernel, groups, span),
        out_shape=(whole, outer),
        in_specs=[hbm] * len(given),
        out_specs=(hbm, hbm),
        scratch_shapes=scratch,
        compiler_params=pltpu.CompilerParams(
            collective_id=0, has_side_effects=True, vmem_limit_bytes=60 << 20
        ),
        name="section",
    )(*given)
    return pl.pallas_call(
        functools.partial(finish, span),
        out_shape=whole,
        in_specs=[hbm, hbm],
        out_specs=hbm,
        scratch_shapes=[
            pltpu.VMEM(whole.shape, F32), pltpu.VMEM(outer.shape, F32), pltpu.VMEM(whole.shape, F32),
            pltpu.SemaphoreType.DMA((2,)), pltpu.SemaphoreType.DMA((4,)),
        ],
        compiler_params=pltpu.CompilerParams(vmem_limit_bytes=60 << 20),
        name="finish",
    )(base, outer_rows)


def solution(mesh):
    specs = (
        P(None, "span", "elem"), P(None, "elem"), P("elem", None),
        P("elem", None), P("elem", None), P(None, "elem"),
    )
    return jax.shard_map(
        functools.partial(body, mesh.shape["elem"], mesh.shape["span"]),
        mesh=mesh, in_specs=specs, out_specs=P(None, "span", "elem"), check_vma=False,
    )
```

```python
import functools
import math

import jax
import jax.numpy as jnp
import numpy as np
from jax import lax
from jax.experimental import pallas as pl
from jax.experimental.pallas import tpu as pltpu
from jax.sharding import PartitionSpec as P

TIME_STEP = 0.001
VISCOSITY = 0.02
MESH = pl.DeviceIdType.MESH
F32 = jnp.float32
BF16 = jnp.bfloat16
NODES = 36
PAIR = 72
LANES = 128
INNER = ((6, 30), (42, 66))
OUTER = ((0, 6), (30, 36), (36, 42), (66, 72))


def differentiation():
    near = math.sqrt(1.0 / 3.0 - 2.0 * math.sqrt(7.0) / 21.0)
    far = math.sqrt(1.0 / 3.0 + 2.0 * math.sqrt(7.0) / 21.0)
    points = np.array([-1.0, -far, -near, near, far, 1.0])
    weights = np.array(
        [1.0 / np.prod([points[c] - points[s] for s in range(6) if s != c]) for c in range(6)]
    )
    deriv = np.zeros((6, 6))
    for t in range(6):
        for s in range(6):
            if s != t:
                deriv[t, s] = weights[s] / weights[t] / (points[t] - points[s])
        deriv[t, t] = -np.sum(deriv[t])
    return deriv


def split_np(x):
    high = x.astype(jnp.bfloat16)
    low = (x - high.astype(np.float64)).astype(jnp.bfloat16)
    return high, low


def basis_tables(count):
    m = np.arange(count)[:, None]
    n = np.arange(count)[None, :]
    angle = (m // 2 * n % count) * (2.0 * math.pi / count)
    basis = np.where(m % 2 == 1, np.sin(angle), np.cos(angle)) * math.sqrt(2.0 / count)
    basis[0] = 1.0 / math.sqrt(count)
    basis[1] = (1.0 - 2.0 * (np.arange(count) % 2)) / math.sqrt(count)
    minus = np.zeros_like(basis)
    k = np.arange(count // 2)[:, None]
    minus[0::2] = -k * basis[1::2]
    minus[1::2] = k * basis[0::2]
    both = np.concatenate([basis, minus], axis=1)
    return split_np(both)


def node_tables():
    deriv = differentiation()
    ident = np.eye(6)
    two = np.eye(2)
    along_x = np.zeros((PAIR, 168))
    along_y = np.zeros((PAIR, 168))
    lift = np.zeros((PAIR, 168))
    order = np.concatenate([np.arange(a, b) for a, b in INNER + OUTER])
    along_x[:, 0:72] = -np.kron(two, np.kron(deriv, ident))[order][:, order]
    along_y[:, 72:144] = -np.kron(two, np.kron(ident, deriv))[order][:, order]
    for e in range(2):
        for s2 in range(2):
            for j in range(6):
                lift[e * 36 + 6 * j + 5 * s2, 144 + e * 12 + s2 * 6 + j] = 1.0
    lift = lift[order]
    tables = np.stack([along_x, along_y, lift]).astype(np.float32)
    marks = np.zeros((PAIR, 8), np.float32)
    p = order % 36
    marks[:, 0] = 1.0 * (p // 6 == 5) - 1.0 * (p // 6 == 0)
    marks[:, 1] = 1.0 * (p % 6 == 5) - 1.0 * (p % 6 == 0)
    marks[:, 2] = np.abs(marks[:, 0])
    marks[:, 3] = np.abs(marks[:, 1])
    marks[:, 4] = order >= 36
    return tables, marks


def lookup_tables(elems, rows):
    spread = np.zeros((elems, elems // 2 * 32))
    marks = np.zeros((8, elems // 2 * 32), np.float32)
    lane = np.arange(elems // 2 * 32)
    r = lane % 32
    used = r < 24
    e = 2 * (lane // 32) + r % 24 // 12
    spread[e[used], lane[used]] = 1.0
    marks[0] = np.where(used, r % 6, 0)
    marks[1] = np.where(used, r // 6 % 2, 0)
    marks[3] = used
    rim_spread = np.zeros((rows, LANES))
    rim_lane = np.arange(6 * rows)
    rim_spread[rim_lane // 6, rim_lane] = 1.0
    marks[2, : 6 * rows] = rim_lane % 6
    return spread.astype(jnp.bfloat16), rim_spread.astype(jnp.bfloat16), marks


def split(x):
    high = x.astype(BF16)
    low = (x - high.astype(F32)).astype(BF16)
    return high, low


def dot3(a, b, dims):
    go = lambda x, y: lax.dot_general(x, y, (dims, ((), ())), preferred_element_type=F32)
    return go(a[0], b[0]) + (go(a[0], b[1]) + go(a[1], b[0]))


def pieces(src, dst, length):
    out = []
    done = 0
    while done < length:
        s, d = src + done, dst + done
        size = min(length - done, LANES - s % LANES, LANES - d % LANES)
        out.append((s // LANES, d // LANES, (d - s) % LANES, d % LANES, d % LANES + size))
        done += size
    return out


class Builder:
    def __init__(self, lane):
        self.lane = lane
        self.tiles = {}
        self.turned = {}

    def add(self, key, load, src, dst, length):
        for st, dt, shift, lo, hi in pieces(src, dst, length):
            name = (key, st, shift)
            if name not in self.turned:
                tile = load(st)
                self.turned[name] = pltpu.roll(tile, shift, 1) if shift else tile
            value = self.turned[name]
            if dt in self.tiles:
                value = jnp.where((self.lane >= lo) & (self.lane < hi), value, self.tiles[dt])
            self.tiles[dt] = value


def picked(tile, at):
    return jnp.take_along_axis(tile, at, axis=1, mode="promise_in_bounds")


def tile_indices():
    return tuple(lax.broadcasted_iota(jnp.int32, (8, LANES), dim) for dim in range(2))


def fold(tile, start, width, store):
    row8, lane = tile_indices()
    every = LANES // width
    tile = picked(tile, start + (lane & (width - 1)))
    tile = jnp.where(lane // width == (row8 & (every - 1)), tile, 0.0)
    for a in range(8 // every):
        store(a, jnp.sum(tile[every * a : every * (a + 1)], axis=0, keepdims=True))


def unfold(load, width):
    row8, lane = tile_indices()
    every = LANES // width
    tile = load(0)
    for a in range(1, 8 // every):
        tile = jnp.where(row8 < every * a, tile, load(a))
    return picked(jnp.broadcast_to(tile, (8, LANES)), (lane & (width - 1)) + width * (row8 & (every - 1)))


def fold_96(tile, store):
    fold(tile, 0, 64, store)
    fold(tile, 64, 32, lambda a, row: store(4 + a, row))


def unfold_96(load):
    lane = tile_indices()[1]
    return jnp.where(lane < 64, unfold(load, 64), unfold(lambda a: load(4 + a), 32))


def rows_of(ref, top):
    def store(a, row):
        ref[top + a : top + a + 1, :] = row

    return store, lambda a: ref[top + a : top + a + 1, :]


INNER_ROWS = 12
OUTER_ROWS = 6


def kernel(groups, span, *refs):
    given, refs = refs[:13], refs[13:]
    (result, outer_recv), refs = refs[:2], refs[2:]
    held, refs = refs[:13], refs[13:]
    (
        index, flip, others, rim_send, rim_recv, send_a, send_b, send_c, recv_a, recv_b, recv_c,
        modal_c, fields, rows_r, inner_sum, outer_sum, inner_send, outer_send, inner_recv, settled,
        load_sems, rim_sems, a_sems, b_sems, c_sems, inner_sems, outer_sems, result_sem, hello,
    ) = refs
    (
        state, rim, rim_spread, lane_marks, neighbour, orient, wall, spread,
        metric, node_tab, node_marks, both_high, both_low,
    ) = held
    me = lax.axis_index("span")
    group = lax.axis_index("elem")
    lower = lax.rem(group + groups - 1, groups)
    upper = lax.rem(group + 1, groups)
    elems = metric.shape[1]
    modes = span * 8
    state_tiles = elems * NODES // LANES

    loads = [pltpu.make_async_copy(a, b, load_sems.at[i]) for i, (a, b) in enumerate(zip(given, held))]
    for load in loads[:4]:
        load.start()

    barrier = pltpu.get_barrier_semaphore()

    def greet(k, carry):
        pl.semaphore_signal(
            barrier, 1, device_id=(group, lax.rem(me + k, span)), device_id_type=MESH
        )
        return carry

    pl.semaphore_signal(barrier, 1, device_id=(lower, me), device_id_type=MESH)
    lax.fori_loop(1, span, greet, 0)
    for load in loads[4:]:
        load.start()

    lane = lax.broadcasted_iota(jnp.int32, (8, LANES), 1)
    row8 = lax.broadcasted_iota(jnp.int32, (8, LANES), 0)

    def bases(slot):
        side = slot & 3
        vertical = side >= 2
        step = jnp.where(vertical, 6, 1)
        first = jnp.where(vertical, jnp.where(side == 3, 5, 0), jnp.where(side == 1, 30, 0))
        return NODES * (slot >> 2) + first, step

    def spread_over(values, matrix):
        high = (values >> 6).astype(F32).astype(BF16)
        low = (values & 63).astype(F32).astype(BF16)
        go = lambda x: jnp.dot(x, matrix, preferred_element_type=F32)
        return (go(high) * 64.0 + go(low)).astype(jnp.int32)

    def gather(at, start, tiles):
        low = at & (LANES - 1)
        high = at >> 7
        totals = list(start)
        for k in tiles:
            here = high == k
            for v in range(4):
                tile = (
                    state[v, :, k * LANES : (k + 1) * LANES]
                    if k < state_tiles
                    else rim_recv[k - state_tiles, v]
                )
                totals[v] = jnp.where(here, picked(tile, low), totals[v])
        return totals

    for load in loads[1:4]:
        load.wait()
    rim_base, rim_step = bases(rim[...])
    node_r = lane_marks[2:3, 0:LANES].astype(jnp.int32)
    rim_index = spread_over(rim_base, rim_spread[...]) + node_r * spread_over(
        rim_step, rim_spread[...]
    )
    loads[0].wait()
    zero = [jnp.zeros((8, LANES), F32)] * 4
    for way in range(2):
        at = jnp.broadcast_to(rim_index[way : way + 1], (8, LANES))
        got = gather(at, zero, range(state_tiles))
        for v in range(4):
            rim_send[way, v] = got[v]

    def rim_copy(way, to):
        return pltpu.make_async_remote_copy(
            rim_send.at[way], rim_recv.at[1 - way], rim_sems.at[way], rim_sems.at[3 - way],
            device_id=(to, me), device_id_type=MESH,
        )

    rim_up, rim_down = rim_copy(1, upper), rim_copy(0, lower)
    for d in range(span):
        b = Builder(lane)
        for v in range(4):
            b.add(v, lambda k, v=v: state[v, :, k * LANES : (k + 1) * LANES], PAIR * d, PAIR * v, PAIR)
        rows = slice(8 * d, 8 * d + 8)
        send_a[rows, 0:LANES] = b.tiles[0]
        send_a[rows, LANES:] = b.tiles[1]
        send_b[rows, :] = b.tiles[2]

    pl.semaphore_wait(barrier, span)
    pl.semaphore_signal(hello, 1, device_id=(upper, me), device_id_type=MESH)
    rim_up.start()

    def exchange(send, recv, rows, sems):
        arrived = sems.at[1]
        at = lambda who: pl.ds(pl.multiple_of(rows * who, 8) if rows == 8 else rows * who, rows)

        def one(k, carry):
            to = lax.rem(me + k, span)
            pltpu.make_async_remote_copy(
                send.at[at(to), :], recv.at[at(me), :], sems.at[0], arrived,
                device_id=(group, to), device_id_type=MESH,
            ).start()
            return carry

        lax.fori_loop(1, span, one, 0)
        pltpu.make_async_copy(send.at[at(me), :], recv.at[at(me), :], arrived).start()

    exchange(send_a, recv_a, 8, a_sems)

    @pl.when(group > 0)
    def _():
        pl.semaphore_wait(hello, 1)
        rim_down.start()


    for load in loads[4:8]:
        load.wait()
    slot = neighbour[...]
    turn = orient[...]
    remote = slot >= 4 * elems
    base, step = bases(slot)
    row = slot - 4 * elems
    base = jnp.where(remote, state_tiles * LANES + LANES * (row >> 4) + 6 * (row & 15), base)
    step = jnp.where(remote, 1, step)
    base = jnp.where(turn == 1, base + 5 * step, base)
    step = jnp.where(turn == 1, -step, step)
    matrix = spread[...]
    base_l = spread_over(base, matrix)
    step_l = spread_over(step + 8, matrix) - 8
    wall_l = spread_over(wall[...], matrix)
    node_l = lane_marks[0:1, :].astype(jnp.int32)
    second = lane_marks[1:2, :] > 0.5
    used = lane_marks[3:4, :] > 0.5
    for axis in range(2):
        pick = lambda x: jnp.where(second, x[2 * axis + 1 : 2 * axis + 2], x[2 * axis : 2 * axis + 1])
        lanes_at = jnp.where(used, pick(base_l) + pick(step_l) * node_l, 0)
        walls = 1.0 - 2.0 * pick(wall_l).astype(F32)
        for t in range(index.shape[1]):
            cut = slice(t * LANES, (t + 1) * LANES)
            index[axis, t] = jnp.broadcast_to(lanes_at[:, cut], (8, LANES))
            flip[axis, t] = jnp.broadcast_to(walls[:, cut], (8, LANES))

    def gather_axis(axis, tiles, first):
        def one(t, carry):
            at = index[axis, t]
            start = zero if first else [others[axis, v, t] for v in range(4)]
            got = gather(at, start, tiles)
            for v in range(4):
                others[axis, v, t] = got[v]
            return carry

        lax.fori_loop(0, index.shape[1], one, 0)

    def reflected(axis, v, t):
        tile = others[axis, v, t]
        return tile * flip[axis, t] if v < 3 else tile

    gather_axis(1, range(state_tiles), True)
    for d in range(span):
        b = Builder(lane)
        b.tiles[0] = send_b[8 * d : 8 * d + 8, :]
        for v in range(4):
            b.add(v, lambda k, v=v: reflected(1, v, k), 32 * d, 32 + 24 * v, 24)
        send_b[8 * d : 8 * d + 8, :] = b.tiles[0]
    exchange(send_b, recv_b, 8, b_sems)
    gather_axis(0, range(state_tiles), True)

    @pl.when(group == 0)
    def _():
        pl.semaphore_wait(hello, 1)
        rim_down.start()

    rim_up.wait()
    rim_down.wait()
    gather_axis(0, range(state_tiles, state_tiles + 2), False)

    for d in range(span):
        b = Builder(lane)
        for v in range(4):
            b.add(v, lambda k, v=v: reflected(0, v, k), 32 * d, 24 * v, 24)
        fold_96(b.tiles[0], rows_of(send_c, OUTER_ROWS * d)[0])
    exchange(send_c, recv_c, OUTER_ROWS, c_sems)

    for load in loads[8:]:
        load.wait()
    at = lax.broadcasted_iota(jnp.int32, (2, elems), 1)
    scale = metric[...]
    first = jnp.sum(jnp.where(at == 2 * me, scale, 0.0), axis=1, keepdims=True)
    last = jnp.sum(jnp.where(at == 2 * me + 1, scale, 0.0), axis=1, keepdims=True)

    def per_row(on_first, which):
        return jnp.where(on_first, first[which : which + 1], last[which : which + 1])

    marks = node_marks[...]
    on_first = marks[:, 4:5] < 0.5
    rx, ry = per_row(on_first, 0), per_row(on_first, 1)
    coef_u = 7.5 * rx * marks[:, 0:1]
    coef_v = 7.5 * ry * marks[:, 1:2]
    coef_c = 7.5 * (jnp.abs(rx) * marks[:, 2:3] + jnp.abs(ry) * marks[:, 3:4])
    operator = split(rx * node_tab[0, :, 0:144] + ry * node_tab[1, :, 0:144])
    lift_y = node_tab[2, :, 144:168].astype(BF16)
    over1_0 = ((1,), (0,))
    side = lax.broadcasted_iota(jnp.int32, (24, 1), 0)
    low_side = (side < 6) | ((side >= 12) & (side < 18))
    toward = jnp.where(low_side, 7.5, -7.5)
    ox, oy = per_row(side < 12, 0), per_row(side < 12, 1)

    over0, over1 = ((0,), (0,)), ((1,), (1,))
    basis = (both_high[:, 0:modes], both_low[:, 0:modes])
    pltpu.make_async_copy(recv_a, recv_a, a_sems.at[1]).wait()
    planes_a = dot3(split(recv_a[...]), basis, over0)
    reorder = lambda x: jnp.concatenate([x[a:b] for a, b in INNER + OUTER], axis=0)
    own = [reorder(planes_a[PAIR * v : PAIR * (v + 1)]) for v in range(3)]
    own_coef = coef_u * own[0] + coef_v * own[1] - coef_c

    def own_terms(v):
        fields[v, 0:72] = own[0] * own[v]
        fields[v, 72:144] = own[1] * own[v]
        planar = own_coef * own[v] + dot3(operator, split(fields[v]), over1_0)
        for part, at in ((planar, slice(0, modes)), (own[2] * own[v], slice(modes, 2 * modes))):
            rows_r[48 * v : 48 * v + 48, at] = part[0:48]
            rows_r[192 + 24 * v : 216 + 24 * v, at] = part[48:72]

    for v in range(3):
        own_terms(v)
    pltpu.make_async_copy(recv_b, recv_b, b_sems.at[1]).wait()
    planes_b = dot3(split(recv_b[...]), basis, over0)
    own.append(reorder(jnp.concatenate([planes_a[3 * PAIR :], planes_b[0:32]], axis=0)))
    facing_y_coef = (toward * oy) * planes_b[56:80] + 7.5 * jnp.abs(oy)
    facing_y = [split(facing_y_coef * planes_b[32 + 24 * v : 56 + 24 * v]) for v in range(4)]
    own_terms(3)
    for v in range(4):
        lifted = sum(jnp.dot(lift_y, part, preferred_element_type=F32) for part in facing_y[v])
        rows_r[48 * v : 48 * v + 48, 0:modes] += lifted[0:48]
        rows_r[192 + 24 * v : 216 + 24 * v, 0:modes] += lifted[48:72]
    both = (both_high[...], both_low[...])

    def damped(mode):
        k = jnp.where(mode == 1, modes // 2, mode >> 1).astype(F32)
        return 1.0 / (1.0 + TIME_STEP * VISCOSITY * k * k)

    step_of = TIME_STEP * damped(lax.broadcasted_iota(jnp.int32, (modes, 1), 0))

    inner_sum[:, 0:192] = step_of * dot3(both, split(rows_r[0:192, :]), over1)
    for d in range(span):
        mine = inner_sum[8 * d : 8 * d + 8, :]
        top = INNER_ROWS * d
        inner_send[top : top + 8, :] = mine[:, 0:LANES]
        fold(mine[:, LANES:], 0, 64, rows_of(inner_send, top + 8)[0])
    exchange(inner_send, inner_recv, INNER_ROWS, inner_sems)
    outer_sum[:, 0:96] = dot3(both, split(rows_r[192:288, :]), over1)

    pltpu.make_async_copy(recv_c, recv_c, c_sems.at[1]).wait()
    for s in range(span):
        modal_c[8 * s : 8 * s + 8, :] = unfold_96(rows_of(recv_c, OUTER_ROWS * s)[1])
    planes_c = dot3(split(modal_c[:, 0:96]), basis, over0)
    facing_x_coef = (toward * ox) * planes_c[0:24] + 7.5 * jnp.abs(ox)
    jump = split(jnp.concatenate([facing_x_coef] * 4, axis=0) * planes_c)
    outer_sum[:, 0:96] = step_of * (outer_sum[:, 0:96] + dot3(basis, jump, over1))
    for d in range(span):
        fold_96(outer_sum[8 * d : 8 * d + 8, :], rows_of(outer_send, OUTER_ROWS * d)[0])
    exchange(outer_send, outer_recv, OUTER_ROWS, outer_sems)

    shrink = damped(8 * me + row8)
    pltpu.make_async_copy(inner_recv, inner_recv, inner_sems.at[1]).wait()
    nothing = jnp.zeros((8, LANES), F32)
    builders = [Builder(lane) for _ in range(4)]
    for v in range(4):
        builders[v].tiles = {t: nothing for t in range(state_tiles)}
    for s in range(span):
        top = INNER_ROWS * s

        def inner(t, top=top):
            if t == 0:
                return inner_recv[top : top + 8, :]
            return unfold(rows_of(inner_recv, top + 8)[1], 64)

        tiles = [inner(0), inner(1)]
        for v in range(4):
            for e, (a, b) in enumerate(INNER):
                builders[v].add((s, e), lambda t, x=tiles: x[t], 48 * v + 24 * e, PAIR * s + a, 24)
    for v in range(4):
        for t in range(state_tiles):
            cut = slice(t * LANES, (t + 1) * LANES)
            settled[v, :, cut] = state[v, :, cut] * shrink + builders[v].tiles[t]
    put = pltpu.make_async_copy(settled, result, result_sem)
    put.start()
    pltpu.make_async_copy(outer_recv, outer_recv, outer_sems.at[1]).wait()
    put.wait()

    for send, rows, sems in (
        (send_a, 8, a_sems), (send_b, 8, b_sems), (send_c, OUTER_ROWS, c_sems),
        (inner_send, INNER_ROWS, inner_sems), (outer_send, OUTER_ROWS, outer_sems),
    ):
        sent = send.at[0 : rows * (span - 1), :]
        pltpu.make_async_copy(sent, sent, sems.at[0]).wait()


def finish(span, base, outer, out, base_v, outer_v, out_v, load_sems, store_sems):
    loads = [
        pltpu.make_async_copy(a, b, load_sems.at[i])
        for i, (a, b) in enumerate([(outer, outer_v)] + [(base.at[v], base_v.at[v]) for v in range(4)])
    ]
    for load in loads:
        load.start()
    loads[0].wait()
    lane = tile_indices()[1]
    tiles = [unfold_96(rows_of(outer_v, OUTER_ROWS * s)[1]) for s in range(span)]
    stores = []
    for v in range(4):
        b = Builder(lane)
        for t in range(base.shape[2] // LANES):
            b.tiles[t] = jnp.zeros((8, LANES), F32)
        for s in range(span):
            for src, dst, length in ((0, 0, 6), (6, 30, 12), (18, 66, 6)):
                b.add((s, src), lambda t, x=tiles[s]: x, 24 * v + src, PAIR * s + dst, length)
        loads[1 + v].wait()
        for t in range(base.shape[2] // LANES):
            cut = slice(t * LANES, (t + 1) * LANES)
            out_v[v, :, cut] = base_v[v, :, cut] + b.tiles[t]
        store = pltpu.make_async_copy(out_v.at[v], out.at[v], store_sems.at[v])
        store.start()
        stores.append(store)
    for store in stores:
        store.wait()


def body(groups, span, state, metric, neighbour, orient, wall, rim):
    elems = metric.shape[1]
    modes = span * 8
    tables, marks = node_tables()
    spread, rim_spread, lane_marks = lookup_tables(elems, rim.shape[1])
    both_high, both_low = basis_tables(modes)
    given = [
        state, rim, rim_spread, lane_marks, neighbour.T, orient.T, wall.T, spread,
        metric, tables, marks, both_high, both_low,
    ]
    given = [jnp.asarray(x) for x in given]
    gathered = elems // 2 * 32 // LANES
    scratch = [pltpu.VMEM(x.shape, x.dtype) for x in given] + [
        pltpu.VMEM((2, gathered, 8, LANES), jnp.int32),
        pltpu.VMEM((2, gathered, 8, LANES), F32),
        pltpu.VMEM((2, 4, gathered, 8, LANES), F32),
        pltpu.VMEM((2, 4, 8, LANES), F32),
        pltpu.VMEM((2, 4, 8, LANES), F32),
        pltpu.VMEM((modes, 256), F32),
        pltpu.VMEM((modes, LANES), F32),
        pltpu.VMEM((OUTER_ROWS * span, LANES), F32),
        pltpu.VMEM((modes, 256), F32),
        pltpu.VMEM((modes, LANES), F32),
        pltpu.VMEM((OUTER_ROWS * span, LANES), F32),
        pltpu.VMEM((modes, LANES), F32),
        pltpu.VMEM((4, 144, modes), F32),
        pltpu.VMEM((288, 2 * modes), F32),
        pltpu.VMEM((modes, 256), F32),
        pltpu.VMEM((modes, LANES), F32),
        pltpu.VMEM((INNER_ROWS * span, LANES), F32),
        pltpu.VMEM((OUTER_ROWS * span, LANES), F32),
        pltpu.VMEM((INNER_ROWS * span, LANES), F32),
        pltpu.VMEM(state.shape, F32),
        pltpu.SemaphoreType.DMA((len(given),)),
        pltpu.SemaphoreType.DMA((4,)),
        pltpu.SemaphoreType.DMA((2,)),
        pltpu.SemaphoreType.DMA((2,)),
        pltpu.SemaphoreType.DMA((2,)),
        pltpu.SemaphoreType.DMA((2,)),
        pltpu.SemaphoreType.DMA((2,)),
        pltpu.SemaphoreType.DMA,
        pltpu.SemaphoreType.REGULAR,
    ]
    hbm = pl.BlockSpec(memory_space=pltpu.HBM)
    outer = jax.ShapeDtypeStruct((OUTER_ROWS * span, LANES), F32)
    whole = jax.ShapeDtypeStruct(state.shape, F32)
    base, outer_rows = pl.pallas_call(
        functools.partial(kernel, groups, span),
        out_shape=(whole, outer),
        in_specs=[hbm] * len(given),
        out_specs=(hbm, hbm),
        scratch_shapes=scratch,
        compiler_params=pltpu.CompilerParams(
            collective_id=0, has_side_effects=True, vmem_limit_bytes=60 << 20
        ),
        name="section",
    )(*given)
    return pl.pallas_call(
        functools.partial(finish, span),
        out_shape=whole,
        in_specs=[hbm, hbm],
        out_specs=hbm,
        scratch_shapes=[
            pltpu.VMEM(whole.shape, F32), pltpu.VMEM(outer.shape, F32), pltpu.VMEM(whole.shape, F32),
            pltpu.SemaphoreType.DMA((5,)), pltpu.SemaphoreType.DMA((4,)),
        ],
        compiler_params=pltpu.CompilerParams(vmem_limit_bytes=60 << 20),
        name="finish",
    )(base, outer_rows)


def solution(mesh):
    specs = (
        P(None, "span", "elem"), P(None, "elem"), P("elem", None),
        P("elem", None), P("elem", None), P(None, "elem"),
    )
    return jax.shard_map(
        functools.partial(body, mesh.shape["elem"], mesh.shape["span"]),
        mesh=mesh, in_specs=specs, out_specs=P(None, "span", "elem"), check_vma=False,
    )
```

```python
import functools
import math

import jax
import jax.numpy as jnp
import numpy as np
from jax import lax
from jax.experimental import pallas as pl
from jax.experimental.pallas import tpu as pltpu
from jax.sharding import PartitionSpec as P

TIME_STEP = 0.001
VISCOSITY = 0.02
MESH = pl.DeviceIdType.MESH
F32 = jnp.float32
BF16 = jnp.bfloat16
NODES = 36
PAIR = 72
LANES = 128
INNER = ((6, 30), (42, 66))
OUTER = ((0, 6), (30, 36), (36, 42), (66, 72))


def differentiation():
    near = math.sqrt(1.0 / 3.0 - 2.0 * math.sqrt(7.0) / 21.0)
    far = math.sqrt(1.0 / 3.0 + 2.0 * math.sqrt(7.0) / 21.0)
    points = np.array([-1.0, -far, -near, near, far, 1.0])
    weights = np.array(
        [1.0 / np.prod([points[c] - points[s] for s in range(6) if s != c]) for c in range(6)]
    )
    deriv = np.zeros((6, 6))
    for t in range(6):
        for s in range(6):
            if s != t:
                deriv[t, s] = weights[s] / weights[t] / (points[t] - points[s])
        deriv[t, t] = -np.sum(deriv[t])
    return deriv


def split_np(x):
    high = x.astype(jnp.bfloat16)
    low = (x - high.astype(np.float64)).astype(jnp.bfloat16)
    return high, low


def basis_tables(count):
    m = np.arange(count)[:, None]
    n = np.arange(count)[None, :]
    angle = (m // 2 * n % count) * (2.0 * math.pi / count)
    basis = np.where(m % 2 == 1, np.sin(angle), np.cos(angle)) * math.sqrt(2.0 / count)
    basis[0] = 1.0 / math.sqrt(count)
    basis[1] = (1.0 - 2.0 * (np.arange(count) % 2)) / math.sqrt(count)
    minus = np.zeros_like(basis)
    k = np.arange(count // 2)[:, None]
    minus[0::2] = -k * basis[1::2]
    minus[1::2] = k * basis[0::2]
    both = np.concatenate([basis, minus], axis=1)
    return split_np(both)


def node_tables():
    deriv = differentiation()
    ident = np.eye(6)
    two = np.eye(2)
    along_x = np.zeros((PAIR, 168))
    along_y = np.zeros((PAIR, 168))
    lift = np.zeros((PAIR, 168))
    order = np.concatenate([np.arange(a, b) for a, b in INNER + OUTER])
    along_x[:, 0:72] = -np.kron(two, np.kron(deriv, ident))[order][:, order]
    along_y[:, 72:144] = -np.kron(two, np.kron(ident, deriv))[order][:, order]
    for e in range(2):
        for s2 in range(2):
            for j in range(6):
                lift[e * 36 + 6 * j + 5 * s2, 144 + e * 12 + s2 * 6 + j] = 1.0
    lift = lift[order]
    tables = np.stack([along_x, along_y, lift]).astype(np.float32)
    marks = np.zeros((PAIR, 8), np.float32)
    p = order % 36
    marks[:, 0] = 1.0 * (p // 6 == 5) - 1.0 * (p // 6 == 0)
    marks[:, 1] = 1.0 * (p % 6 == 5) - 1.0 * (p % 6 == 0)
    marks[:, 2] = np.abs(marks[:, 0])
    marks[:, 3] = np.abs(marks[:, 1])
    marks[:, 4] = order >= 36
    return tables, marks


def lookup_tables(elems, rows):
    spread = np.zeros((elems, elems // 2 * 32))
    marks = np.zeros((8, elems // 2 * 32), np.float32)
    lane = np.arange(elems // 2 * 32)
    r = lane % 32
    used = r < 24
    e = 2 * (lane // 32) + r % 24 // 12
    spread[e[used], lane[used]] = 1.0
    marks[0] = np.where(used, r % 6, 0)
    marks[1] = np.where(used, r // 6 % 2, 0)
    marks[3] = used
    rim_spread = np.zeros((rows, LANES))
    rim_lane = np.arange(6 * rows)
    rim_spread[rim_lane // 6, rim_lane] = 1.0
    marks[2, : 6 * rows] = rim_lane % 6
    return spread.astype(jnp.bfloat16), rim_spread.astype(jnp.bfloat16), marks


def split(x):
    high = x.astype(BF16)
    low = (x - high.astype(F32)).astype(BF16)
    return high, low


def dot3(a, b, dims):
    go = lambda x, y: lax.dot_general(x, y, (dims, ((), ())), preferred_element_type=F32)
    return go(a[0], b[0]) + (go(a[0], b[1]) + go(a[1], b[0]))


def pieces(src, dst, length):
    out = []
    done = 0
    while done < length:
        s, d = src + done, dst + done
        size = min(length - done, LANES - s % LANES, LANES - d % LANES)
        out.append((s // LANES, d // LANES, (d - s) % LANES, d % LANES, d % LANES + size))
        done += size
    return out


class Builder:
    def __init__(self, lane):
        self.lane = lane
        self.tiles = {}
        self.turned = {}

    def add(self, key, load, src, dst, length):
        for st, dt, shift, lo, hi in pieces(src, dst, length):
            name = (key, st, shift)
            if name not in self.turned:
                tile = load(st)
                self.turned[name] = pltpu.roll(tile, shift, 1) if shift else tile
            value = self.turned[name]
            if dt in self.tiles:
                value = jnp.where((self.lane >= lo) & (self.lane < hi), value, self.tiles[dt])
            self.tiles[dt] = value


def picked(tile, at):
    return jnp.take_along_axis(tile, at, axis=1, mode="promise_in_bounds")


def tile_indices():
    return tuple(lax.broadcasted_iota(jnp.int32, (8, LANES), dim) for dim in range(2))


def fold(tile, start, width, store):
    row8, lane = tile_indices()
    every = LANES // width
    tile = picked(tile, start + (lane & (width - 1)))
    tile = jnp.where(lane // width == (row8 & (every - 1)), tile, 0.0)
    for a in range(8 // every):
        store(a, jnp.sum(tile[every * a : every * (a + 1)], axis=0, keepdims=True))


def unfold(load, width):
    row8, lane = tile_indices()
    every = LANES // width
    tile = load(0)
    for a in range(1, 8 // every):
        tile = jnp.where(row8 < every * a, tile, load(a))
    return picked(jnp.broadcast_to(tile, (8, LANES)), (lane & (width - 1)) + width * (row8 & (every - 1)))


def fold_96(tile, store):
    fold(tile, 0, 64, store)
    fold(tile, 64, 32, lambda a, row: store(4 + a, row))


def unfold_96(load):
    lane = tile_indices()[1]
    return jnp.where(lane < 64, unfold(load, 64), unfold(lambda a: load(4 + a), 32))


def rows_of(ref, top):
    def store(a, row):
        ref[top + a : top + a + 1, :] = row

    return store, lambda a: ref[top + a : top + a + 1, :]


INNER_ROWS = 12
OUTER_ROWS = 6


def kernel(groups, span, *refs):
    given, refs = refs[:13], refs[13:]
    (result, outer_recv), refs = refs[:2], refs[2:]
    held, refs = refs[:13], refs[13:]
    (
        index, flip, others, rim_send, rim_recv, send_a, send_b, send_c, recv_a, recv_b, recv_c,
        modal_c, fields, rows_r, inner_sum, outer_sum, inner_send, outer_send, inner_recv, settled,
        load_sems, rim_sems, a_sems, b_sems, c_sems, inner_sems, outer_sems, result_sem, hello,
    ) = refs
    (
        state, rim, rim_spread, lane_marks, neighbour, orient, wall, spread,
        metric, node_tab, node_marks, both_high, both_low,
    ) = held
    me = lax.axis_index("span")
    group = lax.axis_index("elem")
    lower = lax.rem(group + groups - 1, groups)
    upper = lax.rem(group + 1, groups)
    elems = metric.shape[1]
    modes = span * 8
    state_tiles = elems * NODES // LANES

    loads = [pltpu.make_async_copy(a, b, load_sems.at[i]) for i, (a, b) in enumerate(zip(given, held))]
    barrier = pltpu.get_barrier_semaphore()

    def greet(k, carry):
        pl.semaphore_signal(
            barrier, 1, device_id=(group, lax.rem(me + k, span)), device_id_type=MESH
        )
        return carry

    pl.semaphore_signal(barrier, 1, device_id=(lower, me), device_id_type=MESH)
    lax.fori_loop(1, span, greet, 0)
    for load in loads:
        load.start()

    lane = lax.broadcasted_iota(jnp.int32, (8, LANES), 1)
    row8 = lax.broadcasted_iota(jnp.int32, (8, LANES), 0)

    def bases(slot):
        side = slot & 3
        vertical = side >= 2
        step = jnp.where(vertical, 6, 1)
        first = jnp.where(vertical, jnp.where(side == 3, 5, 0), jnp.where(side == 1, 30, 0))
        return NODES * (slot >> 2) + first, step

    def spread_over(values, matrix):
        high = (values >> 6).astype(F32).astype(BF16)
        low = (values & 63).astype(F32).astype(BF16)
        go = lambda x: jnp.dot(x, matrix, preferred_element_type=F32)
        return (go(high) * 64.0 + go(low)).astype(jnp.int32)

    def gather(at, start, tiles):
        low = at & (LANES - 1)
        high = at >> 7
        totals = list(start)
        for k in tiles:
            here = high == k
            for v in range(4):
                tile = (
                    state[v, :, k * LANES : (k + 1) * LANES]
                    if k < state_tiles
                    else rim_recv[k - state_tiles, v]
                )
                totals[v] = jnp.where(here, picked(tile, low), totals[v])
        return totals

    for load in loads[1:4]:
        load.wait()
    rim_base, rim_step = bases(rim[...])
    node_r = lane_marks[2:3, 0:LANES].astype(jnp.int32)
    rim_index = spread_over(rim_base, rim_spread[...]) + node_r * spread_over(
        rim_step, rim_spread[...]
    )
    loads[0].wait()
    zero = [jnp.zeros((8, LANES), F32)] * 4
    for way in range(2):
        at = jnp.broadcast_to(rim_index[way : way + 1], (8, LANES))
        got = gather(at, zero, range(state_tiles))
        for v in range(4):
            rim_send[way, v] = got[v]

    def rim_copy(way, to):
        return pltpu.make_async_remote_copy(
            rim_send.at[way], rim_recv.at[1 - way], rim_sems.at[way], rim_sems.at[3 - way],
            device_id=(to, me), device_id_type=MESH,
        )

    rim_up, rim_down = rim_copy(1, upper), rim_copy(0, lower)
    for d in range(span):
        b = Builder(lane)
        for v in range(4):
            b.add(v, lambda k, v=v: state[v, :, k * LANES : (k + 1) * LANES], PAIR * d, PAIR * v, PAIR)
        rows = slice(8 * d, 8 * d + 8)
        send_a[rows, 0:LANES] = b.tiles[0]
        send_a[rows, LANES:] = b.tiles[1]
        send_b[rows, :] = b.tiles[2]

    pl.semaphore_wait(barrier, span)
    pl.semaphore_signal(hello, 1, device_id=(upper, me), device_id_type=MESH)
    rim_up.start()

    def exchange(send, recv, rows, sems):
        arrived = sems.at[1]
        at = lambda who: pl.ds(pl.multiple_of(rows * who, 8) if rows == 8 else rows * who, rows)

        def one(k, carry):
            to = lax.rem(me + k, span)
            pltpu.make_async_remote_copy(
                send.at[at(to), :], recv.at[at(me), :], sems.at[0], arrived,
                device_id=(group, to), device_id_type=MESH,
            ).start()
            return carry

        lax.fori_loop(1, span, one, 0)
        pltpu.make_async_copy(send.at[at(me), :], recv.at[at(me), :], arrived).start()

    exchange(send_a, recv_a, 8, a_sems)

    @pl.when(group > 0)
    def _():
        pl.semaphore_wait(hello, 1)
        rim_down.start()


    for load in loads[4:8]:
        load.wait()
    slot = neighbour[...]
    turn = orient[...]
    remote = slot >= 4 * elems
    base, step = bases(slot)
    row = slot - 4 * elems
    base = jnp.where(remote, state_tiles * LANES + LANES * (row >> 4) + 6 * (row & 15), base)
    step = jnp.where(remote, 1, step)
    base = jnp.where(turn == 1, base + 5 * step, base)
    step = jnp.where(turn == 1, -step, step)
    matrix = spread[...]
    base_l = spread_over(base, matrix)
    step_l = spread_over(step + 8, matrix) - 8
    wall_l = spread_over(wall[...], matrix)
    node_l = lane_marks[0:1, :].astype(jnp.int32)
    second = lane_marks[1:2, :] > 0.5
    used = lane_marks[3:4, :] > 0.5
    for axis in range(2):
        pick = lambda x: jnp.where(second, x[2 * axis + 1 : 2 * axis + 2], x[2 * axis : 2 * axis + 1])
        lanes_at = jnp.where(used, pick(base_l) + pick(step_l) * node_l, 0)
        walls = 1.0 - 2.0 * pick(wall_l).astype(F32)
        for t in range(index.shape[1]):
            cut = slice(t * LANES, (t + 1) * LANES)
            index[axis, t] = jnp.broadcast_to(lanes_at[:, cut], (8, LANES))
            flip[axis, t] = jnp.broadcast_to(walls[:, cut], (8, LANES))

    def gather_axis(axis, tiles, first):
        def one(t, carry):
            at = index[axis, t]
            start = zero if first else [others[axis, v, t] for v in range(4)]
            got = gather(at, start, tiles)
            for v in range(4):
                others[axis, v, t] = got[v]
            return carry

        lax.fori_loop(0, index.shape[1], one, 0)

    def reflected(axis, v, t):
        tile = others[axis, v, t]
        return tile * flip[axis, t] if v < 3 else tile

    gather_axis(1, range(state_tiles), True)
    for d in range(span):
        b = Builder(lane)
        b.tiles[0] = send_b[8 * d : 8 * d + 8, :]
        for v in range(4):
            b.add(v, lambda k, v=v: reflected(1, v, k), 32 * d, 32 + 24 * v, 24)
        send_b[8 * d : 8 * d + 8, :] = b.tiles[0]
    exchange(send_b, recv_b, 8, b_sems)
    gather_axis(0, range(state_tiles), True)

    @pl.when(group == 0)
    def _():
        pl.semaphore_wait(hello, 1)
        rim_down.start()

    rim_up.wait()
    rim_down.wait()
    gather_axis(0, range(state_tiles, state_tiles + 2), False)

    for d in range(span):
        b = Builder(lane)
        for v in range(4):
            b.add(v, lambda k, v=v: reflected(0, v, k), 32 * d, 24 * v, 24)
        fold_96(b.tiles[0], rows_of(send_c, OUTER_ROWS * d)[0])
    exchange(send_c, recv_c, OUTER_ROWS, c_sems)

    for load in loads[8:]:
        load.wait()
    at = lax.broadcasted_iota(jnp.int32, (2, elems), 1)
    scale = metric[...]
    first = jnp.sum(jnp.where(at == 2 * me, scale, 0.0), axis=1, keepdims=True)
    last = jnp.sum(jnp.where(at == 2 * me + 1, scale, 0.0), axis=1, keepdims=True)

    def per_row(on_first, which):
        return jnp.where(on_first, first[which : which + 1], last[which : which + 1])

    marks = node_marks[...]
    on_first = marks[:, 4:5] < 0.5
    rx, ry = per_row(on_first, 0), per_row(on_first, 1)
    coef_u = 7.5 * rx * marks[:, 0:1]
    coef_v = 7.5 * ry * marks[:, 1:2]
    coef_c = 7.5 * (jnp.abs(rx) * marks[:, 2:3] + jnp.abs(ry) * marks[:, 3:4])
    operator = split(rx * node_tab[0, :, 0:144] + ry * node_tab[1, :, 0:144])
    lift_y = node_tab[2, :, 144:168].astype(BF16)
    over1_0 = ((1,), (0,))
    side = lax.broadcasted_iota(jnp.int32, (24, 1), 0)
    low_side = (side < 6) | ((side >= 12) & (side < 18))
    toward = jnp.where(low_side, 7.5, -7.5)
    ox, oy = per_row(side < 12, 0), per_row(side < 12, 1)

    over0, over1 = ((0,), (0,)), ((1,), (1,))
    basis = (both_high[:, 0:modes], both_low[:, 0:modes])
    pltpu.make_async_copy(recv_a, recv_a, a_sems.at[1]).wait()
    planes_a = dot3(split(recv_a[...]), basis, over0)
    reorder = lambda x: jnp.concatenate([x[a:b] for a, b in INNER + OUTER], axis=0)
    own = [reorder(planes_a[PAIR * v : PAIR * (v + 1)]) for v in range(3)]
    own_coef = coef_u * own[0] + coef_v * own[1] - coef_c

    def own_terms(v):
        fields[v, 0:72] = own[0] * own[v]
        fields[v, 72:144] = own[1] * own[v]
        planar = own_coef * own[v] + dot3(operator, split(fields[v]), over1_0)
        for part, at in ((planar, slice(0, modes)), (own[2] * own[v], slice(modes, 2 * modes))):
            rows_r[48 * v : 48 * v + 48, at] = part[0:48]
            rows_r[192 + 24 * v : 216 + 24 * v, at] = part[48:72]

    for v in range(3):
        own_terms(v)
    pltpu.make_async_copy(recv_b, recv_b, b_sems.at[1]).wait()
    planes_b = dot3(split(recv_b[...]), basis, over0)
    own.append(reorder(jnp.concatenate([planes_a[3 * PAIR :], planes_b[0:32]], axis=0)))
    facing_y_coef = (toward * oy) * planes_b[56:80] + 7.5 * jnp.abs(oy)
    facing_y = [split(facing_y_coef * planes_b[32 + 24 * v : 56 + 24 * v]) for v in range(4)]
    own_terms(3)
    for v in range(4):
        lifted = sum(jnp.dot(lift_y, part, preferred_element_type=F32) for part in facing_y[v])
        rows_r[48 * v : 48 * v + 48, 0:modes] += lifted[0:48]
        rows_r[192 + 24 * v : 216 + 24 * v, 0:modes] += lifted[48:72]
    both = (both_high[...], both_low[...])

    def damped(mode):
        k = jnp.where(mode == 1, modes // 2, mode >> 1).astype(F32)
        return 1.0 / (1.0 + TIME_STEP * VISCOSITY * k * k)

    step_of = TIME_STEP * damped(lax.broadcasted_iota(jnp.int32, (modes, 1), 0))

    inner_sum[:, 0:192] = step_of * dot3(both, split(rows_r[0:192, :]), over1)
    for d in range(span):
        mine = inner_sum[8 * d : 8 * d + 8, :]
        top = INNER_ROWS * d
        inner_send[top : top + 8, :] = mine[:, 0:LANES]
        fold(mine[:, LANES:], 0, 64, rows_of(inner_send, top + 8)[0])
    exchange(inner_send, inner_recv, INNER_ROWS, inner_sems)
    outer_sum[:, 0:96] = dot3(both, split(rows_r[192:288, :]), over1)

    pltpu.make_async_copy(recv_c, recv_c, c_sems.at[1]).wait()
    for s in range(span):
        modal_c[8 * s : 8 * s + 8, :] = unfold_96(rows_of(recv_c, OUTER_ROWS * s)[1])
    planes_c = dot3(split(modal_c[:, 0:96]), basis, over0)
    facing_x_coef = (toward * ox) * planes_c[0:24] + 7.5 * jnp.abs(ox)
    jump = split(jnp.concatenate([facing_x_coef] * 4, axis=0) * planes_c)
    outer_sum[:, 0:96] = step_of * (outer_sum[:, 0:96] + dot3(basis, jump, over1))
    for d in range(span):
        fold_96(outer_sum[8 * d : 8 * d + 8, :], rows_of(outer_send, OUTER_ROWS * d)[0])
    exchange(outer_send, outer_recv, OUTER_ROWS, outer_sems)

    shrink = damped(8 * me + row8)
    pltpu.make_async_copy(inner_recv, inner_recv, inner_sems.at[1]).wait()
    nothing = jnp.zeros((8, LANES), F32)
    builders = [Builder(lane) for _ in range(4)]
    for v in range(4):
        builders[v].tiles = {t: nothing for t in range(state_tiles)}
    for s in range(span):
        top = INNER_ROWS * s

        def inner(t, top=top):
            if t == 0:
                return inner_recv[top : top + 8, :]
            return unfold(rows_of(inner_recv, top + 8)[1], 64)

        tiles = [inner(0), inner(1)]
        for v in range(4):
            for e, (a, b) in enumerate(INNER):
                builders[v].add((s, e), lambda t, x=tiles: x[t], 48 * v + 24 * e, PAIR * s + a, 24)
    for v in range(4):
        for t in range(state_tiles):
            cut = slice(t * LANES, (t + 1) * LANES)
            settled[v, :, cut] = state[v, :, cut] * shrink + builders[v].tiles[t]
    put = pltpu.make_async_copy(settled, result, result_sem)
    put.start()
    pltpu.make_async_copy(outer_recv, outer_recv, outer_sems.at[1]).wait()
    put.wait()

    for send, rows, sems in (
        (send_a, 8, a_sems), (send_b, 8, b_sems), (send_c, OUTER_ROWS, c_sems),
        (inner_send, INNER_ROWS, inner_sems), (outer_send, OUTER_ROWS, outer_sems),
    ):
        sent = send.at[0 : rows * (span - 1), :]
        pltpu.make_async_copy(sent, sent, sems.at[0]).wait()


def finish(span, base, outer, out, base_v, outer_v, out_v, load_sems, store_sems):
    loads = [
        pltpu.make_async_copy(a, b, load_sems.at[i])
        for i, (a, b) in enumerate(((outer, outer_v), (base, base_v)))
    ]
    for load in loads:
        load.start()
    loads[0].wait()
    lane = tile_indices()[1]
    tiles = [unfold_96(rows_of(outer_v, OUTER_ROWS * s)[1]) for s in range(span)]
    loads[1].wait()
    stores = []
    for v in range(4):
        b = Builder(lane)
        for t in range(base.shape[2] // LANES):
            b.tiles[t] = jnp.zeros((8, LANES), F32)
        for s in range(span):
            for src, dst, length in ((0, 0, 6), (6, 30, 12), (18, 66, 6)):
                b.add((s, src), lambda t, x=tiles[s]: x, 24 * v + src, PAIR * s + dst, length)
        for t in range(base.shape[2] // LANES):
            cut = slice(t * LANES, (t + 1) * LANES)
            out_v[v, :, cut] = base_v[v, :, cut] + b.tiles[t]
        store = pltpu.make_async_copy(out_v.at[v], out.at[v], store_sems.at[v])
        store.start()
        stores.append(store)
    for store in stores:
        store.wait()


def body(groups, span, state, metric, neighbour, orient, wall, rim):
    elems = metric.shape[1]
    modes = span * 8
    tables, marks = node_tables()
    spread, rim_spread, lane_marks = lookup_tables(elems, rim.shape[1])
    both_high, both_low = basis_tables(modes)
    given = [
        state, rim, rim_spread, lane_marks, neighbour.T, orient.T, wall.T, spread,
        metric, tables, marks, both_high, both_low,
    ]
    given = [jnp.asarray(x) for x in given]
    gathered = elems // 2 * 32 // LANES
    scratch = [pltpu.VMEM(x.shape, x.dtype) for x in given] + [
        pltpu.VMEM((2, gathered, 8, LANES), jnp.int32),
        pltpu.VMEM((2, gathered, 8, LANES), F32),
        pltpu.VMEM((2, 4, gathered, 8, LANES), F32),
        pltpu.VMEM((2, 4, 8, LANES), F32),
        pltpu.VMEM((2, 4, 8, LANES), F32),
        pltpu.VMEM((modes, 256), F32),
        pltpu.VMEM((modes, LANES), F32),
        pltpu.VMEM((OUTER_ROWS * span, LANES), F32),
        pltpu.VMEM((modes, 256), F32),
        pltpu.VMEM((modes, LANES), F32),
        pltpu.VMEM((OUTER_ROWS * span, LANES), F32),
        pltpu.VMEM((modes, LANES), F32),
        pltpu.VMEM((4, 144, modes), F32),
        pltpu.VMEM((288, 2 * modes), F32),
        pltpu.VMEM((modes, 256), F32),
        pltpu.VMEM((modes, LANES), F32),
        pltpu.VMEM((INNER_ROWS * span, LANES), F32),
        pltpu.VMEM((OUTER_ROWS * span, LANES), F32),
        pltpu.VMEM((INNER_ROWS * span, LANES), F32),
        pltpu.VMEM(state.shape, F32),
        pltpu.SemaphoreType.DMA((len(given),)),
        pltpu.SemaphoreType.DMA((4,)),
        pltpu.SemaphoreType.DMA((2,)),
        pltpu.SemaphoreType.DMA((2,)),
        pltpu.SemaphoreType.DMA((2,)),
        pltpu.SemaphoreType.DMA((2,)),
        pltpu.SemaphoreType.DMA((2,)),
        pltpu.SemaphoreType.DMA,
        pltpu.SemaphoreType.REGULAR,
    ]
    hbm = pl.BlockSpec(memory_space=pltpu.HBM)
    outer = jax.ShapeDtypeStruct((OUTER_ROWS * span, LANES), F32)
    whole = jax.ShapeDtypeStruct(state.shape, F32)
    base, outer_rows = pl.pallas_call(
        functools.partial(kernel, groups, span),
        out_shape=(whole, outer),
        in_specs=[hbm] * len(given),
        out_specs=(hbm, hbm),
        scratch_shapes=scratch,
        compiler_params=pltpu.CompilerParams(
            collective_id=0, has_side_effects=True, vmem_limit_bytes=60 << 20
        ),
        name="section",
    )(*given)
    return pl.pallas_call(
        functools.partial(finish, span),
        out_shape=whole,
        in_specs=[hbm, hbm],
        out_specs=hbm,
        scratch_shapes=[
            pltpu.VMEM(whole.shape, F32), pltpu.VMEM(outer.shape, F32), pltpu.VMEM(whole.shape, F32),
            pltpu.SemaphoreType.DMA((2,)), pltpu.SemaphoreType.DMA((4,)),
        ],
        compiler_params=pltpu.CompilerParams(vmem_limit_bytes=60 << 20),
        name="finish",
    )(base, outer_rows)


def solution(mesh):
    specs = (
        P(None, "span", "elem"), P(None, "elem"), P("elem", None),
        P("elem", None), P("elem", None), P(None, "elem"),
    )
    return jax.shard_map(
        functools.partial(body, mesh.shape["elem"], mesh.shape["span"]),
        mesh=mesh, in_specs=specs, out_specs=P(None, "span", "elem"), check_vma=False,
    )
```
